512 devices in a mesh: lat: 16 (over y, core), lon: 32 (over z, x).
Axes of the slice: x: 4, y: 8, z: 8, core: 2. Of those that a mesh axis runs over, the one named last changes fastest.
Arguments:
- base_state: float32 [16, 48, 128, 128], P(None, 'lat', 'lon'), may hold values from -6 to 6
- tangent: float32 [16, 48, 128, 128], P(None, 'lat', 'lon'), may hold values from -6 to 6
- blocks: bfloat16 [48, 128, 9, 128, 128], P('lat', 'lon'), may hold values from -0.26516504 to 1.26516504
- pattern: int32 [48, 128, 9], P('lat', 'lon'), may hold values from 0 to 6143, as said below
- live: int32 [48, 128, 9], P('lat', 'lon'), may hold values from 0 to 1, as said below
- column_inverse: float32 [48, 128, 8, 16, 16], P('lat', 'lon'), may hold values from -0.4 to 1
- col_depth: int32 [48, 128, 8], P('lat', 'lon'), may hold values from 1 to 16
- uptake_rate: float32 [48, 128, 128], P('lat', 'lon'), may hold values from 0.3 to 3
- stoich: float32 [16], replicated, may hold values from -4 to 4
- basis: float32 [4, 16, 48, 128, 128], P(None, None, 'lat', 'lon'), may hold values from -0.00169145587 to 0.00169145587
Outputs:
- product: float32 [16, 48, 128, 128], P(None, 'lat', 'lon')
- next_basis: float32 [16, 48, 128, 128], P(None, 'lat', 'lon')
- coeffs: float32 [5], replicated
The draws below stay inside these ranges and needn't reach their ends.
Inputs may be any that keep to these rules, and one draw needn't show every extreme that they name: pattern[i, j, s] is the flat index i2 * 128 + j2 of a block with |i2 - i| <= 1 and |j2 - j| <= 1; slot 0 names the block itself; the live slots of a row block name different blocks. Slot 0 is always live.
All inputs are finite; a program needn't handle non-finite values.
Results may differ from the reference program's by a relative error of at most 0.0046.
Values may be sent and summed in bfloat16 or wider, within the bound.
No kernel may reach another device: no remote copies, remote signals or barrier semaphores. Data moves between devices by JAX's collectives and lax.ppermute only.
A program may use at most 64 MiB of HBM per device.

```python
import math
import jax
import jax.numpy as jnp
import numpy as np
from jax import lax

NTR = 16
COLS = 8
LEV = 16
BLK = 128
SLOTS = 9
KB = 4
NBLAT = 48
NBLON = 128


OFFSETS_LAT = np.array([0, -1, -1, -1, 0, 0, 1, 1, 1], dtype=np.int32)


OFFSETS_LON = np.array([0, -1, 0, 1, -1, 1, -1, 0, 1], dtype=np.int32)


def slot_order(key):
    scores = jax.random.randint(key, (NBLAT, NBLON, 8), 0, 2 ** 20) * 8 + jnp.arange(8, dtype=jnp.int32)
    others = jnp.argsort(scores, axis=-1).astype(jnp.int32) + 1
    return jnp.concatenate([jnp.zeros((NBLAT, NBLON, 1), jnp.int32), others], -1)


def slot_targets(order):
    lat_rows = jnp.arange(NBLAT, dtype=jnp.int32)[:, None, None] + jnp.asarray(OFFSETS_LAT)[order]
    lon_rows = jnp.arange(NBLON, dtype=jnp.int32)[None, :, None] + jnp.asarray(OFFSETS_LON)[order]
    inside = (lat_rows >= 0) & (lat_rows < NBLAT) & (lon_rows >= 0) & (lon_rows < NBLON)
    itself = jnp.arange(NBLAT, dtype=jnp.int32)[:, None, None] * NBLON + jnp.arange(NBLON, dtype=jnp.int32)[None, :, None]
    target = jnp.where(inside, lat_rows * NBLON + lon_rows, itself)
    return (target.astype(jnp.int32), inside)


def common_field(key):
    field_key = jax.random.fold_in(key, 7)
    return jnp.clip(jax.random.normal(field_key, (NTR, NBLAT, NBLON, BLK), jnp.float32), -6.0, 6.0)


def draw_pattern(key, part):
    order = slot_order(key)
    target, inside = slot_targets(order)
    return target


def draw_live(key, part):
    order = slot_order(key)
    key = jax.random.fold_in(key, 12)
    first_key, second_key = jax.random.split(key)
    target, inside = slot_targets(order)
    level = jax.random.randint(first_key, (NBLAT, NBLON, 1), 0, 4)
    coins = jax.random.randint(second_key, (NBLAT, NBLON, SLOTS), 0, 4)
    chosen = (coins <= level) & inside
    chosen = jnp.where(jnp.arange(SLOTS)[None, None, :] == 0, True, chosen)
    return chosen.astype(jnp.int32)


def draw_tangent(key, part):
    shared = common_field(key)
    return shared


def draw_basis(key, part):
    shared = common_field(key)
    key = jax.random.fold_in(key, 21)
    shape = (KB, NTR, NBLAT, NBLON, BLK)
    share = 0.6
    own = jnp.clip(jax.random.normal(key, shape, jnp.float32), -6.0, 6.0)
    mixed = share * shared[None] + (1.0 - share * share) ** 0.5 * own
    scale = float(NTR * BLK * NBLAT * NBLON) ** (-0.5)
    return jnp.clip(mixed, -6.0, 6.0) * scale


def draw_blocks(key, part):
    key = jax.random.fold_in(key, 22)
    noise = jnp.clip(jax.random.normal(key, (NBLAT, NBLON, SLOTS, BLK, BLK), jnp.float32), -6.0, 6.0)
    noise = noise * float(4 * BLK) ** (-0.5)
    identity = (jnp.arange(BLK)[:, None] == jnp.arange(BLK)[None, :]).astype(jnp.float32)
    first_slot = (jnp.arange(SLOTS) == 0).astype(jnp.float32)
    return (noise + first_slot[None, None, :, None, None] * identity[None, None, None]).astype(jnp.bfloat16)


def draw_column_inverse(key, part):
    key = jax.random.fold_in(key, 23)
    diag_key, off_key = jax.random.split(key)
    diagonal = jnp.exp(jax.random.uniform(diag_key, (NBLAT, NBLON, COLS, LEV), jnp.float32, -0.35667494, 0.0))
    off = jnp.clip(jax.random.normal(off_key, (NBLAT, NBLON, COLS, LEV, LEV), jnp.float32), -4.0, 4.0)
    off = off * (0.4 * float(LEV) ** (-0.5))
    identity = jnp.arange(LEV)[:, None] == jnp.arange(LEV)[None, :]
    return jnp.where(identity[None, None, None], diagonal[..., :, None], off)


def plant(values, key, least, largest):
    index_at = [jax.random.randint(jax.random.fold_in(key, axis), (), 0, length) for axis, length in enumerate(values.shape)]
    widest = values.shape.index(max(values.shape))
    beside = index_at[:widest] + [(index_at[widest] + 1) % values.shape[widest]] + index_at[widest + 1:]
    return values.at[tuple(index_at)].set(least).at[tuple(beside)].set(largest)


def block_scale(rng, shape, cuts, least, top_value):
    gain, own = 1.0, jax.random.fold_in(rng, 6)
    for axis_at, shards_of in cuts:
        draws = jnp.exp(jax.random.uniform(jax.random.fold_in(own, axis_at), (shards_of,), jnp.float32, least / len(cuts), top_value / len(cuts)))
        gain = gain * jnp.repeat(draws, shape[axis_at] // shards_of).reshape([-1 if axis == axis_at else 1 for axis in range(len(shape))])
    return gain


def gaussian(rng, dims, spread, limit, shards=(), kind=jnp.bfloat16):
    values = spread * jax.random.normal(rng, dims, jnp.float32)
    if shards:
        values = values * block_scale(rng, dims, shards, -0.22, 0.18)
    return jnp.clip(values, -limit, limit).astype(kind)


def setup_inputs(seed: int = 0) -> dict:
    seeds = jax.random.split(jax.random.key(seed), 11)
    return {
        "base_state": gaussian(seeds[0], (NTR, NBLAT, NBLON, BLK), 1.0, 6.0, ((1, 16), (2, 32)), jnp.float32),
        "tangent": draw_tangent(jax.random.fold_in(seeds[10], 71), 0),
        "blocks": draw_blocks(jax.random.fold_in(seeds[10], 71), 0),
        "pattern": draw_pattern(jax.random.fold_in(seeds[10], 71), 0),
        "live": draw_live(jax.random.fold_in(seeds[10], 71), 0),
        "column_inverse": draw_column_inverse(jax.random.fold_in(seeds[10], 71), 0),
        "col_depth": plant(jax.random.randint(seeds[6], (NBLAT, NBLON, COLS), 1, LEV + 1), jax.random.fold_in(seeds[6], 1), 1, LEV).astype(jnp.int32),
        "uptake_rate": jnp.clip(jnp.exp(math.log(3.0) - 2.3025851 * jax.random.uniform(seeds[7], (NBLAT, NBLON, BLK), jnp.float32) ** block_scale(seeds[7], (NBLAT, NBLON, BLK), ((0, 16), (1, 32)), -0.2, 0.2)), 0.3, 3.0),
        "stoich": gaussian(seeds[8], (NTR,), 1.0, 4.0, (), jnp.float32),
        "basis": draw_basis(jax.random.fold_in(seeds[10], 71), 0),
    }


def explicit(stacked, blocks, pattern, live):
    flat = stacked.reshape(stacked.shape[0], NBLAT * NBLON, BLK)

    def one_row(items):
        row_blocks, row_pattern, row_live = items
        gathered = flat[:, row_pattern, :].astype(jnp.float32)
        gathered = gathered * row_live.astype(jnp.float32)[None, :, :, None]
        return jnp.einsum('jspq,tjsq->tjp', row_blocks.astype(jnp.float32), gathered, precision=lax.Precision.HIGHEST)
    moved = lax.map(one_row, (blocks, pattern, live))
    return jnp.transpose(moved, (1, 0, 2, 3))

def reference(base_state, tangent, blocks, pattern, live, column_inverse, col_depth, uptake_rate, stoich, basis):
    wet = (jnp.arange(LEV)[None, None, None, :] < col_depth[..., None]).astype(jnp.float32)
    state = base_state
    along = tangent
    scaled = stoich[:, None, None, None]
    for turn in range(2):
        stacked = jnp.concatenate([state, along], 0).astype(jnp.bfloat16)
        moved = explicit(stacked, blocks, pattern, live)
        nutrient = state[0]
        denom = nutrient * nutrient + 1.0
        uptake = uptake_rate * nutrient * nutrient / denom
        slope = uptake_rate * 2.0 * nutrient / (denom * denom)
        source = jnp.concatenate([scaled * uptake[None], scaled * (slope * along[0])[None]], 0)
        mixed = (moved + source).reshape(2 * NTR, NBLAT, NBLON, COLS, LEV) * wet
        result = jnp.einsum('abclm,tabcm->tabcl', column_inverse, mixed, precision=lax.Precision.HIGHEST) * wet
        result = result.reshape(2 * NTR, NBLAT, NBLON, BLK)
        state = result[:NTR]
        along = result[NTR:]
    product = along
    heights = jnp.einsum('ktabp,tabp->k', basis, product, precision=lax.Precision.HIGHEST)
    rest = product - jnp.einsum('k,ktabp->tabp', heights, basis, precision=lax.Precision.HIGHEST)
    beta = jnp.sqrt(jnp.sum(rest * rest) + 1e-06)
    next_basis = rest / beta
    coeffs = jnp.concatenate([heights, beta[None]])
    return (product, next_basis, coeffs)
```

```python
import jax
import jax.numpy as jnp
from jax import lax
from jax.sharding import PartitionSpec as P


def padded_2(x, sides, width):
    for axis, dim in sides:
        size, length = (lax.axis_size(axis), x.shape[dim])
        up = [(i, (i + 1) % size) for i in range(size - 1)]
        down = [(j, i) for i, j in up]
        last = lax.slice_in_dim(x, length - width, length, axis=dim)
        first = lax.slice_in_dim(x, 0, width, axis=dim)
        before = lax.ppermute(last, axis, up)
        after = lax.ppermute(first, axis, down)
        x = jnp.concatenate([before, x, after], axis=dim)
    return x


def extend(stacked):
    return padded_2(stacked, (("lat", 1), ("lon", 2)), 1)


def summed(part):
    length = part.shape[0]
    row = jnp.pad(part, (0, 128 - length))
    for axis in ("lat", "lon"):
        copies = jnp.broadcast_to(row[None], (lax.axis_size(axis), 128))
        row = jnp.sum(lax.all_to_all(copies, axis, 0, 0), 0)
    return row[:length]


def body(
    base_state,
    tangent,
    blocks,
    pattern,
    live,
    column_inverse,
    col_depth,
    uptake_rate,
    stoich,
    basis,
):
    tracers = base_state.shape[0]
    lat_blocks = base_state.shape[1]
    lon_blocks = base_state.shape[2]
    points = base_state.shape[3]
    columns = column_inverse.shape[2]
    levels = column_inverse.shape[3]
    total_lon = lon_blocks * lax.axis_size("lon")
    lat_first = lax.axis_index("lat") * lat_blocks
    lon_first = lax.axis_index("lon") * lon_blocks
    row_lat = pattern // total_lon - lat_first + 1
    row_lon = pattern % total_lon - lon_first + 1
    local_index = row_lat * (lon_blocks + 2) + row_lon
    live_weight = live.astype(jnp.bfloat16)[None, :, :, :, None]
    wet = (jnp.arange(levels)[None, None, None, :] < col_depth[..., None]).astype(jnp.float32)
    scaled = stoich[:, None, None, None]
    state = base_state
    along = tangent
    for turn in range(2):
        stacked = jnp.concatenate([state, along], 0).astype(jnp.bfloat16)
        padded = extend(stacked)
        flat = padded.reshape(2 * tracers, (lat_blocks + 2) * (lon_blocks + 2), points)
        gathered = jnp.take(flat, local_index, axis=1) * live_weight
        moved = jnp.einsum(
            "abspq,tabsq->tabp", blocks, gathered, preferred_element_type=jnp.float32
        )
        nutrient = state[0]
        denom = nutrient * nutrient + 1.0
        uptake = uptake_rate * nutrient * nutrient / denom
        slope = uptake_rate * 2.0 * nutrient / (denom * denom)
        source = jnp.concatenate([scaled * uptake[None], scaled * (slope * along[0])[None]], 0)
        mixed = (moved + source).reshape(2 * tracers, lat_blocks, lon_blocks, columns, levels) * wet
        result = (
            jnp.einsum("abclm,tabcm->tabcl", column_inverse, mixed, precision=lax.Precision.HIGHEST)
            * wet
        )
        result = result.reshape(2 * tracers, lat_blocks, lon_blocks, points)
        state = result[:tracers]
        along = result[tracers:]
    vectors = jnp.concatenate([basis, along[None]], 0)
    gram = jnp.einsum("ktabp,jtabp->kj", vectors, vectors, precision=lax.Precision.HIGHEST)
    total = summed(gram.reshape(25)).reshape(5, 5)
    heights = total[:4, 4]
    rest = along - jnp.einsum("k,ktabp->tabp", heights, basis, precision=lax.Precision.HIGHEST)
    cross = jnp.sum(heights[:, None] * heights[None, :] * total[:4, :4])
    squares = jnp.sum(heights * heights)
    short = total[4, 4] - 2.0 * squares + cross
    size = total[4, 4] + 2.0 * squares + cross
    squared = lax.cond(
        short < 0.01 * size,
        lambda r: summed(jnp.sum(r * r).reshape(1))[0],
        lambda r: short,
        rest,
    )
    beta = jnp.sqrt(squared + 1e-06)
    next_basis = rest / beta
    coeffs = jnp.concatenate([heights, beta[None]])
    return (along, next_basis, coeffs)


def solution(mesh):
    placed = (
        P(None, "lat", "lon", None),
        P(None, "lat", "lon", None),
        P("lat", "lon", None, None, None),
        P("lat", "lon", None),
        P("lat", "lon", None),
        P("lat", "lon", None, None, None),
        P("lat", "lon", None),
        P("lat", "lon", None),
        P(),
        P(None, None, "lat", "lon", None),
    )
    return jax.shard_map(
        body,
        mesh=mesh,
        in_specs=placed,
        out_specs=(P(None, "lat", "lon", None), P(None, "lat", "lon", None), P()),
        check_vma=False,
    )
```

```python
import functools

import jax
import jax.numpy as jnp
from jax import lax
from jax.experimental import pallas as pl
from jax.experimental.pallas import tpu as pltpu
from jax.sharding import PartitionSpec as P

F32 = jnp.float32
BF16 = jnp.bfloat16
VMEM = pl.BlockSpec(memory_space=pltpu.VMEM)
SMEM = pl.BlockSpec(memory_space=pltpu.SMEM)
ANY = pl.BlockSpec(memory_space=pl.ANY)
NT = (((1,), (1,)), ((), ()))


def call(kernel, outs, ins, out_specs, scratch=(), flops=0, size=0, limit=16):
    return pl.pallas_call(
        kernel,
        out_shape=outs,
        in_specs=ins,
        out_specs=out_specs,
        scratch_shapes=list(scratch),
        compiler_params=pltpu.CompilerParams(vmem_limit_bytes=limit * 2**20),
        cost_estimate=pl.CostEstimate(flops=flops, bytes_accessed=size, transcendentals=0),
    )


def like(shape, dtype=F32):
    return jax.ShapeDtypeStruct(shape, dtype)


def iota(shape, dim):
    return lax.broadcasted_iota(jnp.int32, shape, dim)


def pack_kernel(lon, c_ref, v_ref, x_ref, first_ref, last_ref, own_ref):
    rows = x_ref.shape[0]
    tracers = c_ref.shape[0] // rows
    for r in range(rows):
        at = pl.ds(r, tracers, stride=rows)
        x = jnp.concatenate([c_ref[at, :], v_ref[at, :]], 0).astype(BF16)
        x_ref[r] = x
        if r < lon:
            first_ref[r] = x
        if r >= rows - lon:
            last_ref[r - (rows - lon)] = x
    own_ref[0] = c_ref[:rows, :]
    own_ref[1] = v_ref[:rows, :]


def sources(own_c, own_v, rate):
    denom = own_c * own_c + 1.0
    uptake = rate * own_c * own_c / denom
    slope = rate * 2.0 * own_c / (denom * denom)
    return uptake, slope * own_v


def prep_kernel(
    total_lon,
    pattern_ref,
    live_ref,
    inverse_ref,
    depth_ref,
    rate_ref,
    own_ref,
    stoich_ref,
    basis_ref,
    index_ref,
    high_ref,
    low_ref,
    wet_ref,
    source_ref,
    share_ref,
    gram_ref,
):
    lat, lon, slots = pattern_ref.shape
    rows, points, levels = inverse_ref.shape
    pattern = pattern_ref[...]
    itself = pattern[:, :, :1]
    far_lat = pattern // total_lon - itself // total_lon
    far_lon = pattern % total_lon - itself % total_lon
    shape = pattern.shape
    place = (iota(shape, 0) + 1 + far_lat) * (lon + 2) + iota(shape, 1) + 1 + far_lon
    index_ref[...] = jnp.where(live_ref[...] > 0, place, (lat + 2) * (lon + 2))

    lane = iota((rows, points), 1)
    depth = depth_ref[...]
    below = jnp.zeros((rows, points), jnp.int32)
    for k in range(points // levels):
        below = jnp.where(lane // levels == k, depth[:, k : k + 1], below)
    wet = (lane % levels < below).astype(F32)
    wet_ref[...] = wet

    uptake, pull = sources(own_ref[0], own_ref[1], rate_ref[...])
    source_ref[0] = uptake
    source_ref[1] = pull

    tracers = share_ref.shape[0]
    square = (tracers, tracers)
    stoich = jnp.broadcast_to(stoich_ref[...], square)
    column = jnp.sum(jnp.where(iota(square, 0) == iota(square, 1), stoich, 0.0), 1, keepdims=True)
    share_ref[...] = jnp.broadcast_to(column, share_ref.shape)

    spread = (iota((levels, points), 1) % levels == iota((levels, points), 0)).astype(BF16)
    full = (points, points)
    same = iota(full, 0) // levels == iota(full, 1) // levels
    for r in range(rows):
        inverse = inverse_ref[r]
        high = inverse.astype(BF16)
        low = (inverse - high.astype(F32)).astype(BF16)
        keep = jnp.where(same, wet[r : r + 1, :], 0.0)
        for ref, part in ((high_ref, high), (low_ref, low)):
            tiled = jnp.dot(part, spread, preferred_element_type=F32)
            ref[r] = (tiled * keep).astype(BF16)

    gram_ref[...] = jnp.zeros(gram_ref.shape, F32)
    count = basis_ref.shape[0]
    row = 0
    for k in range(count):
        for j in range(k, count):
            gram_ref[row : row + 1, :] = jnp.sum(basis_ref[k] * basis_ref[j], 0, keepdims=True)
            row += 1


def fill(pad_ref, x_ref, north_ref, south_ref, west_ref, east_ref, lat, lon):
    wide = lon + 2
    for j in range(lon):
        pad_ref[1 + j] = north_ref[j]
        pad_ref[(lat + 1) * wide + 1 + j] = south_ref[j]
        for i in range(lat):
            pad_ref[(i + 1) * wide + 1 + j] = x_ref[i * lon + j]
    for i in range(lat + 2):
        pad_ref[i * wide] = west_ref[i]
        pad_ref[i * wide + lon + 1] = east_ref[i]
    pad_ref[(lat + 2) * wide] = jnp.zeros(pad_ref.shape[1:], BF16)


def transport(r, index_ref, pad_ref, held_ref, lon, slots):
    total = None
    for s in range(slots):
        x = pad_ref[index_ref[r // lon, r % lon, s]]
        term = lax.dot_general(x, held_ref[r * slots + s], NT, preferred_element_type=F32)
        total = term if total is None else total + term
    return total


def mix(z, high, low, wet):
    z_high = z.astype(BF16)
    z_low = (z - z_high.astype(F32)).astype(BF16)
    dot = functools.partial(lax.dot_general, dimension_numbers=NT, preferred_element_type=F32)
    return (dot(z_high, high) + (dot(z_high, low) + dot(z_low, high))) * wet


def fetches(blocks_ref, held_ref, sems, slots, rows):
    copies = []
    for r in range(rows):
        part = pl.ds(r * slots, slots)
        copies.append(pltpu.make_async_copy(blocks_ref.at[part], held_ref.at[part], sems.at[r]))
        copies[-1].start()
    return copies


def first_kernel(
    lat,
    lon,
    slots,
    index_ref,
    x_ref,
    north_ref,
    south_ref,
    west_ref,
    east_ref,
    high_ref,
    low_ref,
    wet_ref,
    source_ref,
    share_ref,
    rate_ref,
    blocks_ref,
    y_ref,
    first_ref,
    last_ref,
    pull_ref,
    pad_ref,
    held_ref,
    own_ref,
    sems,
):
    rows = lat * lon
    copies = fetches(blocks_ref, held_ref, sems, slots, rows)
    fill(pad_ref, x_ref, north_ref, south_ref, west_ref, east_ref, lat, lon)
    share = share_ref[...]
    tracers = share.shape[0]
    for r in range(rows):
        copies[r].wait()
        at = slice(r, r + 1)
        added = jnp.concatenate([share * source_ref[0, at, :], share * source_ref[1, at, :]], 0)
        z = transport(r, index_ref, pad_ref, held_ref, lon, slots) + added
        out = mix(z, high_ref[r], low_ref[r], wet_ref[at, :])
        own_ref[0, at, :] = out[:1]
        own_ref[1, at, :] = out[tracers : tracers + 1]
        y = out[tracers:].astype(BF16)
        y_ref[r] = y
        if r < lon:
            first_ref[r] = y
        if r >= rows - lon:
            last_ref[r - (rows - lon)] = y
    pull_ref[...] = sources(own_ref[0], own_ref[1], rate_ref[...])[1]


def second_kernel(
    lat,
    lon,
    slots,
    index_ref,
    x_ref,
    north_ref,
    south_ref,
    west_ref,
    east_ref,
    high_ref,
    low_ref,
    wet_ref,
    pull_ref,
    share_ref,
    gram_ref,
    basis_ref,
    blocks_ref,
    product_ref,
    sums_ref,
    pad_ref,
    held_ref,
    sems,
):
    rows = lat * lon
    copies = fetches(blocks_ref, held_ref, sems, slots, rows)
    fill(pad_ref, x_ref, north_ref, south_ref, west_ref, east_ref, lat, lon)
    share = share_ref[...]
    tracers = share.shape[0]
    for r in range(rows):
        copies[r].wait()
        at = slice(r, r + 1)
        z = transport(r, index_ref, pad_ref, held_ref, lon, slots) + share * pull_ref[at, :]
        out = mix(z, high_ref[r], low_ref[r], wet_ref[at, :])
        product_ref[pl.ds(r, tracers, stride=rows), :] = out
    product = product_ref[...]
    parts = [gram_ref[...]]
    count = basis_ref.shape[0]
    pairs = count * (count + 1) // 2
    height = gram_ref.shape[0]
    spot = iota(gram_ref.shape, 0)
    all_sums = gram_ref[...]
    for k in range(count + 1):
        other = basis_ref[k] if k < count else product
        part = jnp.sum(product * other, 0, keepdims=True)
        all_sums = jnp.where(spot == pairs + k, part, all_sums)
    column = jnp.sum(all_sums, 1, keepdims=True)
    row = jnp.sum(jnp.where(spot == iota(spot.shape, 1), column, 0.0), 0, keepdims=True)
    sums_ref[...] = jnp.broadcast_to(row, sums_ref.shape)


def last_kernel(parts_ref, product_ref, basis_ref, next_ref, coeffs_ref, flag_ref):
    count = basis_ref.shape[0]
    row = jnp.sum(parts_ref[...], 0, keepdims=True)
    lane = iota(row.shape, 1)

    def pick(at):
        return jnp.sum(jnp.where(lane == at, row, 0.0), 1, keepdims=True)

    pairs = count * (count + 1) // 2
    heights = [pick(pairs + k) for k in range(count)]
    whole = pick(pairs + count)
    cross = jnp.zeros((1, 1), F32)
    at = 0
    for k in range(count):
        for j in range(k, count):
            twice = 1.0 if k == j else 2.0
            cross = cross + twice * (heights[k] * heights[j] * pick(at))
            at += 1
    squares = sum(h * h for h in heights)
    short = whole - 2.0 * squares + cross
    size = whole + 2.0 * squares + cross
    beta = jnp.sqrt(jnp.maximum(short, 0.0) + 1e-06)
    rest = product_ref[...]
    for k in range(count):
        rest = rest - heights[k] * basis_ref[k]
    next_ref[...] = rest / beta
    for k in range(count):
        coeffs_ref[k] = heights[k][0, 0]
    coeffs_ref[count] = beta[0, 0]
    flag_ref[0] = jnp.where(short < 0.01 * size, 1, 0)[0, 0]


def summed(rows):
    row = jnp.sum(lax.all_to_all(rows, "lat", 0, 0), 0, keepdims=True)
    rows = jnp.broadcast_to(row, (lax.axis_size("lon"), row.shape[1]))
    return lax.all_to_all(rows, "lon", 0, 0)


def halo(x, first, last, lat, lon):
    def moved(a, axis, step):
        size = lax.axis_size(axis)
        pairs = [(i, i + step) for i in range(size) if 0 <= i + step < size]
        return lax.ppermute(a, axis, pairs)

    north = moved(last, "lat", 1)
    south = moved(first, "lat", -1)
    grid = x.reshape((lat, lon) + x.shape[1:])
    right = jnp.concatenate([north[None, lon - 1], grid[:, lon - 1], south[None, lon - 1]], 0)
    left = jnp.concatenate([north[None, 0], grid[:, 0], south[None, 0]], 0)
    west = moved(right, "lon", 1)
    east = moved(left, "lon", -1)
    return north, south, west, east


def body(
    base_state,
    tangent,
    blocks,
    pattern,
    live,
    column_inverse,
    col_depth,
    uptake_rate,
    stoich,
    basis,
):
    tracers, lat, lon, points = base_state.shape
    columns, levels = column_inverse.shape[2:4]
    slots = pattern.shape[2]
    count = basis.shape[0]
    rows = lat * lon
    total_lon = lon * lax.axis_size("lon")
    size = tracers * rows
    places = (lat + 2) * (lon + 2) + 1
    flat_basis = basis.reshape(count, size, points)
    rate = uptake_rate.reshape(rows, points)
    matrices = blocks.reshape(rows * slots, points, points)

    x, first, last, own = call(
        functools.partial(pack_kernel, lon),
        (
            like((rows, 2 * tracers, points), BF16),
            like((lon, 2 * tracers, points), BF16),
            like((lon, 2 * tracers, points), BF16),
            like((2, rows, points)),
        ),
        [VMEM] * 2,
        [VMEM] * 4,
        size=400000,
    )(base_state.reshape(size, points), tangent.reshape(size, points))

    index, high, low, wet, source, share, gram = call(
        functools.partial(prep_kernel, total_lon),
        (
            like((lat, lon, slots), jnp.int32),
            like((rows, points, points), BF16),
            like((rows, points, points), BF16),
            like((rows, points)),
            like((2, rows, points)),
            like((tracers, points)),
            like((16, points)),
        ),
        [VMEM] * 8,
        [VMEM] * 7,
        size=2500000,
    )(
        pattern,
        live,
        column_inverse.reshape(rows, points, levels),
        col_depth.reshape(rows, columns),
        rate,
        own,
        stoich.reshape(1, tracers),
        flat_basis,
    )

    north, south, west, east = halo(x, first, last, lat, lon)
    held = pltpu.VMEM((rows * slots, points, points), BF16)
    work = 2 * 2 * tracers * rows * slots * points * points
    x, first, last, pull = call(
        functools.partial(first_kernel, lat, lon, slots),
        (
            like((rows, tracers, points), BF16),
            like((lon, tracers, points), BF16),
            like((lon, tracers, points), BF16),
            like((rows, points)),
        ),
        [SMEM] + [VMEM] * 11 + [ANY],
        [VMEM] * 4,
        scratch=[
            pltpu.VMEM((places, 2 * tracers, points), BF16),
            held,
            pltpu.VMEM((2, rows, points), F32),
            pltpu.SemaphoreType.DMA((rows,)),
        ],
        flops=work,
        size=5000000,
    )(index, x, north, south, west, east, high, low, wet, source, share, rate, matrices)

    north, south, west, east = halo(x, first, last, lat, lon)
    product, sums = call(
        functools.partial(second_kernel, lat, lon, slots),
        (like((size, points)), like((lax.axis_size("lat"), points))),
        [SMEM] + [VMEM] * 12 + [ANY],
        [VMEM] * 2,
        scratch=[
            pltpu.VMEM((places, tracers, points), BF16),
            held,
            pltpu.SemaphoreType.DMA((rows,)),
        ],
        flops=work // 2,
        size=5000000,
    )(index, x, north, south, west, east, high, low, wet, pull, share, gram, flat_basis, matrices)

    parts = summed(sums)
    following, coeffs, flag = call(
        last_kernel,
        (like((size, points)), like((count + 1,)), like((1,), jnp.int32)),
        [VMEM] * 3,
        [VMEM, SMEM, SMEM],
        size=700000,
    )(parts, product, flat_basis)

    def again(carry):
        following, coeffs, flag = carry
        rest = product - jnp.einsum(
            "k,ksp->sp", coeffs[:count], flat_basis, precision=lax.Precision.HIGHEST
        )
        part = jnp.pad(jnp.sum(rest * rest).reshape(1, 1), ((0, 0), (0, points - 1)))
        squared = jnp.sum(summed(jnp.broadcast_to(part, (lax.axis_size("lat"), points))), 0)[0]
        beta = jnp.sqrt(squared + 1e-06)
        return rest / beta, jnp.concatenate([coeffs[:count], beta[None]]), flag * 0

    following, coeffs, flag = lax.while_loop(
        lambda carry: carry[2][0] > 0, again, (following, coeffs, flag)
    )
    shape = base_state.shape
    return product.reshape(shape), following.reshape(shape), coeffs


def solution(mesh):
    placed = (
        P(None, "lat", "lon", None),
        P(None, "lat", "lon", None),
        P("lat", "lon", None, None, None),
        P("lat", "lon", None),
        P("lat", "lon", None),
        P("lat", "lon", None, None, None),
        P("lat", "lon", None),
        P("lat", "lon", None),
        P(),
        P(None, None, "lat", "lon", None),
    )
    return jax.shard_map(
        body,
        mesh=mesh,
        in_specs=placed,
        out_specs=(P(None, "lat", "lon", None), P(None, "lat", "lon", None), P()),
        check_vma=False,
    )
```

```python
import functools

import jax
import jax.numpy as jnp
from jax import lax
from jax.experimental import pallas as pl
from jax.experimental.pallas import tpu as pltpu
from jax.sharding import PartitionSpec as P

F32 = jnp.float32
BF16 = jnp.bfloat16
VMEM = pl.BlockSpec(memory_space=pltpu.VMEM)
SMEM = pl.BlockSpec(memory_space=pltpu.SMEM)
HBM = pl.BlockSpec(memory_space=pltpu.HBM)
NT = (((1,), (1,)), ((), ()))


def call(kernel, outs, ins, out_specs, scratch=(), flops=0, size=0, limit=16):
    return pl.pallas_call(
        kernel,
        out_shape=outs,
        in_specs=ins,
        out_specs=out_specs,
        scratch_shapes=list(scratch),
        compiler_params=pltpu.CompilerParams(vmem_limit_bytes=limit * 2**20),
        cost_estimate=pl.CostEstimate(flops=flops, bytes_accessed=size, transcendentals=0),
    )


def like(shape, dtype=F32):
    return jax.ShapeDtypeStruct(shape, dtype)


def iota(shape, dim):
    return lax.broadcasted_iota(jnp.int32, shape, dim)


def pack_kernel(lon, c_hbm, v_hbm, x_ref, first_ref, last_ref, own_ref, c_ref, v_ref, sems):
    copies = [
        pltpu.make_async_copy(c_hbm, c_ref, sems.at[0]),
        pltpu.make_async_copy(v_hbm, v_ref, sems.at[1]),
    ]
    for copy in copies:
        copy.start()
    for copy in copies:
        copy.wait()
    rows = x_ref.shape[0]
    tracers = c_ref.shape[0] // rows
    for r in range(rows):
        at = pl.ds(r, tracers, stride=rows)
        x = jnp.concatenate([c_ref[at, :], v_ref[at, :]], 0).astype(BF16)
        x_ref[r] = x
        if r < lon:
            first_ref[r] = x
        if r >= rows - lon:
            last_ref[r - (rows - lon)] = x
    own_ref[0] = c_ref[:rows, :]
    own_ref[1] = v_ref[:rows, :]


def prep_kernel(
    total_lon,
    pattern_hbm,
    live_hbm,
    inverse_hbm,
    depth_hbm,
    rate_hbm,
    stoich_hbm,
    basis_hbm,
    blocks_hbm,
    own_ref,
    index_ref,
    high_ref,
    low_ref,
    source_ref,
    rate_column_ref,
    gram_ref,
    basis_ref,
    held_ref,
    pattern_ref,
    live_ref,
    inverse_ref,
    depth_ref,
    rate_ref,
    stoich_ref,
    sems,
):
    pairs = [
        (pattern_hbm, pattern_ref),
        (live_hbm, live_ref),
        (depth_hbm, depth_ref),
        (rate_hbm, rate_ref),
        (stoich_hbm, stoich_ref),
        (inverse_hbm, inverse_ref),
        (basis_hbm, basis_ref),
        (blocks_hbm, held_ref),
    ]
    copies = [pltpu.make_async_copy(a, b, sems.at[i]) for i, (a, b) in enumerate(pairs)]
    for copy in copies:
        copy.start()
    for copy in copies[:5]:
        copy.wait()
    lat, lon, slots = pattern_ref.shape
    rows = lat * lon
    columns, levels = inverse_ref.shape[2:4]
    points = columns * levels
    pattern = pattern_ref[...]
    itself = pattern[:, :, :1]
    far_lat = pattern // total_lon - itself // total_lon
    far_lon = pattern % total_lon - itself % total_lon
    shape = pattern.shape
    place = (iota(shape, 0) + 1 + far_lat) * (lon + 2) + iota(shape, 1) + 1 + far_lon
    index_ref[...] = jnp.where(live_ref[...] > 0, place, (lat + 2) * (lon + 2))

    lane = iota((rows, points), 1)
    depth = jnp.concatenate([depth_ref[i] for i in range(lat)], 0)
    below = jnp.zeros((rows, points), jnp.int32)
    for k in range(columns):
        below = jnp.where(lane // levels == k, depth[:, k : k + 1], below)
    wet = (lane % levels < below).astype(F32)

    rate = jnp.concatenate([rate_ref[i] for i in range(lat)], 0)
    uptake, pull = sources(own_ref[0], own_ref[1], rate)
    spare = 8 - rows % 8 if rows % 8 else 0
    blank = [jnp.zeros((spare, points), F32)] if spare else []
    columns_of = [
        jnp.transpose(jnp.concatenate([part] + blank, 0)) for part in (uptake, pull, rate, wet)
    ]
    rate_column_ref[...] = columns_of[2]
    tracers = source_ref.shape[2] // 2
    share = stoich_ref[...]
    nothing = jnp.zeros((1, tracers), F32)
    share_c = jnp.concatenate([share, nothing], 1)
    share_v = jnp.concatenate([nothing, share], 1)
    for r in range(rows):
        at = slice(r, r + 1)
        source_ref[r] = columns_of[0][:, at] * share_c + columns_of[1][:, at] * share_v

    copies[5].wait()
    spread = (iota((levels, points), 1) % levels == iota((levels, points), 0)).astype(BF16)
    full = (points, points)
    same = iota(full, 0) // levels == iota(full, 1) // levels
    for r in range(rows):
        at = slice(r, r + 1)
        inverse = inverse_ref[r // lon, r % lon].reshape(points, levels)
        high = inverse.astype(BF16)
        low = (inverse - high.astype(F32)).astype(BF16)
        keep = jnp.where(same, wet[at, :] * columns_of[3][:, at], 0.0)
        for ref, part in ((high_ref, high), (low_ref, low)):
            tiled = jnp.dot(part, spread, preferred_element_type=F32)
            ref[r] = (tiled * keep).astype(BF16)

    copies[6].wait()
    gram_ref[...] = jnp.zeros(gram_ref.shape, F32)
    count = basis_ref.shape[0]
    row = 0
    for k in range(count):
        for j in range(k, count):
            gram_ref[row : row + 1, :] = jnp.sum(basis_ref[k] * basis_ref[j], 0, keepdims=True)
            row += 1
    copies[7].wait()


def sources(own_c, own_v, rate):
    denom = own_c * own_c + 1.0
    uptake = rate * own_c * own_c / denom
    slope = rate * 2.0 * own_c / (denom * denom)
    return uptake, slope * own_v


def pull_kernel(state_ref, rate_column_ref, stoich_ref, source_ref):
    rows, _, tracers = source_ref.shape
    share = stoich_ref[...]
    for r in range(rows):
        own_c = state_ref[r, :, 0:1]
        own_v = state_ref[r, :, tracers : tracers + 1]
        source_ref[r] = sources(own_c, own_v, rate_column_ref[:, r : r + 1])[1] * share


def fill(pad_ref, x_ref, north_ref, south_ref, west_ref, east_ref, lat, lon):
    wide = lon + 2
    for j in range(lon):
        pad_ref[1 + j] = north_ref[j]
        pad_ref[(lat + 1) * wide + 1 + j] = south_ref[j]
        for i in range(lat):
            pad_ref[(i + 1) * wide + 1 + j] = x_ref[i * lon + j]
    for i in range(lat + 2):
        pad_ref[i * wide] = west_ref[i]
        pad_ref[i * wide + lon + 1] = east_ref[i]
    pad_ref[(lat + 2) * wide] = jnp.zeros(pad_ref.shape[1:], BF16)


def advance(r, index_ref, pad_ref, held_ref, high_ref, low_ref, source_ref):
    slots = index_ref.shape[2]
    lon = index_ref.shape[1]
    z = source_ref[r]
    for s in range(slots):
        x = pad_ref[index_ref[r // lon, r % lon, s]]
        z = z + lax.dot_general(held_ref[r * slots + s], x, NT, preferred_element_type=F32)
    z_high = z.astype(BF16)
    z_low = (z - z_high.astype(F32)).astype(BF16)
    dot = functools.partial(jnp.dot, preferred_element_type=F32)
    return dot(high_ref[r], z_high) + (dot(low_ref[r], z_high) + dot(high_ref[r], z_low))


def first_kernel(
    lat,
    lon,
    index_ref,
    x_ref,
    north_ref,
    south_ref,
    west_ref,
    east_ref,
    held_ref,
    high_ref,
    low_ref,
    source_ref,
    y_ref,
    first_ref,
    last_ref,
    state_ref,
    pad_ref,
):
    rows = lat * lon
    fill(pad_ref, x_ref, north_ref, south_ref, west_ref, east_ref, lat, lon)
    tracers = y_ref.shape[1]
    for r in range(rows):
        out = advance(r, index_ref, pad_ref, held_ref, high_ref, low_ref, source_ref)
        state_ref[r] = out
        y = jnp.transpose(out)[tracers:].astype(BF16)
        y_ref[r] = y
        if r < lon:
            first_ref[r] = y
        if r >= rows - lon:
            last_ref[r - (rows - lon)] = y


def second_kernel(
    lat,
    lon,
    index_ref,
    x_ref,
    north_ref,
    south_ref,
    west_ref,
    east_ref,
    held_ref,
    high_ref,
    low_ref,
    source_ref,
    gram_ref,
    basis_ref,
    product_ref,
    sums_ref,
    pad_ref,
):
    rows = lat * lon
    fill(pad_ref, x_ref, north_ref, south_ref, west_ref, east_ref, lat, lon)
    tracers = x_ref.shape[1]
    for r in range(rows):
        out = advance(r, index_ref, pad_ref, held_ref, high_ref, low_ref, source_ref)
        product_ref[pl.ds(r, tracers, stride=rows), :] = jnp.transpose(out)
    product = product_ref[...]
    count = basis_ref.shape[0]
    pairs = count * (count + 1) // 2
    all_sums = gram_ref[...]
    spot = iota(all_sums.shape, 0)
    for k in range(count + 1):
        other = basis_ref[k] if k < count else product
        part = jnp.sum(product * other, 0, keepdims=True)
        all_sums = jnp.where(spot == pairs + k, part, all_sums)
    column = jnp.sum(all_sums, 1, keepdims=True)
    row = jnp.sum(jnp.where(spot == iota(spot.shape, 1), column, 0.0), 0, keepdims=True)
    sums_ref[...] = jnp.broadcast_to(row, sums_ref.shape)


def last_kernel(
    parts_ref, product_ref, basis_ref, next_ref, out_hbm, coeffs_ref, flag_ref, sem
):
    copy = pltpu.make_async_copy(product_ref, out_hbm, sem)
    copy.start()
    count = basis_ref.shape[0]
    row = jnp.sum(parts_ref[...], 0, keepdims=True)
    lane = iota(row.shape, 1)

    def pick(at):
        return jnp.sum(jnp.where(lane == at, row, 0.0), 1, keepdims=True)

    pairs = count * (count + 1) // 2
    heights = [pick(pairs + k) for k in range(count)]
    whole = pick(pairs + count)
    cross = jnp.zeros((1, 1), F32)
    at = 0
    for k in range(count):
        for j in range(k, count):
            twice = 1.0 if k == j else 2.0
            cross = cross + twice * (heights[k] * heights[j] * pick(at))
            at += 1
    squares = sum(h * h for h in heights)
    short = whole - 2.0 * squares + cross
    size = whole + 2.0 * squares + cross
    beta = jnp.sqrt(jnp.maximum(short, 0.0) + 1e-06)
    rest = product_ref[...]
    for k in range(count):
        rest = rest - heights[k] * basis_ref[k]
    next_ref[...] = rest / beta
    for k in range(count):
        coeffs_ref[k] = heights[k][0, 0]
    coeffs_ref[count] = beta[0, 0]
    flag_ref[0] = jnp.where(short < 0.01 * size, 1, 0)[0, 0]
    copy.wait()


def summed(rows):
    row = jnp.sum(lax.all_to_all(rows, "lat", 0, 0), 0, keepdims=True)
    rows = jnp.broadcast_to(row, (lax.axis_size("lon"), row.shape[1]))
    return lax.all_to_all(rows, "lon", 0, 0)


def halo(x, first, last, lat, lon):
    def moved(a, axis, step):
        size = lax.axis_size(axis)
        pairs = [(i, i + step) for i in range(size) if 0 <= i + step < size]
        return lax.ppermute(a, axis, pairs)

    north = moved(last, "lat", 1)
    south = moved(first, "lat", -1)
    grid = x.reshape((lat, lon) + x.shape[1:])
    right = jnp.concatenate([north[None, lon - 1], grid[:, lon - 1], south[None, lon - 1]], 0)
    left = jnp.concatenate([north[None, 0], grid[:, 0], south[None, 0]], 0)
    west = moved(right, "lon", 1)
    east = moved(left, "lon", -1)
    return north, south, west, east


def body(
    base_state,
    tangent,
    blocks,
    pattern,
    live,
    column_inverse,
    col_depth,
    uptake_rate,
    stoich,
    basis,
):
    tracers, lat, lon, points = base_state.shape
    slots = pattern.shape[2]
    count = basis.shape[0]
    rows = lat * lon
    total_lon = lon * lax.axis_size("lon")
    size = tracers * rows
    places = (lat + 2) * (lon + 2) + 1
    share = stoich.reshape(1, tracers)

    x, first, last, own = call(
        functools.partial(pack_kernel, lon),
        (
            like((rows, 2 * tracers, points), BF16),
            like((lon, 2 * tracers, points), BF16),
            like((lon, 2 * tracers, points), BF16),
            like((2, rows, points)),
        ),
        [HBM] * 2,
        [VMEM] * 4,
        scratch=[pltpu.VMEM((size, points), F32)] * 2 + [pltpu.SemaphoreType.DMA((2,))],
        size=400000,
    )(base_state.reshape(size, points), tangent.reshape(size, points))

    index, high, low, source, rate_column, gram, flat_basis, held = call(
        functools.partial(prep_kernel, total_lon),
        (
            like((lat, lon, slots), jnp.int32),
            like((rows, points, points), BF16),
            like((rows, points, points), BF16),
            like((rows, points, 2 * tracers)),
            like((points, (rows + 7) // 8 * 8)),
            like((16, points)),
            like((count, size, points)),
            like((rows * slots, points, points), BF16),
        ),
        [HBM] * 8 + [VMEM],
        [VMEM] * 8,
        scratch=[
            pltpu.VMEM(pattern.shape, jnp.int32),
            pltpu.VMEM(live.shape, jnp.int32),
            pltpu.VMEM(column_inverse.shape, F32),
            pltpu.VMEM(col_depth.shape, jnp.int32),
            pltpu.VMEM(uptake_rate.shape, F32),
            pltpu.VMEM(share.shape, F32),
            pltpu.SemaphoreType.DMA((8,)),
        ],
        flops=20000000,
        size=8000000,
    )(
        pattern,
        live,
        column_inverse,
        col_depth,
        uptake_rate,
        share,
        basis.reshape(count, size, points),
        blocks.reshape(rows * slots, points, points),
        own,
    )

    north, south, west, east = halo(x, first, last, lat, lon)
    work = 2 * 2 * tracers * rows * slots * points * points
    x, first, last, state = call(
        functools.partial(first_kernel, lat, lon),
        (
            like((rows, tracers, points), BF16),
            like((lon, tracers, points), BF16),
            like((lon, tracers, points), BF16),
            like((rows, points, 2 * tracers)),
        ),
        [SMEM] + [VMEM] * 9,
        [VMEM] * 4,
        scratch=[pltpu.VMEM((places, 2 * tracers, points), BF16)],
        flops=work,
        size=5000000,
    )(index, x, north, south, west, east, held, high, low, source)

    source = call(
        pull_kernel, like((rows, points, tracers)), [VMEM] * 3, VMEM, flops=100000, size=2000000
    )(state, rate_column, share)

    north, south, west, east = halo(x, first, last, lat, lon)
    product, sums = call(
        functools.partial(second_kernel, lat, lon),
        (like((size, points)), like((lax.axis_size("lat"), points))),
        [SMEM] + [VMEM] * 11,
        [VMEM] * 2,
        scratch=[pltpu.VMEM((places, tracers, points), BF16)],
        flops=work // 2,
        size=5000000,
    )(index, x, north, south, west, east, held, high, low, source, gram, flat_basis)

    parts = summed(sums)
    following, written, coeffs, flag = call(
        last_kernel,
        (like((size, points)), like((size, points)), like((count + 1,)), like((1,), jnp.int32)),
        [VMEM] * 3,
        [VMEM, HBM, SMEM, SMEM],
        scratch=[pltpu.SemaphoreType.DMA],
        size=700000,
    )(parts, product, flat_basis)

    def again(carry):
        following, coeffs, flag = carry
        rest = product - jnp.einsum(
            "k,ksp->sp", coeffs[:count], flat_basis, precision=lax.Precision.HIGHEST
        )
        part = jnp.pad(jnp.sum(rest * rest).reshape(1, 1), ((0, 0), (0, points - 1)))
        squared = jnp.sum(summed(jnp.broadcast_to(part, (lax.axis_size("lat"), points))), 0)[0]
        beta = jnp.sqrt(squared + 1e-06)
        return rest / beta, jnp.concatenate([coeffs[:count], beta[None]]), flag * 0

    following, coeffs, flag = lax.while_loop(
        lambda carry: carry[2][0] > 0, again, (following, coeffs, flag)
    )
    shape = base_state.shape
    return written.reshape(shape), following.reshape(shape), coeffs


def solution(mesh):
    placed = (
        P(None, "lat", "lon", None),
        P(None, "lat", "lon", None),
        P("lat", "lon", None, None, None),
        P("lat", "lon", None),
        P("lat", "lon", None),
        P("lat", "lon", None, None, None),
        P("lat", "lon", None),
        P("lat", "lon", None),
        P(),
        P(None, None, "lat", "lon", None),
    )
    return jax.shard_map(
        body,
        mesh=mesh,
        in_specs=placed,
        out_specs=(P(None, "lat", "lon", None), P(None, "lat", "lon", None), P()),
        check_vma=False,
    )
```

```python
import functools

import jax
import jax.numpy as jnp
from jax import lax
from jax.experimental import pallas as pl
from jax.experimental.pallas import tpu as pltpu
from jax.sharding import PartitionSpec as P

F32 = jnp.float32
BF16 = jnp.bfloat16
VMEM = pl.BlockSpec(memory_space=pltpu.VMEM)
SMEM = pl.BlockSpec(memory_space=pltpu.SMEM)
HBM = pl.BlockSpec(memory_space=pltpu.HBM)
PACK = 20000000000
PREP = 10000000000
NT = (((1,), (1,)), ((), ()))


def call(kernel, outs, ins, out_specs, scratch=(), flops=0, size=0, limit=16):
    return pl.pallas_call(
        kernel,
        out_shape=outs,
        in_specs=ins,
        out_specs=out_specs,
        scratch_shapes=list(scratch),
        compiler_params=pltpu.CompilerParams(vmem_limit_bytes=limit * 2**20),
        cost_estimate=pl.CostEstimate(flops=flops, bytes_accessed=size, transcendentals=0),
    )


def like(shape, dtype=F32):
    return jax.ShapeDtypeStruct(shape, dtype)


def iota(shape, dim):
    return lax.broadcasted_iota(jnp.int32, shape, dim)


def pack_kernel(lon, c_hbm, v_hbm, x_ref, first_ref, last_ref, c_ref, v_ref, sems):
    copies = [
        pltpu.make_async_copy(c_hbm, c_ref, sems.at[0]),
        pltpu.make_async_copy(v_hbm, v_ref, sems.at[1]),
    ]
    for copy in copies:
        copy.start()
    for copy in copies:
        copy.wait()
    rows = x_ref.shape[0]
    tracers = c_ref.shape[0] // rows
    for r in range(rows):
        at = pl.ds(r, tracers, stride=rows)
        x = jnp.concatenate([c_ref[at, :], v_ref[at, :]], 0).astype(BF16)
        x_ref[r] = x
        if r < lon:
            first_ref[r] = x
        if r >= rows - lon:
            last_ref[r - (rows - lon)] = x


def prep_kernel(
    total_lon,
    pattern_ref,
    live_ref,
    inverse_ref,
    depth_ref,
    rate_ref,
    stoich_ref,
    basis_ref,
    c_ref,
    v_ref,
    index_ref,
    high_ref,
    low_ref,
    source_ref,
    rate_column_ref,
    gram_ref,
):
    lat, lon, slots = pattern_ref.shape
    rows = lat * lon
    columns, levels = inverse_ref.shape[2:4]
    points = columns * levels
    pattern = pattern_ref[...]
    itself = pattern[:, :, :1]
    far_lat = pattern // total_lon - itself // total_lon
    far_lon = pattern % total_lon - itself % total_lon
    shape = pattern.shape
    place = (iota(shape, 0) + 1 + far_lat) * (lon + 2) + iota(shape, 1) + 1 + far_lon
    index_ref[...] = jnp.where(live_ref[...] > 0, place, (lat + 2) * (lon + 2))

    lane = iota((rows, points), 1)
    depth = jnp.concatenate([depth_ref[i] for i in range(lat)], 0)
    below = jnp.zeros((rows, points), jnp.int32)
    for k in range(columns):
        below = jnp.where(lane // levels == k, depth[:, k : k + 1], below)
    wet = (lane % levels < below).astype(F32)

    rate = jnp.concatenate([rate_ref[i] for i in range(lat)], 0)
    uptake, pull = sources(c_ref[:rows, :], v_ref[:rows, :], rate)
    spare = 8 - rows % 8 if rows % 8 else 0
    blank = [jnp.zeros((spare, points), F32)] if spare else []
    columns_of = [
        jnp.transpose(jnp.concatenate([part] + blank, 0)) for part in (uptake, pull, rate, wet)
    ]
    rate_column_ref[...] = columns_of[2]
    tracers = source_ref.shape[2] // 2
    share = stoich_ref[...]
    nothing = jnp.zeros((1, tracers), F32)
    share_c = jnp.concatenate([share, nothing], 1)
    share_v = jnp.concatenate([nothing, share], 1)
    for r in range(rows):
        at = slice(r, r + 1)
        source_ref[r] = columns_of[0][:, at] * share_c + columns_of[1][:, at] * share_v

    spread = (iota((levels, points), 1) % levels == iota((levels, points), 0)).astype(BF16)
    full = (points, points)
    same = iota(full, 0) // levels == iota(full, 1) // levels
    for r in range(rows):
        at = slice(r, r + 1)
        inverse = inverse_ref[r // lon, r % lon].reshape(points, levels)
        high = inverse.astype(BF16)
        low = (inverse - high.astype(F32)).astype(BF16)
        keep = jnp.where(same, wet[at, :] * columns_of[3][:, at], 0.0)
        for ref, part in ((high_ref, high), (low_ref, low)):
            tiled = jnp.dot(part, spread, preferred_element_type=F32)
            ref[r] = (tiled * keep).astype(BF16)

    gram_ref[...] = jnp.zeros(gram_ref.shape, F32)
    count = basis_ref.shape[0]
    row = 0
    for k in range(count):
        for j in range(k, count):
            gram_ref[row : row + 1, :] = jnp.sum(basis_ref[k] * basis_ref[j], 0, keepdims=True)
            row += 1


def sources(own_c, own_v, rate):
    denom = own_c * own_c + 1.0
    uptake = rate * own_c * own_c / denom
    slope = rate * 2.0 * own_c / (denom * denom)
    return uptake, slope * own_v


def pull_kernel(state_ref, rate_column_ref, stoich_ref, source_ref):
    rows, _, tracers = source_ref.shape
    share = stoich_ref[...]
    for r in range(rows):
        own_c = state_ref[r, :, 0:1]
        own_v = state_ref[r, :, tracers : tracers + 1]
        source_ref[r] = sources(own_c, own_v, rate_column_ref[:, r : r + 1])[1] * share


def fill(pad_ref, x_ref, north_ref, south_ref, west_ref, east_ref, lat, lon):
    wide = lon + 2
    for j in range(lon):
        pad_ref[1 + j] = north_ref[j]
        pad_ref[(lat + 1) * wide + 1 + j] = south_ref[j]
        for i in range(lat):
            pad_ref[(i + 1) * wide + 1 + j] = x_ref[i * lon + j]
    for i in range(lat + 2):
        pad_ref[i * wide] = west_ref[i]
        pad_ref[i * wide + lon + 1] = east_ref[i]
    pad_ref[(lat + 2) * wide] = jnp.zeros(pad_ref.shape[1:], BF16)


def transport(r, index_ref, pad_ref, held_ref, source_ref):
    lon, slots = index_ref.shape[1:]
    z = source_ref[r]
    for s in range(slots):
        x = pad_ref[index_ref[r // lon, r % lon, s]]
        z = z + lax.dot_general(held_ref[r * slots + s], x, NT, preferred_element_type=F32)
    return z


def mix(z, high, low):
    z_high = z.astype(BF16)
    z_low = (z - z_high.astype(F32)).astype(BF16)
    dot = functools.partial(jnp.dot, preferred_element_type=F32)
    return dot(high, z_high) + (dot(low, z_high) + dot(high, z_low))


def first_kernel(
    lat,
    lon,
    index_ref,
    x_ref,
    north_ref,
    south_ref,
    west_ref,
    east_ref,
    held_ref,
    high_ref,
    low_ref,
    source_ref,
    y_ref,
    first_ref,
    last_ref,
    state_ref,
    pad_ref,
):
    rows = lat * lon
    fill(pad_ref, x_ref, north_ref, south_ref, west_ref, east_ref, lat, lon)
    tracers = y_ref.shape[1]
    for r in range(rows):
        state_ref[r] = transport(r, index_ref, pad_ref, held_ref, source_ref)
    for r in range(rows):
        state_ref[r] = mix(state_ref[r], high_ref[r], low_ref[r])
    for r in range(rows):
        y = jnp.transpose(state_ref[r])[tracers:].astype(BF16)
        y_ref[r] = y
        if r < lon:
            first_ref[r] = y
        if r >= rows - lon:
            last_ref[r - (rows - lon)] = y


def second_kernel(
    lat,
    lon,
    index_ref,
    x_ref,
    north_ref,
    south_ref,
    west_ref,
    east_ref,
    held_ref,
    high_ref,
    low_ref,
    source_ref,
    gram_ref,
    basis_ref,
    product_ref,
    sums_ref,
    pad_ref,
    state_ref,
):
    rows = lat * lon
    fill(pad_ref, x_ref, north_ref, south_ref, west_ref, east_ref, lat, lon)
    tracers = x_ref.shape[1]
    for r in range(rows):
        state_ref[r] = transport(r, index_ref, pad_ref, held_ref, source_ref)
    for r in range(rows):
        state_ref[r] = mix(state_ref[r], high_ref[r], low_ref[r])
    for r in range(rows):
        product_ref[pl.ds(r, tracers, stride=rows), :] = jnp.transpose(state_ref[r])
    product = product_ref[...]
    count = basis_ref.shape[0]
    pairs = count * (count + 1) // 2
    all_sums = gram_ref[...]
    spot = iota(all_sums.shape, 0)
    for k in range(count + 1):
        other = basis_ref[k] if k < count else product
        part = jnp.sum(product * other, 0, keepdims=True)
        all_sums = jnp.where(spot == pairs + k, part, all_sums)
    column = jnp.sum(all_sums, 1, keepdims=True)
    row = jnp.sum(jnp.where(spot == iota(spot.shape, 1), column, 0.0), 0, keepdims=True)
    sums_ref[...] = jnp.broadcast_to(row, sums_ref.shape)


def last_kernel(
    parts_ref, product_ref, basis_ref, next_ref, out_hbm, coeffs_ref, flag_ref, sem
):
    copy = pltpu.make_async_copy(product_ref, out_hbm, sem)
    copy.start()
    count = basis_ref.shape[0]
    row = jnp.sum(parts_ref[...], 0, keepdims=True)
    lane = iota(row.shape, 1)

    def pick(at):
        return jnp.sum(jnp.where(lane == at, row, 0.0), 1, keepdims=True)

    pairs = count * (count + 1) // 2
    heights = [pick(pairs + k) for k in range(count)]
    whole = pick(pairs + count)
    cross = jnp.zeros((1, 1), F32)
    at = 0
    for k in range(count):
        for j in range(k, count):
            twice = 1.0 if k == j else 2.0
            cross = cross + twice * (heights[k] * heights[j] * pick(at))
            at += 1
    squares = sum(h * h for h in heights)
    short = whole - 2.0 * squares + cross
    size = whole + 2.0 * squares + cross
    beta = jnp.sqrt(jnp.maximum(short, 0.0) + 1e-06)
    rest = product_ref[...]
    for k in range(count):
        rest = rest - heights[k] * basis_ref[k]
    next_ref[...] = rest / beta
    for k in range(count):
        coeffs_ref[k] = heights[k][0, 0]
    coeffs_ref[count] = beta[0, 0]
    flag_ref[0] = jnp.where(short < 0.01 * size, 1, 0)[0, 0]
    copy.wait()


def summed(rows):
    row = jnp.sum(lax.all_to_all(rows, "lat", 0, 0), 0, keepdims=True)
    rows = jnp.broadcast_to(row, (lax.axis_size("lon"), row.shape[1]))
    return lax.all_to_all(rows, "lon", 0, 0)


def halo(x, first, last, lat, lon):
    def moved(a, axis, step):
        size = lax.axis_size(axis)
        pairs = [(i, i + step) for i in range(size) if 0 <= i + step < size]
        return lax.ppermute(a, axis, pairs)

    north = moved(last, "lat", 1)
    south = moved(first, "lat", -1)
    grid = x.reshape((lat, lon) + x.shape[1:])
    right = jnp.concatenate([north[None, lon - 1], grid[:, lon - 1], south[None, lon - 1]], 0)
    left = jnp.concatenate([north[None, 0], grid[:, 0], south[None, 0]], 0)
    west = moved(right, "lon", 1)
    east = moved(left, "lon", -1)
    return north, south, west, east


def body(
    base_state,
    tangent,
    blocks,
    pattern,
    live,
    column_inverse,
    col_depth,
    uptake_rate,
    stoich,
    basis,
):
    tracers, lat, lon, points = base_state.shape
    slots = pattern.shape[2]
    count = basis.shape[0]
    rows = lat * lon
    total_lon = lon * lax.axis_size("lon")
    size = tracers * rows
    places = (lat + 2) * (lon + 2) + 1
    share = stoich.reshape(1, tracers)

    flat_c = base_state.reshape(size, points)
    flat_v = tangent.reshape(size, points)
    x, first, last = call(
        functools.partial(pack_kernel, lon),
        (
            like((rows, 2 * tracers, points), BF16),
            like((lon, 2 * tracers, points), BF16),
            like((lon, 2 * tracers, points), BF16),
        ),
        [HBM] * 2,
        [VMEM] * 3,
        scratch=[pltpu.VMEM((size, points), F32)] * 2 + [pltpu.SemaphoreType.DMA((2,))],
        size=400000,
        flops=PACK,
        limit=59,
    )(flat_c, flat_v)

    flat_basis = basis.reshape(count, size, points)
    held = blocks.reshape(rows * slots, points, points)
    index, high, low, source, rate_column, gram = call(
        functools.partial(prep_kernel, total_lon),
        (
            like((lat, lon, slots), jnp.int32),
            like((rows, points, points), BF16),
            like((rows, points, points), BF16),
            like((rows, points, 2 * tracers)),
            like((points, (rows + 7) // 8 * 8)),
            like((16, points)),
        ),
        [VMEM] * 9,
        [VMEM] * 6,
        flops=PREP,
        size=8000000,
    )(
        pattern,
        live,
        column_inverse,
        col_depth,
        uptake_rate,
        share,
        flat_basis,
        flat_c,
        flat_v,
    )

    north, south, west, east = halo(x, first, last, lat, lon)
    work = 2 * 2 * tracers * rows * slots * points * points
    x, first, last, state = call(
        functools.partial(first_kernel, lat, lon),
        (
            like((rows, tracers, points), BF16),
            like((lon, tracers, points), BF16),
            like((lon, tracers, points), BF16),
            like((rows, points, 2 * tracers)),
        ),
        [SMEM] + [VMEM] * 9,
        [VMEM] * 4,
        scratch=[pltpu.VMEM((places, 2 * tracers, points), BF16)],
        flops=work,
        size=5000000,
    )(index, x, north, south, west, east, held, high, low, source)

    source = call(
        pull_kernel, like((rows, points, tracers)), [VMEM] * 3, VMEM, flops=100000, size=2000000
    )(state, rate_column, share)

    north, south, west, east = halo(x, first, last, lat, lon)
    product, sums = call(
        functools.partial(second_kernel, lat, lon),
        (like((size, points)), like((lax.axis_size("lat"), points))),
        [SMEM] + [VMEM] * 11,
        [VMEM] * 2,
        scratch=[
            pltpu.VMEM((places, tracers, points), BF16),
            pltpu.VMEM((rows, points, tracers), F32),
        ],
        flops=work // 2,
        size=5000000,
    )(index, x, north, south, west, east, held, high, low, source, gram, flat_basis)

    parts = summed(sums)
    following, written, coeffs, flag = call(
        last_kernel,
        (like((size, points)), like((size, points)), like((count + 1,)), like((1,), jnp.int32)),
        [VMEM] * 3,
        [VMEM, HBM, SMEM, SMEM],
        scratch=[pltpu.SemaphoreType.DMA],
        size=700000,
    )(parts, product, flat_basis)

    def again(carry):
        following, coeffs, flag = carry
        rest = product - jnp.einsum(
            "k,ksp->sp", coeffs[:count], flat_basis, precision=lax.Precision.HIGHEST
        )
        part = jnp.pad(jnp.sum(rest * rest).reshape(1, 1), ((0, 0), (0, points - 1)))
        squared = jnp.sum(summed(jnp.broadcast_to(part, (lax.axis_size("lat"), points))), 0)[0]
        beta = jnp.sqrt(squared + 1e-06)
        return rest / beta, jnp.concatenate([coeffs[:count], beta[None]]), flag * 0

    following, coeffs, flag = lax.while_loop(
        lambda carry: carry[2][0] > 0, again, (following, coeffs, flag)
    )
    shape = base_state.shape
    return written.reshape(shape), following.reshape(shape), coeffs


def solution(mesh):
    placed = (
        P(None, "lat", "lon", None),
        P(None, "lat", "lon", None),
        P("lat", "lon", None, None, None),
        P("lat", "lon", None),
        P("lat", "lon", None),
        P("lat", "lon", None, None, None),
        P("lat", "lon", None),
        P("lat", "lon", None),
        P(),
        P(None, None, "lat", "lon", None),
    )
    return jax.shard_map(
        body,
        mesh=mesh,
        in_specs=placed,
        out_specs=(P(None, "lat", "lon", None), P(None, "lat", "lon", None), P()),
        check_vma=False,
    )
```

```python
import functools

import jax
import jax.numpy as jnp
from jax import lax
from jax.experimental import pallas as pl
from jax.experimental.pallas import tpu as pltpu
from jax.sharding import PartitionSpec as P

F32 = jnp.float32
BF16 = jnp.bfloat16
VMEM = pl.BlockSpec(memory_space=pltpu.VMEM)
SMEM = pl.BlockSpec(memory_space=pltpu.SMEM)
HBM = pl.BlockSpec(memory_space=pltpu.HBM)
PACK = 20000000000
PREP = 10000000000
NT = (((1,), (1,)), ((), ()))


def call(kernel, outs, ins, out_specs, scratch=(), flops=0, size=0, limit=16):
    return pl.pallas_call(
        kernel,
        out_shape=outs,
        in_specs=ins,
        out_specs=out_specs,
        scratch_shapes=list(scratch),
        compiler_params=pltpu.CompilerParams(vmem_limit_bytes=limit * 2**20),
        cost_estimate=pl.CostEstimate(flops=flops, bytes_accessed=size, transcendentals=0),
    )


def like(shape, dtype=F32):
    return jax.ShapeDtypeStruct(shape, dtype)


def iota(shape, dim):
    return lax.broadcasted_iota(jnp.int32, shape, dim)


def pack_kernel(lon, c_hbm, v_hbm, x_ref, first_ref, last_ref, c_ref, v_ref, sems):
    copies = [
        pltpu.make_async_copy(c_hbm, c_ref, sems.at[0]),
        pltpu.make_async_copy(v_hbm, v_ref, sems.at[1]),
    ]
    for copy in copies:
        copy.start()
    for copy in copies:
        copy.wait()
    rows = x_ref.shape[0]
    tracers = c_ref.shape[0] // rows
    for r in range(rows):
        at = pl.ds(r, tracers, stride=rows)
        x = jnp.concatenate([c_ref[at, :], v_ref[at, :]], 0).astype(BF16)
        x_ref[r] = x
        if r < lon:
            first_ref[r] = x
        if r >= rows - lon:
            last_ref[r - (rows - lon)] = x


def prep_kernel(
    total_lon,
    pattern_ref,
    live_ref,
    inverse_ref,
    depth_ref,
    rate_ref,
    stoich_ref,
    basis_ref,
    c_ref,
    v_ref,
    index_ref,
    high_ref,
    low_ref,
    source_ref,
    rate_column_ref,
    gram_ref,
):
    lat, lon, slots = pattern_ref.shape
    rows = lat * lon
    columns, levels = inverse_ref.shape[2:4]
    points = columns * levels
    pattern = pattern_ref[...]
    itself = pattern[:, :, :1]
    far_lat = pattern // total_lon - itself // total_lon
    far_lon = pattern % total_lon - itself % total_lon
    shape = pattern.shape
    place = (iota(shape, 0) + 1 + far_lat) * (lon + 2) + iota(shape, 1) + 1 + far_lon
    index_ref[...] = jnp.where(live_ref[...] > 0, place, (lat + 2) * (lon + 2))

    lane = iota((rows, points), 1)
    depth = jnp.concatenate([depth_ref[i] for i in range(lat)], 0)
    below = jnp.zeros((rows, points), jnp.int32)
    for k in range(columns):
        below = jnp.where(lane // levels == k, depth[:, k : k + 1], below)
    wet = (lane % levels < below).astype(F32)

    rate = jnp.concatenate([rate_ref[i] for i in range(lat)], 0)
    uptake, pull = sources(c_ref[:rows, :], v_ref[:rows, :], rate)
    spare = 8 - rows % 8 if rows % 8 else 0
    blank = [jnp.zeros((spare, points), F32)] if spare else []
    columns_of = [
        jnp.transpose(jnp.concatenate([part] + blank, 0)) for part in (uptake, pull, rate, wet)
    ]
    rate_column_ref[...] = columns_of[2]
    tracers = source_ref.shape[2] // 2
    share = stoich_ref[...]
    nothing = jnp.zeros((1, tracers), F32)
    share_c = jnp.concatenate([share, nothing], 1)
    share_v = jnp.concatenate([nothing, share], 1)
    for r in range(rows):
        at = slice(r, r + 1)
        source_ref[r] = columns_of[0][:, at] * share_c + columns_of[1][:, at] * share_v

    spread = (iota((levels, points), 1) % levels == iota((levels, points), 0)).astype(BF16)
    full = (points, points)
    same = iota(full, 0) // levels == iota(full, 1) // levels
    for r in range(rows):
        at = slice(r, r + 1)
        inverse = inverse_ref[r // lon, r % lon].reshape(points, levels)
        high = inverse.astype(BF16)
        low = (inverse - high.astype(F32)).astype(BF16)
        keep = jnp.where(same, wet[at, :] * columns_of[3][:, at], 0.0)
        for ref, part in ((high_ref, high), (low_ref, low)):
            tiled = jnp.dot(part, spread, preferred_element_type=F32)
            ref[r] = (tiled * keep).astype(BF16)

    gram_ref[...] = jnp.zeros(gram_ref.shape, F32)
    count = basis_ref.shape[0]
    row = 0
    for k in range(count):
        for j in range(k, count):
            gram_ref[row : row + 1, :] = jnp.sum(basis_ref[k] * basis_ref[j], 0, keepdims=True)
            row += 1


def sources(own_c, own_v, rate):
    denom = own_c * own_c + 1.0
    uptake = rate * own_c * own_c / denom
    slope = rate * 2.0 * own_c / (denom * denom)
    return uptake, slope * own_v


def pull_kernel(state_ref, rate_column_ref, stoich_ref, source_ref):
    rows, _, tracers = source_ref.shape
    share = stoich_ref[...]
    for r in range(rows):
        own_c = state_ref[r, :, 0:1]
        own_v = state_ref[r, :, tracers : tracers + 1]
        source_ref[r] = sources(own_c, own_v, rate_column_ref[:, r : r + 1])[1] * share


def fill(pad_ref, x_ref, north_ref, south_ref, west_ref, east_ref, lat, lon):
    wide = lon + 2
    for j in range(lon):
        pad_ref[1 + j] = north_ref[j]
        pad_ref[(lat + 1) * wide + 1 + j] = south_ref[j]
        for i in range(lat):
            pad_ref[(i + 1) * wide + 1 + j] = x_ref[i * lon + j]
    for i in range(lat + 2):
        pad_ref[i * wide] = west_ref[i]
        pad_ref[i * wide + lon + 1] = east_ref[i]
    pad_ref[(lat + 2) * wide] = jnp.zeros(pad_ref.shape[1:], BF16)


def transport(r, index_ref, pad_ref, held_ref, source_ref):
    lon, slots = index_ref.shape[1:]
    z = source_ref[r]
    for s in range(slots):
        x = pad_ref[index_ref[r // lon, r % lon, s]]
        z = z + lax.dot_general(held_ref[r * slots + s], x, NT, preferred_element_type=F32)
    return z


def mix(z, high, low):
    z_high = z.astype(BF16)
    z_low = (z - z_high.astype(F32)).astype(BF16)
    dot = functools.partial(jnp.dot, preferred_element_type=F32)
    return dot(high, z_high) + (dot(low, z_high) + dot(high, z_low))


def first_kernel(
    lat,
    lon,
    index_ref,
    x_ref,
    north_ref,
    south_ref,
    west_ref,
    east_ref,
    held_ref,
    high_ref,
    low_ref,
    source_ref,
    y_ref,
    first_ref,
    last_ref,
    state_ref,
    pad_ref,
):
    rows = lat * lon
    fill(pad_ref, x_ref, north_ref, south_ref, west_ref, east_ref, lat, lon)
    tracers = y_ref.shape[1]
    for r in range(rows):
        state_ref[r] = transport(r, index_ref, pad_ref, held_ref, source_ref)
    for r in range(rows):
        state_ref[r] = mix(state_ref[r], high_ref[r], low_ref[r])
    for r in range(rows):
        y = jnp.transpose(state_ref[r])[tracers:].astype(BF16)
        y_ref[r] = y
        if r < lon:
            first_ref[r] = y
        if r >= rows - lon:
            last_ref[r - (rows - lon)] = y


def second_kernel(
    lat,
    lon,
    index_ref,
    x_ref,
    north_ref,
    south_ref,
    west_ref,
    east_ref,
    held_ref,
    high_ref,
    low_ref,
    source_ref,
    gram_ref,
    basis_ref,
    product_ref,
    sums_ref,
    pad_ref,
    state_ref,
):
    rows = lat * lon
    fill(pad_ref, x_ref, north_ref, south_ref, west_ref, east_ref, lat, lon)
    tracers = x_ref.shape[1]
    for r in range(rows):
        state_ref[r] = transport(r, index_ref, pad_ref, held_ref, source_ref)
    for r in range(rows):
        state_ref[r] = mix(state_ref[r], high_ref[r], low_ref[r])
    for r in range(rows):
        product_ref[pl.ds(r, tracers, stride=rows), :] = jnp.transpose(state_ref[r])
    product = product_ref[...]
    count = basis_ref.shape[0]
    pairs = count * (count + 1) // 2
    all_sums = gram_ref[...]
    spot = iota(all_sums.shape, 0)
    for k in range(count + 1):
        other = basis_ref[k] if k < count else product
        part = jnp.sum(product * other, 0, keepdims=True)
        all_sums = jnp.where(spot == pairs + k, part, all_sums)
    column = jnp.sum(all_sums, 1, keepdims=True)
    row = jnp.sum(jnp.where(spot == iota(spot.shape, 1), column, 0.0), 0, keepdims=True)
    sums_ref[...] = jnp.broadcast_to(row, sums_ref.shape)


def last_kernel(
    parts_ref, product_ref, basis_ref, next_ref, out_hbm, coeffs_ref, flag_ref, sem
):
    copy = pltpu.make_async_copy(product_ref, out_hbm, sem)
    copy.start()
    count = basis_ref.shape[0]
    row = jnp.sum(parts_ref[...], 0, keepdims=True)
    lane = iota(row.shape, 1)

    def pick(at):
        return jnp.sum(jnp.where(lane == at, row, 0.0), 1, keepdims=True)

    pairs = count * (count + 1) // 2
    heights = [pick(pairs + k) for k in range(count)]
    whole = pick(pairs + count)
    cross = jnp.zeros((1, 1), F32)
    at = 0
    for k in range(count):
        for j in range(k, count):
            twice = 1.0 if k == j else 2.0
            cross = cross + twice * (heights[k] * heights[j] * pick(at))
            at += 1
    squares = sum(h * h for h in heights)
    short = whole - 2.0 * squares + cross
    size = whole + 2.0 * squares + cross
    beta = jnp.sqrt(jnp.maximum(short, 0.0) + 1e-06)
    rest = product_ref[...]
    for k in range(count):
        rest = rest - heights[k] * basis_ref[k]
    next_ref[...] = rest / beta
    for k in range(count):
        coeffs_ref[k] = heights[k][0, 0]
    coeffs_ref[count] = beta[0, 0]
    flag_ref[0] = jnp.where(short < 0.01 * size, 1, 0)[0, 0]
    copy.wait()


def summed(rows):
    row = jnp.sum(lax.all_to_all(rows, "lon", 0, 0), 0, keepdims=True)
    rows = jnp.broadcast_to(row, (lax.axis_size("lat"), row.shape[1]))
    return lax.all_to_all(rows, "lat", 0, 0)


def halo(x, first, last, lat, lon, beside=None):
    def moved(a, axis, step):
        size = lax.axis_size(axis)
        return lax.ppermute(a, axis, [(i, (i + step) % size) for i in range(size)])

    north = moved(last, "lat", 1)
    south = moved(first, "lat", -1)
    if beside is not None:
        north, south, beside = lax.optimization_barrier((north, south, beside))
    grid = x.reshape((lat, lon) + x.shape[1:])
    right = jnp.concatenate([north[None, lon - 1], grid[:, lon - 1], south[None, lon - 1]], 0)
    left = jnp.concatenate([north[None, 0], grid[:, 0], south[None, 0]], 0)
    west = moved(right, "lon", 1)
    east = moved(left, "lon", -1)
    return north, south, west, east, beside


def body(
    base_state,
    tangent,
    blocks,
    pattern,
    live,
    column_inverse,
    col_depth,
    uptake_rate,
    stoich,
    basis,
):
    tracers, lat, lon, points = base_state.shape
    slots = pattern.shape[2]
    count = basis.shape[0]
    rows = lat * lon
    total_lon = lon * lax.axis_size("lon")
    size = tracers * rows
    places = (lat + 2) * (lon + 2) + 1
    share = stoich.reshape(1, tracers)

    flat_c = base_state.reshape(size, points)
    flat_v = tangent.reshape(size, points)
    x, first, last = call(
        functools.partial(pack_kernel, lon),
        (
            like((rows, 2 * tracers, points), BF16),
            like((lon, 2 * tracers, points), BF16),
            like((lon, 2 * tracers, points), BF16),
        ),
        [HBM] * 2,
        [VMEM] * 3,
        scratch=[pltpu.VMEM((size, points), F32)] * 2 + [pltpu.SemaphoreType.DMA((2,))],
        size=400000,
        flops=PACK,
        limit=59,
    )(flat_c, flat_v)

    flat_basis = basis.reshape(count, size, points)
    held = blocks.reshape(rows * slots, points, points)
    index, high, low, source, rate_column, gram = call(
        functools.partial(prep_kernel, total_lon),
        (
            like((lat, lon, slots), jnp.int32),
            like((rows, points, points), BF16),
            like((rows, points, points), BF16),
            like((rows, points, 2 * tracers)),
            like((points, (rows + 7) // 8 * 8)),
            like((16, points)),
        ),
        [VMEM] * 9,
        [VMEM] * 6,
        flops=PREP,
        size=8000000,
    )(
        pattern,
        live,
        column_inverse,
        col_depth,
        uptake_rate,
        share,
        flat_basis,
        flat_c,
        flat_v,
    )

    north, south, west, east, _ = halo(x, first, last, lat, lon)
    work = 2 * 2 * tracers * rows * slots * points * points
    x, first, last, state = call(
        functools.partial(first_kernel, lat, lon),
        (
            like((rows, tracers, points), BF16),
            like((lon, tracers, points), BF16),
            like((lon, tracers, points), BF16),
            like((rows, points, 2 * tracers)),
        ),
        [SMEM] + [VMEM] * 9,
        [VMEM] * 4,
        scratch=[pltpu.VMEM((places, 2 * tracers, points), BF16)],
        flops=work,
        size=5000000,
    )(index, x, north, south, west, east, held, high, low, source)

    source = call(
        pull_kernel, like((rows, points, tracers)), [VMEM] * 3, VMEM, flops=100000, size=2000000
    )(state, rate_column, share)

    north, south, west, east, source = halo(x, first, last, lat, lon, source)
    product, sums = call(
        functools.partial(second_kernel, lat, lon),
        (like((size, points)), like((lax.axis_size("lon"), points))),
        [SMEM] + [VMEM] * 11,
        [VMEM] * 2,
        scratch=[
            pltpu.VMEM((places, tracers, points), BF16),
            pltpu.VMEM((rows, points, tracers), F32),
        ],
        flops=work // 2,
        size=5000000,
    )(index, x, north, south, west, east, held, high, low, source, gram, flat_basis)

    parts = summed(sums)
    following, written, coeffs, flag = call(
        last_kernel,
        (like((size, points)), like((size, points)), like((count + 1,)), like((1,), jnp.int32)),
        [VMEM] * 3,
        [VMEM, HBM, SMEM, SMEM],
        scratch=[pltpu.SemaphoreType.DMA],
        size=700000,
    )(parts, product, flat_basis)

    def again(carry):
        following, coeffs, flag = carry
        rest = product - jnp.einsum(
            "k,ksp->sp", coeffs[:count], flat_basis, precision=lax.Precision.HIGHEST
        )
        part = jnp.pad(jnp.sum(rest * rest).reshape(1, 1), ((0, 0), (0, points - 1)))
        squared = jnp.sum(summed(jnp.broadcast_to(part, (lax.axis_size("lon"), points))), 0)[0]
        beta = jnp.sqrt(squared + 1e-06)
        return rest / beta, jnp.concatenate([coeffs[:count], beta[None]]), flag * 0

    following, coeffs, flag = lax.while_loop(
        lambda carry: carry[2][0] > 0, again, (following, coeffs, flag)
    )
    shape = base_state.shape
    return written.reshape(shape), following.reshape(shape), coeffs


def solution(mesh):
    placed = (
        P(None, "lat", "lon", None),
        P(None, "lat", "lon", None),
        P("lat", "lon", None, None, None),
        P("lat", "lon", None),
        P("lat", "lon", None),
        P("lat", "lon", None, None, None),
        P("lat", "lon", None),
        P("lat", "lon", None),
        P(),
        P(None, None, "lat", "lon", None),
    )
    return jax.shard_map(
        body,
        mesh=mesh,
        in_specs=placed,
        out_specs=(P(None, "lat", "lon", None), P(None, "lat", "lon", None), P()),
        check_vma=False,
    )
```

```python
import functools

import jax
import jax.numpy as jnp
from jax import lax
from jax.experimental import pallas as pl
from jax.experimental.pallas import tpu as pltpu
from jax.sharding import PartitionSpec as P

F32 = jnp.float32
BF16 = jnp.bfloat16
VMEM = pl.BlockSpec(memory_space=pltpu.VMEM)
SMEM = pl.BlockSpec(memory_space=pltpu.SMEM)
HBM = pl.BlockSpec(memory_space=pltpu.HBM)
PACK = 20000000000
PREP = 10000000000
BULK = 2000000000
NT = (((1,), (1,)), ((), ()))


def call(kernel, outs, ins, out_specs, scratch=(), flops=0, size=0, limit=16):
    return pl.pallas_call(
        kernel,
        out_shape=outs,
        in_specs=ins,
        out_specs=out_specs,
        scratch_shapes=list(scratch),
        compiler_params=pltpu.CompilerParams(vmem_limit_bytes=limit * 2**20),
        cost_estimate=pl.CostEstimate(flops=flops, bytes_accessed=size, transcendentals=0),
    )


def like(shape, dtype=F32):
    return jax.ShapeDtypeStruct(shape, dtype)


def iota(shape, dim):
    return lax.broadcasted_iota(jnp.int32, shape, dim)


def pack_kernel(
    c_hbm, v_hbm, x_ref, first_ref, last_ref, left_ref, right_ref, c_ref, v_ref, sems
):
    copies = [
        pltpu.make_async_copy(c_hbm, c_ref, sems.at[0]),
        pltpu.make_async_copy(v_hbm, v_ref, sems.at[1]),
    ]
    for copy in copies:
        copy.start()
    for copy in copies:
        copy.wait()
    rows = x_ref.shape[0]
    tracers = c_ref.shape[0] // rows
    for r in range(rows):
        at = pl.ds(r, tracers, stride=rows)
        x = jnp.concatenate([c_ref[at, :], v_ref[at, :]], 0).astype(BF16)
        share_out(r, x, x_ref, first_ref, last_ref, left_ref, right_ref)


def prep_kernel(
    total_lon,
    pattern_ref,
    live_ref,
    inverse_ref,
    depth_ref,
    rate_ref,
    stoich_ref,
    basis_ref,
    c_ref,
    v_ref,
    index_ref,
    high_ref,
    low_ref,
    source_ref,
    rate_column_ref,
    gram_ref,
):
    lat, lon, slots = pattern_ref.shape
    rows = lat * lon
    columns, levels = inverse_ref.shape[2:4]
    points = columns * levels
    pattern = pattern_ref[...]
    itself = pattern[:, :, :1]
    far_lat = pattern // total_lon - itself // total_lon
    far_lon = pattern % total_lon - itself % total_lon
    shape = pattern.shape
    named = jnp.where(live_ref[...] > 0, (far_lat + 1) * 3 + far_lon + 1, -1)
    slot = iota(shape, 2)
    place = (iota(shape, 0) + slot // 3) * (lon + 2) + iota(shape, 1) + slot % 3
    held_at = jnp.zeros(shape, jnp.int32)
    found_at = jnp.zeros(shape, jnp.int32)
    for k in range(9):
        match = named == k
        held_at = jnp.where(
            slot == k, jnp.sum(jnp.where(match, slot, 0), 2, keepdims=True), held_at
        )
        found_at = jnp.where(
            slot == k, jnp.sum(jnp.where(match, 1, 0), 2, keepdims=True), found_at
        )
    index_ref[0] = held_at
    index_ref[1] = jnp.where(found_at > 0, place, (lat + 2) * (lon + 2))

    lane = iota((rows, points), 1)
    depth = jnp.concatenate([depth_ref[i] for i in range(lat)], 0)
    below = jnp.zeros((rows, points), jnp.int32)
    for k in range(columns):
        below = jnp.where(lane // levels == k, depth[:, k : k + 1], below)
    wet = (lane % levels < below).astype(F32)

    rate = jnp.concatenate([rate_ref[i] for i in range(lat)], 0)
    uptake, pull = sources(c_ref[:rows, :], v_ref[:rows, :], rate)
    spare = 8 - rows % 8 if rows % 8 else 0
    blank = [jnp.zeros((spare, points), F32)] if spare else []
    columns_of = [
        jnp.transpose(jnp.concatenate([part] + blank, 0)) for part in (uptake, pull, rate, wet)
    ]
    rate_column_ref[...] = columns_of[2]
    tracers = source_ref.shape[2] // 2
    share = stoich_ref[...]
    nothing = jnp.zeros((1, tracers), F32)
    share_c = jnp.concatenate([share, nothing], 1)
    share_v = jnp.concatenate([nothing, share], 1)
    for r in range(rows):
        at = slice(r, r + 1)
        source_ref[r] = columns_of[0][:, at] * share_c + columns_of[1][:, at] * share_v

    spread = (iota((levels, points), 1) % levels == iota((levels, points), 0)).astype(BF16)
    full = (points, points)
    same = iota(full, 0) // levels == iota(full, 1) // levels
    for r in range(rows):
        at = slice(r, r + 1)
        inverse = inverse_ref[r // lon, r % lon].reshape(points, levels)
        high = inverse.astype(BF16)
        low = (inverse - high.astype(F32)).astype(BF16)
        keep = jnp.where(same, wet[at, :] * columns_of[3][:, at], 0.0)
        for ref, part in ((high_ref, high), (low_ref, low)):
            tiled = jnp.dot(part, spread, preferred_element_type=F32)
            ref[r] = (tiled * keep).astype(BF16)

    gram_ref[...] = jnp.zeros(gram_ref.shape, F32)
    count = basis_ref.shape[0]
    row = 0
    for k in range(count):
        for j in range(k, count):
            gram_ref[row : row + 1, :] = jnp.sum(basis_ref[k] * basis_ref[j], 0, keepdims=True)
            row += 1


def sources(own_c, own_v, rate):
    denom = own_c * own_c + 1.0
    uptake = rate * own_c * own_c / denom
    slope = rate * 2.0 * own_c / (denom * denom)
    return uptake, slope * own_v


def corners_of(lat, lon):
    return {0: 0, lon - 1: 2, (lat - 1) * lon: 6, lat * lon - 1: 8}


def pull_kernel(lat, lon, state_ref, corner_ref, rate_column_ref, stoich_ref, source_ref):
    rows, _, tracers = source_ref.shape
    share = stoich_ref[...]
    corners = list(corners_of(lat, lon))
    for r in range(rows):
        ref, at = (corner_ref, corners.index(r)) if r in corners else (state_ref, r)
        own_c = ref[at, :, 0:1]
        own_v = ref[at, :, tracers : tracers + 1]
        source_ref[r] = sources(own_c, own_v, rate_column_ref[:, r : r + 1])[1] * share


def fill(pad_ref, x_ref, north_ref, south_ref, west_ref, east_ref, lat, lon):
    wide = lon + 2
    for j in range(lon):
        pad_ref[1 + j] = north_ref[j]
        pad_ref[(lat + 1) * wide + 1 + j] = south_ref[j]
        for i in range(lat):
            pad_ref[(i + 1) * wide + 1 + j] = x_ref[i * lon + j]
    for i in range(lat):
        pad_ref[(i + 1) * wide] = west_ref[i]
        pad_ref[(i + 1) * wide + lon + 1] = east_ref[i]
    pad_ref[(lat + 2) * wide] = jnp.zeros(pad_ref.shape[1:], BF16)


def transport(r, index_ref, pad_ref, held_ref, z, neighbours):
    lon, slots = index_ref.shape[2:]
    for k in neighbours:
        block = held_ref[r * slots + index_ref[0, r // lon, r % lon, k]]
        x = pad_ref[index_ref[1, r // lon, r % lon, k]]
        z = z + lax.dot_general(block, x, NT, preferred_element_type=F32)
    return z


def mix(z, high, low):
    z_high = z.astype(BF16)
    z_low = (z - z_high.astype(F32)).astype(BF16)
    dot = functools.partial(jnp.dot, preferred_element_type=F32)
    return dot(high, z_high) + (dot(low, z_high) + dot(high, z_low))


def bulk(lat, lon, index_ref, pad_ref, held_ref, high_ref, low_ref, source_ref, state_ref):
    corners = corners_of(lat, lon)
    for r in range(lat * lon):
        neighbours = [k for k in range(9) if k != corners.get(r)]
        state_ref[r] = transport(r, index_ref, pad_ref, held_ref, source_ref[r], neighbours)
    for r in range(lat * lon):
        if r not in corners:
            state_ref[r] = mix(state_ref[r], high_ref[r], low_ref[r])


def finish(
    lat, lon, index_ref, north_ref, south_ref, state_ref, held_ref, high_ref, low_ref, pad_ref, out_ref
):
    wide = lon + 2
    pad_ref[0] = north_ref[0]
    pad_ref[lon + 1] = north_ref[1]
    pad_ref[(lat + 1) * wide] = south_ref[0]
    pad_ref[(lat + 1) * wide + lon + 1] = south_ref[1]
    pad_ref[(lat + 2) * wide] = jnp.zeros(pad_ref.shape[1:], BF16)
    corners = corners_of(lat, lon)
    for n, (r, k) in enumerate(corners.items()):
        out_ref[n] = transport(r, index_ref, pad_ref, held_ref, state_ref[r], [k])
    for n, r in enumerate(corners):
        out_ref[n] = mix(out_ref[n], high_ref[r], low_ref[r])


def first_kernel(
    lat,
    lon,
    index_ref,
    x_ref,
    north_ref,
    south_ref,
    west_ref,
    east_ref,
    held_ref,
    high_ref,
    low_ref,
    source_ref,
    y_ref,
    state_ref,
    pad_ref,
):
    fill(pad_ref, x_ref, north_ref, south_ref, west_ref, east_ref, lat, lon)
    bulk(lat, lon, index_ref, pad_ref, held_ref, high_ref, low_ref, source_ref, state_ref)
    tracers = y_ref.shape[1]
    for r in range(lat * lon):
        if r in corners_of(lat, lon):
            y_ref[r] = jnp.zeros(y_ref.shape[1:], BF16)
        else:
            y_ref[r] = jnp.transpose(state_ref[r])[tracers:].astype(BF16)


def first_end_kernel(
    lat,
    lon,
    index_ref,
    north_ref,
    south_ref,
    state_ref,
    held_ref,
    high_ref,
    low_ref,
    part_ref,
    y_ref,
    first_ref,
    last_ref,
    left_ref,
    right_ref,
    corner_ref,
    pad_ref,
):
    finish(
        lat, lon, index_ref, north_ref, south_ref, state_ref, held_ref, high_ref, low_ref, pad_ref, corner_ref
    )
    corners = list(corners_of(lat, lon))
    tracers = y_ref.shape[1]
    for r in range(lat * lon):
        if r in corners:
            y = jnp.transpose(corner_ref[corners.index(r)])[tracers:].astype(BF16)
        else:
            y = part_ref[r]
        share_out(r, y, y_ref, first_ref, last_ref, left_ref, right_ref)


def share_out(r, x, x_ref, first_ref, last_ref, left_ref, right_ref):
    rows, lon = x_ref.shape[0], first_ref.shape[0]
    x_ref[r] = x
    if r < lon:
        first_ref[r] = x
    if r >= rows - lon:
        last_ref[r - (rows - lon)] = x
    if r % lon == 0:
        left_ref[r // lon] = x
    if r % lon == lon - 1:
        right_ref[r // lon] = x


def second_kernel(
    lat,
    lon,
    index_ref,
    x_ref,
    north_ref,
    south_ref,
    west_ref,
    east_ref,
    held_ref,
    high_ref,
    low_ref,
    source_ref,
    part_ref,
    state_ref,
    pad_ref,
):
    rows = lat * lon
    fill(pad_ref, x_ref, north_ref, south_ref, west_ref, east_ref, lat, lon)
    bulk(lat, lon, index_ref, pad_ref, held_ref, high_ref, low_ref, source_ref, state_ref)
    tracers = x_ref.shape[1]
    for r in range(rows):
        at = pl.ds(r, tracers, stride=rows)
        if r in corners_of(lat, lon):
            part_ref[at, :] = jnp.zeros((tracers, part_ref.shape[1]), F32)
        else:
            part_ref[at, :] = jnp.transpose(state_ref[r])


def second_end_kernel(
    lat,
    lon,
    index_ref,
    north_ref,
    south_ref,
    state_ref,
    held_ref,
    high_ref,
    low_ref,
    part_ref,
    gram_ref,
    basis_ref,
    product_ref,
    sums_ref,
    pad_ref,
    corner_ref,
):
    finish(
        lat, lon, index_ref, north_ref, south_ref, state_ref, held_ref, high_ref, low_ref, pad_ref, corner_ref
    )
    rows = lat * lon
    product_ref[...] = part_ref[...]
    tracers = product_ref.shape[0] // rows
    for n, r in enumerate(corners_of(lat, lon)):
        product_ref[pl.ds(r, tracers, stride=rows), :] = jnp.transpose(corner_ref[n])
    product = product_ref[...]
    count = basis_ref.shape[0]
    pairs = count * (count + 1) // 2
    all_sums = gram_ref[...]
    spot = iota(all_sums.shape, 0)
    for k in range(count + 1):
        other = basis_ref[k] if k < count else product
        part = jnp.sum(product * other, 0, keepdims=True)
        all_sums = jnp.where(spot == pairs + k, part, all_sums)
    column = jnp.sum(all_sums, 1, keepdims=True)
    row = jnp.sum(jnp.where(spot == iota(spot.shape, 1), column, 0.0), 0, keepdims=True)
    sums_ref[...] = jnp.broadcast_to(row, sums_ref.shape)


def last_kernel(
    parts_ref, product_ref, basis_ref, next_ref, out_hbm, coeffs_ref, flag_ref, sem
):
    copy = pltpu.make_async_copy(product_ref, out_hbm, sem)
    copy.start()
    count = basis_ref.shape[0]
    row = jnp.sum(parts_ref[...], 0, keepdims=True)
    lane = iota(row.shape, 1)

    def pick(at):
        return jnp.sum(jnp.where(lane == at, row, 0.0), 1, keepdims=True)

    pairs = count * (count + 1) // 2
    heights = [pick(pairs + k) for k in range(count)]
    whole = pick(pairs + count)
    cross = jnp.zeros((1, 1), F32)
    at = 0
    for k in range(count):
        for j in range(k, count):
            twice = 1.0 if k == j else 2.0
            cross = cross + twice * (heights[k] * heights[j] * pick(at))
            at += 1
    squares = sum(h * h for h in heights)
    short = whole - 2.0 * squares + cross
    size = whole + 2.0 * squares + cross
    beta = jnp.sqrt(jnp.maximum(short, 0.0) + 1e-06)
    rest = product_ref[...]
    for k in range(count):
        rest = rest - heights[k] * basis_ref[k]
    next_ref[...] = rest / beta
    for k in range(count):
        coeffs_ref[k] = heights[k][0, 0]
    coeffs_ref[count] = beta[0, 0]
    flag_ref[0] = jnp.where(short < 0.01 * size, 1, 0)[0, 0]
    copy.wait()


def summed(rows):
    row = jnp.sum(lax.all_to_all(rows, "lon", 0, 0), 0, keepdims=True)
    rows = jnp.broadcast_to(row, (lax.axis_size("lat"), row.shape[1]))
    return lax.all_to_all(rows, "lat", 0, 0)


def moved(a, axis, step):
    size = lax.axis_size(axis)
    return lax.ppermute(a, axis, [(i, (i + step) % size) for i in range(size)])


def halo(first, last, left, right, beside):
    west = moved(right, "lon", 1)
    east = moved(left, "lon", -1)
    north = moved(last, "lat", 1)
    south = moved(first, "lat", -1)
    west, east, beside = lax.optimization_barrier((west, east, beside))
    above = moved(jnp.stack([west[-1], east[-1]]), "lat", 1)
    below = moved(jnp.stack([west[0], east[0]]), "lat", -1)
    return (north, south, west, east), (above, below), beside


def body(
    base_state,
    tangent,
    blocks,
    pattern,
    live,
    column_inverse,
    col_depth,
    uptake_rate,
    stoich,
    basis,
):
    tracers, lat, lon, points = base_state.shape
    slots = pattern.shape[2]
    count = basis.shape[0]
    rows = lat * lon
    total_lon = lon * lax.axis_size("lon")
    size = tracers * rows
    places = (lat + 2) * (lon + 2) + 1
    share = stoich.reshape(1, tracers)

    flat_c = base_state.reshape(size, points)
    flat_v = tangent.reshape(size, points)
    def edges(width):
        return (
            like((rows, width, points), BF16),
            like((lon, width, points), BF16),
            like((lon, width, points), BF16),
            like((lat, width, points), BF16),
            like((lat, width, points), BF16),
        )

    x, *outer = call(
        pack_kernel,
        edges(2 * tracers),
        [HBM] * 2,
        [VMEM] * 5,
        scratch=[pltpu.VMEM((size, points), F32)] * 2 + [pltpu.SemaphoreType.DMA((2,))],
        size=400000,
        flops=PACK,
        limit=59,
    )(flat_c, flat_v)

    flat_basis = basis.reshape(count, size, points)
    held = blocks.reshape(rows * slots, points, points)
    index, high, low, source, rate_column, gram = call(
        functools.partial(prep_kernel, total_lon),
        (
            like((2, lat, lon, slots), jnp.int32),
            like((rows, points, points), BF16),
            like((rows, points, points), BF16),
            like((rows, points, 2 * tracers)),
            like((points, (rows + 7) // 8 * 8)),
            like((16, points)),
        ),
        [VMEM] * 9,
        [VMEM] * 6,
        flops=PREP,
        size=8000000,
    )(
        pattern,
        live,
        column_inverse,
        col_depth,
        uptake_rate,
        share,
        flat_basis,
        flat_c,
        flat_v,
    )

    work = 2 * 2 * tracers * rows * slots * points * points
    ends = len(corners_of(lat, lon))

    near, far, source = halo(*outer, source)
    part, state = call(
        functools.partial(first_kernel, lat, lon),
        (like((rows, tracers, points), BF16), like((rows, points, 2 * tracers))),
        [SMEM] + [VMEM] * 9,
        [VMEM] * 2,
        scratch=[pltpu.VMEM((places, 2 * tracers, points), BF16)],
        flops=BULK,
        size=5000000,
    )(index, x, *near, held, high, low, source)
    x, *outer, corner = call(
        functools.partial(first_end_kernel, lat, lon),
        edges(tracers) + (like((ends, points, 2 * tracers)),),
        [SMEM] + [VMEM] * 7,
        [VMEM] * 6,
        scratch=[pltpu.VMEM((places, 2 * tracers, points), BF16)],
        flops=work // 20,
        size=500000,
    )(index, *far, state, held, high, low, part)

    source = call(
        functools.partial(pull_kernel, lat, lon),
        like((rows, points, tracers)),
        [VMEM] * 4,
        VMEM,
        flops=100000,
        size=2000000,
    )(state, corner, rate_column, share)

    near, far, source = halo(*outer, source)
    part, state = call(
        functools.partial(second_kernel, lat, lon),
        (like((size, points)), like((rows, points, tracers))),
        [SMEM] + [VMEM] * 9,
        [VMEM] * 2,
        scratch=[pltpu.VMEM((places, tracers, points), BF16)],
        flops=BULK,
        size=5000000,
    )(index, x, *near, held, high, low, source)
    product, sums = call(
        functools.partial(second_end_kernel, lat, lon),
        (like((size, points)), like((lax.axis_size("lon"), points))),
        [SMEM] + [VMEM] * 9,
        [VMEM] * 2,
        scratch=[
            pltpu.VMEM((places, tracers, points), BF16),
            pltpu.VMEM((ends, points, tracers), F32),
        ],
        flops=work // 20,
        size=1500000,
    )(index, *far, state, held, high, low, part, gram, flat_basis)

    parts = summed(sums)
    following, written, coeffs, flag = call(
        last_kernel,
        (like((size, points)), like((size, points)), like((count + 1,)), like((1,), jnp.int32)),
        [VMEM] * 3,
        [VMEM, HBM, SMEM, SMEM],
        scratch=[pltpu.SemaphoreType.DMA],
        size=700000,
    )(parts, product, flat_basis)

    def again(carry):
        following, coeffs, flag = carry
        rest = product - jnp.einsum(
            "k,ksp->sp", coeffs[:count], flat_basis, precision=lax.Precision.HIGHEST
        )
        part = jnp.pad(jnp.sum(rest * rest).reshape(1, 1), ((0, 0), (0, points - 1)))
        squared = jnp.sum(summed(jnp.broadcast_to(part, (lax.axis_size("lon"), points))), 0)[0]
        beta = jnp.sqrt(squared + 1e-06)
        return rest / beta, jnp.concatenate([coeffs[:count], beta[None]]), flag * 0

    following, coeffs, flag = lax.while_loop(
        lambda carry: carry[2][0] > 0, again, (following, coeffs, flag)
    )
    shape = base_state.shape
    return written.reshape(shape), following.reshape(shape), coeffs


def solution(mesh):
    placed = (
        P(None, "lat", "lon", None),
        P(None, "lat", "lon", None),
        P("lat", "lon", None, None, None),
        P("lat", "lon", None),
        P("lat", "lon", None),
        P("lat", "lon", None, None, None),
        P("lat", "lon", None),
        P("lat", "lon", None),
        P(),
        P(None, None, "lat", "lon", None),
    )
    return jax.shard_map(
        body,
        mesh=mesh,
        in_specs=placed,
        out_specs=(P(None, "lat", "lon", None), P(None, "lat", "lon", None), P()),
        check_vma=False,
    )
```

```python
import functools

import jax
import jax.numpy as jnp
from jax import lax
from jax.experimental import pallas as pl
from jax.experimental.pallas import tpu as pltpu
from jax.sharding import PartitionSpec as P

F32 = jnp.float32
BF16 = jnp.bfloat16
VMEM = pl.BlockSpec(memory_space=pltpu.VMEM)
SMEM = pl.BlockSpec(memory_space=pltpu.SMEM)
HBM = pl.BlockSpec(memory_space=pltpu.HBM)
PACK = 20000000000
PREP = 10000000000
BULK = 2000000000
NT = (((1,), (1,)), ((), ()))


def call(kernel, outs, ins, out_specs, scratch=(), flops=0, size=0, limit=16):
    return pl.pallas_call(
        kernel,
        out_shape=outs,
        in_specs=ins,
        out_specs=out_specs,
        scratch_shapes=list(scratch),
        compiler_params=pltpu.CompilerParams(vmem_limit_bytes=limit * 2**20),
        cost_estimate=pl.CostEstimate(flops=flops, bytes_accessed=size, transcendentals=0),
    )


def like(shape, dtype=F32):
    return jax.ShapeDtypeStruct(shape, dtype)


def iota(shape, dim):
    return lax.broadcasted_iota(jnp.int32, shape, dim)


def pack_kernel(
    c_hbm, v_hbm, x_ref, first_ref, last_ref, left_ref, right_ref, c_ref, v_ref, sems
):
    copies = [
        pltpu.make_async_copy(c_hbm, c_ref, sems.at[0]),
        pltpu.make_async_copy(v_hbm, v_ref, sems.at[1]),
    ]
    for copy in copies:
        copy.start()
    for copy in copies:
        copy.wait()
    rows = x_ref.shape[0]
    tracers = c_ref.shape[0] // rows
    for r in range(rows):
        at = pl.ds(r, tracers, stride=rows)
        x = jnp.concatenate([c_ref[at, :], v_ref[at, :]], 0).astype(BF16)
        share_out(r, x, x_ref, first_ref, last_ref, left_ref, right_ref)


def prep_kernel(
    total_lon,
    pattern_ref,
    live_ref,
    inverse_ref,
    depth_ref,
    rate_ref,
    stoich_ref,
    basis_ref,
    c_ref,
    v_ref,
    index_ref,
    high_ref,
    low_ref,
    source_ref,
    rate_column_ref,
    gram_ref,
):
    lat, lon, slots = pattern_ref.shape
    rows = lat * lon
    columns, levels = inverse_ref.shape[2:4]
    points = columns * levels
    pattern = pattern_ref[...]
    itself = pattern[:, :, :1]
    far_lat = pattern // total_lon - itself // total_lon
    far_lon = pattern % total_lon - itself % total_lon
    shape = pattern.shape
    named = jnp.where(live_ref[...] > 0, (far_lat + 1) * 3 + far_lon + 1, -1)
    slot = iota(shape, 2)
    place = (iota(shape, 0) + slot // 3) * (lon + 2) + iota(shape, 1) + slot % 3
    held_at = jnp.zeros(shape, jnp.int32)
    found_at = jnp.zeros(shape, jnp.int32)
    for k in range(9):
        match = named == k
        held_at = jnp.where(
            slot == k, jnp.sum(jnp.where(match, slot, 0), 2, keepdims=True), held_at
        )
        found_at = jnp.where(
            slot == k, jnp.sum(jnp.where(match, 1, 0), 2, keepdims=True), found_at
        )
    index_ref[0] = held_at
    index_ref[1] = jnp.where(found_at > 0, place, (lat + 2) * (lon + 2))

    lane = iota((rows, points), 1)
    depth = jnp.concatenate([depth_ref[i] for i in range(lat)], 0)
    below = jnp.zeros((rows, points), jnp.int32)
    for k in range(columns):
        below = jnp.where(lane // levels == k, depth[:, k : k + 1], below)
    wet = (lane % levels < below).astype(F32)

    rate = jnp.concatenate([rate_ref[i] for i in range(lat)], 0)
    uptake, pull = sources(c_ref[:rows, :], v_ref[:rows, :], rate)
    spare = 8 - rows % 8 if rows % 8 else 0
    blank = [jnp.zeros((spare, points), F32)] if spare else []
    columns_of = [
        jnp.transpose(jnp.concatenate([part] + blank, 0)) for part in (uptake, pull, rate, wet)
    ]
    rate_column_ref[...] = columns_of[2]
    tracers = source_ref.shape[2] // 2
    share = stoich_ref[...]
    nothing = jnp.zeros((1, tracers), F32)
    share_c = jnp.concatenate([share, nothing], 1)
    share_v = jnp.concatenate([nothing, share], 1)
    for r in range(rows):
        at = slice(r, r + 1)
        source_ref[r] = columns_of[0][:, at] * share_c + columns_of[1][:, at] * share_v

    spread = (iota((levels, points), 1) % levels == iota((levels, points), 0)).astype(BF16)
    full = (points, points)
    same = iota(full, 0) // levels == iota(full, 1) // levels
    for r in range(rows):
        at = slice(r, r + 1)
        inverse = inverse_ref[r // lon, r % lon].reshape(points, levels)
        high = inverse.astype(BF16)
        low = (inverse - high.astype(F32)).astype(BF16)
        keep = jnp.where(same, wet[at, :] * columns_of[3][:, at], 0.0)
        for ref, part in ((high_ref, high), (low_ref, low)):
            tiled = jnp.dot(part, spread, preferred_element_type=F32)
            ref[r] = (tiled * keep).astype(BF16)

    gram_ref[...] = jnp.zeros(gram_ref.shape, F32)
    count = basis_ref.shape[0]
    row = 0
    for k in range(count):
        for j in range(k, count):
            gram_ref[row : row + 1, :] = jnp.sum(basis_ref[k] * basis_ref[j], 0, keepdims=True)
            row += 1


def sources(own_c, own_v, rate):
    denom = own_c * own_c + 1.0
    uptake = rate * own_c * own_c / denom
    slope = rate * 2.0 * own_c / (denom * denom)
    return uptake, slope * own_v


def beyond(lat, lon):
    found = {}
    for r in range(lat * lon):
        ends = [k for k in range(9) if not 0 <= r % lon + k % 3 - 1 < lon]
        if ends:
            found[r] = ends
    return found


def pull_kernel(lat, lon, state_ref, edge_ref, rate_column_ref, stoich_ref, source_ref):
    rows, _, tracers = source_ref.shape
    share = stoich_ref[...]
    edges = list(beyond(lat, lon))
    for r in range(rows):
        ref, at = (edge_ref, edges.index(r)) if r in edges else (state_ref, r)
        own_c = ref[at, :, 0:1]
        own_v = ref[at, :, tracers : tracers + 1]
        source_ref[r] = sources(own_c, own_v, rate_column_ref[:, r : r + 1])[1] * share


def fill(pad_ref, x_ref, north_ref, south_ref, lat, lon):
    wide = lon + 2
    for j in range(lon):
        pad_ref[1 + j] = north_ref[j]
        pad_ref[(lat + 1) * wide + 1 + j] = south_ref[j]
        for i in range(lat):
            pad_ref[(i + 1) * wide + 1 + j] = x_ref[i * lon + j]
    pad_ref[(lat + 2) * wide] = jnp.zeros(pad_ref.shape[1:], BF16)


def transport(r, index_ref, pad_ref, held_ref, z, neighbours):
    lon, slots = index_ref.shape[2:]
    for k in neighbours:
        block = held_ref[r * slots + index_ref[0, r // lon, r % lon, k]]
        x = pad_ref[index_ref[1, r // lon, r % lon, k]]
        z = z + lax.dot_general(block, x, NT, preferred_element_type=F32)
    return z


def mix(z, high, low):
    z_high = z.astype(BF16)
    z_low = (z - z_high.astype(F32)).astype(BF16)
    dot = functools.partial(jnp.dot, preferred_element_type=F32)
    return dot(high, z_high) + (dot(low, z_high) + dot(high, z_low))


def bulk(lat, lon, index_ref, pad_ref, held_ref, high_ref, low_ref, source_ref, state_ref):
    edges = beyond(lat, lon)
    for r in range(lat * lon):
        neighbours = [k for k in range(9) if k not in edges.get(r, ())]
        state_ref[r] = transport(r, index_ref, pad_ref, held_ref, source_ref[r], neighbours)
    for r in range(lat * lon):
        if r not in edges:
            state_ref[r] = mix(state_ref[r], high_ref[r], low_ref[r])


def finish(
    lat, lon, index_ref, west_ref, east_ref, state_ref, held_ref, high_ref, low_ref, pad_ref, out_ref
):
    wide = lon + 2
    for i in range(lat + 2):
        pad_ref[i * wide] = west_ref[i]
        pad_ref[i * wide + lon + 1] = east_ref[i]
    pad_ref[(lat + 2) * wide] = jnp.zeros(pad_ref.shape[1:], BF16)
    edges = beyond(lat, lon)
    for n, (r, neighbours) in enumerate(edges.items()):
        out_ref[n] = transport(r, index_ref, pad_ref, held_ref, state_ref[r], neighbours)
    for n, r in enumerate(edges):
        out_ref[n] = mix(out_ref[n], high_ref[r], low_ref[r])


def first_kernel(
    lat,
    lon,
    index_ref,
    x_ref,
    north_ref,
    south_ref,
    held_ref,
    high_ref,
    low_ref,
    source_ref,
    y_ref,
    state_ref,
    pad_ref,
):
    fill(pad_ref, x_ref, north_ref, south_ref, lat, lon)
    bulk(lat, lon, index_ref, pad_ref, held_ref, high_ref, low_ref, source_ref, state_ref)
    tracers = y_ref.shape[1]
    for r in range(lat * lon):
        if r in beyond(lat, lon):
            y_ref[r] = jnp.zeros(y_ref.shape[1:], BF16)
        else:
            y_ref[r] = jnp.transpose(state_ref[r])[tracers:].astype(BF16)


def first_end_kernel(
    lat,
    lon,
    index_ref,
    west_ref,
    east_ref,
    state_ref,
    held_ref,
    high_ref,
    low_ref,
    part_ref,
    y_ref,
    first_ref,
    last_ref,
    left_ref,
    right_ref,
    edge_ref,
    pad_ref,
):
    finish(
        lat, lon, index_ref, west_ref, east_ref, state_ref, held_ref, high_ref, low_ref, pad_ref, edge_ref
    )
    edges = list(beyond(lat, lon))
    tracers = y_ref.shape[1]
    for r in range(lat * lon):
        if r in edges:
            y = jnp.transpose(edge_ref[edges.index(r)])[tracers:].astype(BF16)
        else:
            y = part_ref[r]
        share_out(r, y, y_ref, first_ref, last_ref, left_ref, right_ref)


def share_out(r, x, x_ref, first_ref, last_ref, left_ref, right_ref):
    rows, lon = x_ref.shape[0], first_ref.shape[0]
    x_ref[r] = x
    if r < lon:
        first_ref[r] = x
    if r >= rows - lon:
        last_ref[r - (rows - lon)] = x
    if r % lon == 0:
        left_ref[r // lon] = x
    if r % lon == lon - 1:
        right_ref[r // lon] = x


def second_kernel(
    lat,
    lon,
    index_ref,
    x_ref,
    north_ref,
    south_ref,
    held_ref,
    high_ref,
    low_ref,
    source_ref,
    part_ref,
    state_ref,
    pad_ref,
):
    rows = lat * lon
    fill(pad_ref, x_ref, north_ref, south_ref, lat, lon)
    bulk(lat, lon, index_ref, pad_ref, held_ref, high_ref, low_ref, source_ref, state_ref)
    tracers = x_ref.shape[1]
    for r in range(rows):
        at = pl.ds(r, tracers, stride=rows)
        if r in beyond(lat, lon):
            part_ref[at, :] = jnp.zeros((tracers, part_ref.shape[1]), F32)
        else:
            part_ref[at, :] = jnp.transpose(state_ref[r])


def second_end_kernel(
    lat,
    lon,
    index_ref,
    west_ref,
    east_ref,
    state_ref,
    held_ref,
    high_ref,
    low_ref,
    part_ref,
    gram_ref,
    basis_ref,
    product_ref,
    sums_ref,
    pad_ref,
    edge_ref,
):
    finish(
        lat, lon, index_ref, west_ref, east_ref, state_ref, held_ref, high_ref, low_ref, pad_ref, edge_ref
    )
    rows = lat * lon
    product_ref[...] = part_ref[...]
    tracers = product_ref.shape[0] // rows
    for n, r in enumerate(beyond(lat, lon)):
        product_ref[pl.ds(r, tracers, stride=rows), :] = jnp.transpose(edge_ref[n])
    product = product_ref[...]
    count = basis_ref.shape[0]
    pairs = count * (count + 1) // 2
    all_sums = gram_ref[...]
    spot = iota(all_sums.shape, 0)
    for k in range(count + 1):
        other = basis_ref[k] if k < count else product
        part = jnp.sum(product * other, 0, keepdims=True)
        all_sums = jnp.where(spot == pairs + k, part, all_sums)
    column = jnp.sum(all_sums, 1, keepdims=True)
    row = jnp.sum(jnp.where(spot == iota(spot.shape, 1), column, 0.0), 0, keepdims=True)
    sums_ref[...] = jnp.broadcast_to(row, sums_ref.shape)


def last_kernel(
    parts_ref, product_ref, basis_ref, next_ref, out_hbm, coeffs_ref, flag_ref, sem
):
    copy = pltpu.make_async_copy(product_ref, out_hbm, sem)
    copy.start()
    count = basis_ref.shape[0]
    row = jnp.sum(parts_ref[...], 0, keepdims=True)
    lane = iota(row.shape, 1)

    def pick(at):
        return jnp.sum(jnp.where(lane == at, row, 0.0), 1, keepdims=True)

    pairs = count * (count + 1) // 2
    heights = [pick(pairs + k) for k in range(count)]
    whole = pick(pairs + count)
    cross = jnp.zeros((1, 1), F32)
    at = 0
    for k in range(count):
        for j in range(k, count):
            twice = 1.0 if k == j else 2.0
            cross = cross + twice * (heights[k] * heights[j] * pick(at))
            at += 1
    squares = sum(h * h for h in heights)
    short = whole - 2.0 * squares + cross
    size = whole + 2.0 * squares + cross
    beta = jnp.sqrt(jnp.maximum(short, 0.0) + 1e-06)
    rest = product_ref[...]
    for k in range(count):
        rest = rest - heights[k] * basis_ref[k]
    next_ref[...] = rest / beta
    for k in range(count):
        coeffs_ref[k] = heights[k][0, 0]
    coeffs_ref[count] = beta[0, 0]
    flag_ref[0] = jnp.where(short < 0.01 * size, 1, 0)[0, 0]
    copy.wait()


def summed(rows):
    row = jnp.sum(lax.all_to_all(rows, "lon", 0, 0), 0, keepdims=True)
    rows = jnp.broadcast_to(row, (lax.axis_size("lat"), row.shape[1]))
    return lax.all_to_all(rows, "lat", 0, 0)


def moved(a, axis, step):
    size = lax.axis_size(axis)
    return lax.ppermute(a, axis, [(i, (i + step) % size) for i in range(size)])


def rows_around(first, last, beside):
    north = moved(last, "lat", 1)
    south = moved(first, "lat", -1)
    return lax.optimization_barrier((north, south, beside))


def columns_around(left, right, north, south):
    right = jnp.concatenate([north[-1:], right, south[-1:]], 0)
    left = jnp.concatenate([north[:1], left, south[:1]], 0)
    return moved(right, "lon", 1), moved(left, "lon", -1)


def body(
    base_state,
    tangent,
    blocks,
    pattern,
    live,
    column_inverse,
    col_depth,
    uptake_rate,
    stoich,
    basis,
):
    tracers, lat, lon, points = base_state.shape
    slots = pattern.shape[2]
    count = basis.shape[0]
    rows = lat * lon
    total_lon = lon * lax.axis_size("lon")
    size = tracers * rows
    places = (lat + 2) * (lon + 2) + 1
    share = stoich.reshape(1, tracers)

    flat_c = base_state.reshape(size, points)
    flat_v = tangent.reshape(size, points)
    def edges(width):
        return (
            like((rows, width, points), BF16),
            like((lon, width, points), BF16),
            like((lon, width, points), BF16),
            like((lat, width, points), BF16),
            like((lat, width, points), BF16),
        )

    x, first, last, left, right = call(
        pack_kernel,
        edges(2 * tracers),
        [HBM] * 2,
        [VMEM] * 5,
        scratch=[pltpu.VMEM((size, points), F32)] * 2 + [pltpu.SemaphoreType.DMA((2,))],
        size=400000,
        flops=PACK,
        limit=59,
    )(flat_c, flat_v)

    flat_basis = basis.reshape(count, size, points)
    held = blocks.reshape(rows * slots, points, points)
    index, high, low, source, rate_column, gram = call(
        functools.partial(prep_kernel, total_lon),
        (
            like((2, lat, lon, slots), jnp.int32),
            like((rows, points, points), BF16),
            like((rows, points, points), BF16),
            like((rows, points, 2 * tracers)),
            like((points, (rows + 7) // 8 * 8)),
            like((16, points)),
        ),
        [VMEM] * 9,
        [VMEM] * 6,
        flops=PREP,
        size=8000000,
    )(
        pattern,
        live,
        column_inverse,
        col_depth,
        uptake_rate,
        share,
        flat_basis,
        flat_c,
        flat_v,
    )

    work = 2 * 2 * tracers * rows * slots * points * points
    ends = len(beyond(lat, lon))

    prepared = (index, high, low, source, rate_column, gram)
    north, south, prepared = rows_around(first, last, prepared)
    index, high, low, source, rate_column, gram = prepared
    west, east = columns_around(left, right, north, south)
    part, state = call(
        functools.partial(first_kernel, lat, lon),
        (like((rows, tracers, points), BF16), like((rows, points, 2 * tracers))),
        [SMEM] + [VMEM] * 7,
        [VMEM] * 2,
        scratch=[pltpu.VMEM((places, 2 * tracers, points), BF16)],
        flops=BULK,
        size=5000000,
    )(index, x, north, south, held, high, low, source)
    x, first, last, left, right, edge = call(
        functools.partial(first_end_kernel, lat, lon),
        edges(tracers) + (like((ends, points, 2 * tracers)),),
        [SMEM] + [VMEM] * 7,
        [VMEM] * 6,
        scratch=[pltpu.VMEM((places, 2 * tracers, points), BF16)],
        flops=work // 20,
        size=500000,
    )(index, west, east, state, held, high, low, part)

    source = call(
        functools.partial(pull_kernel, lat, lon),
        like((rows, points, tracers)),
        [VMEM] * 4,
        VMEM,
        flops=100000,
        size=2000000,
    )(state, edge, rate_column, share)

    north, south, source = rows_around(first, last, source)
    west, east = columns_around(left, right, north, south)
    part, state = call(
        functools.partial(second_kernel, lat, lon),
        (like((size, points)), like((rows, points, tracers))),
        [SMEM] + [VMEM] * 7,
        [VMEM] * 2,
        scratch=[pltpu.VMEM((places, tracers, points), BF16)],
        flops=BULK,
        size=5000000,
    )(index, x, north, south, held, high, low, source)
    product, sums = call(
        functools.partial(second_end_kernel, lat, lon),
        (like((size, points)), like((lax.axis_size("lon"), points))),
        [SMEM] + [VMEM] * 9,
        [VMEM] * 2,
        scratch=[
            pltpu.VMEM((places, tracers, points), BF16),
            pltpu.VMEM((ends, points, tracers), F32),
        ],
        flops=work // 20,
        size=1500000,
    )(index, west, east, state, held, high, low, part, gram, flat_basis)

    parts = summed(sums)
    following, written, coeffs, flag = call(
        last_kernel,
        (like((size, points)), like((size, points)), like((count + 1,)), like((1,), jnp.int32)),
        [VMEM] * 3,
        [VMEM, HBM, SMEM, SMEM],
        scratch=[pltpu.SemaphoreType.DMA],
        size=700000,
    )(parts, product, flat_basis)

    def again(carry):
        following, coeffs, flag = carry
        rest = product - jnp.einsum(
            "k,ksp->sp", coeffs[:count], flat_basis, precision=lax.Precision.HIGHEST
        )
        part = jnp.pad(jnp.sum(rest * rest).reshape(1, 1), ((0, 0), (0, points - 1)))
        squared = jnp.sum(summed(jnp.broadcast_to(part, (lax.axis_size("lon"), points))), 0)[0]
        beta = jnp.sqrt(squared + 1e-06)
        return rest / beta, jnp.concatenate([coeffs[:count], beta[None]]), flag * 0

    following, coeffs, flag = lax.while_loop(
        lambda carry: carry[2][0] > 0, again, (following, coeffs, flag)
    )
    shape = base_state.shape
    return written.reshape(shape), following.reshape(shape), coeffs


def solution(mesh):
    placed = (
        P(None, "lat", "lon", None),
        P(None, "lat", "lon", None),
        P("lat", "lon", None, None, None),
        P("lat", "lon", None),
        P("lat", "lon", None),
        P("lat", "lon", None, None, None),
        P("lat", "lon", None),
        P("lat", "lon", None),
        P(),
        P(None, None, "lat", "lon", None),
    )
    return jax.shard_map(
        body,
        mesh=mesh,
        in_specs=placed,
        out_specs=(P(None, "lat", "lon", None), P(None, "lat", "lon", None), P()),
        check_vma=False,
    )
```

```python
import functools

import jax
import jax.numpy as jnp
from jax import lax
from jax.experimental import pallas as pl
from jax.experimental.pallas import tpu as pltpu
from jax.sharding import PartitionSpec as P

F32 = jnp.float32
BF16 = jnp.bfloat16
VMEM = pl.BlockSpec(memory_space=pltpu.VMEM)
SMEM = pl.BlockSpec(memory_space=pltpu.SMEM)
HBM = pl.BlockSpec(memory_space=pltpu.HBM)
PACK = 20000000000
PREP = 10000000000
BULK = 2000000000
NT = (((1,), (1,)), ((), ()))


def call(kernel, outs, ins, out_specs, scratch=(), flops=0, size=0, limit=16):
    return pl.pallas_call(
        kernel,
        out_shape=outs,
        in_specs=ins,
        out_specs=out_specs,
        scratch_shapes=list(scratch),
        compiler_params=pltpu.CompilerParams(vmem_limit_bytes=limit * 2**20),
        cost_estimate=pl.CostEstimate(flops=flops, bytes_accessed=size, transcendentals=0),
    )


def like(shape, dtype=F32):
    return jax.ShapeDtypeStruct(shape, dtype)


def iota(shape, dim):
    return lax.broadcasted_iota(jnp.int32, shape, dim)


def begin_kernel(out_ref):
    out_ref[...] = jnp.zeros(out_ref.shape, F32)


def pack_kernel(
    begun_ref, c_ref, v_ref, x_ref, first_ref, last_ref, left_ref, right_ref
):
    rows = x_ref.shape[0]
    tracers = c_ref.shape[0] // rows
    for r in range(rows):
        at = pl.ds(r, tracers, stride=rows)
        x = jnp.concatenate([c_ref[at, :], v_ref[at, :]], 0).astype(BF16)
        share_out(r, x, x_ref, first_ref, last_ref, left_ref, right_ref)


def prep_kernel(
    total_lon,
    pattern_ref,
    live_ref,
    inverse_ref,
    depth_ref,
    rate_ref,
    stoich_ref,
    basis_ref,
    c_ref,
    v_ref,
    index_ref,
    high_ref,
    low_ref,
    source_ref,
    rate_column_ref,
    gram_ref,
):
    lat, lon, slots = pattern_ref.shape
    rows = lat * lon
    columns, levels = inverse_ref.shape[2:4]
    points = columns * levels
    pattern = pattern_ref[...]
    itself = pattern[:, :, :1]
    far_lat = pattern // total_lon - itself // total_lon
    far_lon = pattern % total_lon - itself % total_lon
    shape = pattern.shape
    named = jnp.where(live_ref[...] > 0, (far_lat + 1) * 3 + far_lon + 1, -1)
    slot = iota(shape, 2)
    place = (iota(shape, 0) + slot // 3) * (lon + 2) + iota(shape, 1) + slot % 3
    held_at = jnp.zeros(shape, jnp.int32)
    found_at = jnp.zeros(shape, jnp.int32)
    for k in range(9):
        match = named == k
        held_at = jnp.where(
            slot == k, jnp.sum(jnp.where(match, slot, 0), 2, keepdims=True), held_at
        )
        found_at = jnp.where(
            slot == k, jnp.sum(jnp.where(match, 1, 0), 2, keepdims=True), found_at
        )
    index_ref[0] = held_at
    index_ref[1] = jnp.where(found_at > 0, place, (lat + 2) * (lon + 2))

    lane = iota((rows, points), 1)
    depth = jnp.concatenate([depth_ref[i] for i in range(lat)], 0)
    below = jnp.zeros((rows, points), jnp.int32)
    for k in range(columns):
        below = jnp.where(lane // levels == k, depth[:, k : k + 1], below)
    wet = (lane % levels < below).astype(F32)

    rate = jnp.concatenate([rate_ref[i] for i in range(lat)], 0)
    uptake, pull = sources(c_ref[:rows, :], v_ref[:rows, :], rate)
    spare = 8 - rows % 8 if rows % 8 else 0
    blank = [jnp.zeros((spare, points), F32)] if spare else []
    columns_of = [
        jnp.transpose(jnp.concatenate([part] + blank, 0)) for part in (uptake, pull, rate, wet)
    ]
    rate_column_ref[...] = columns_of[2]
    tracers = source_ref.shape[2] // 2
    share = stoich_ref[...]
    nothing = jnp.zeros((1, tracers), F32)
    share_c = jnp.concatenate([share, nothing], 1)
    share_v = jnp.concatenate([nothing, share], 1)
    for r in range(rows):
        at = slice(r, r + 1)
        source_ref[r] = columns_of[0][:, at] * share_c + columns_of[1][:, at] * share_v

    spread = (iota((levels, points), 1) % levels == iota((levels, points), 0)).astype(BF16)
    full = (points, points)
    same = iota(full, 0) // levels == iota(full, 1) // levels
    for r in range(rows):
        at = slice(r, r + 1)
        inverse = inverse_ref[r // lon, r % lon].reshape(points, levels)
        high = inverse.astype(BF16)
        low = (inverse - high.astype(F32)).astype(BF16)
        keep = jnp.where(same, wet[at, :] * columns_of[3][:, at], 0.0)
        for ref, part in ((high_ref, high), (low_ref, low)):
            tiled = jnp.dot(part, spread, preferred_element_type=F32)
            ref[r] = (tiled * keep).astype(BF16)

    gram_ref[...] = jnp.zeros(gram_ref.shape, F32)
    count = basis_ref.shape[0]
    row = 0
    for k in range(count):
        for j in range(k, count):
            gram_ref[row : row + 1, :] = jnp.sum(basis_ref[k] * basis_ref[j], 0, keepdims=True)
            row += 1


def sources(own_c, own_v, rate):
    denom = own_c * own_c + 1.0
    uptake = rate * own_c * own_c / denom
    slope = rate * 2.0 * own_c / (denom * denom)
    return uptake, slope * own_v


def beyond(lat, lon):
    found = {}
    for r in range(lat * lon):
        ends = [k for k in range(9) if not 0 <= r % lon + k % 3 - 1 < lon]
        if ends:
            found[r] = ends
    return found


def pull_kernel(lat, lon, state_ref, edge_ref, rate_column_ref, stoich_ref, source_ref):
    rows, _, tracers = source_ref.shape
    share = stoich_ref[...]
    edges = list(beyond(lat, lon))
    for r in range(rows):
        ref, at = (edge_ref, edges.index(r)) if r in edges else (state_ref, r)
        own_c = ref[at, :, 0:1]
        own_v = ref[at, :, tracers : tracers + 1]
        source_ref[r] = sources(own_c, own_v, rate_column_ref[:, r : r + 1])[1] * share


def fill(pad_ref, x_ref, north_ref, south_ref, lat, lon):
    wide = lon + 2
    for j in range(lon):
        pad_ref[1 + j] = north_ref[j]
        pad_ref[(lat + 1) * wide + 1 + j] = south_ref[j]
        for i in range(lat):
            pad_ref[(i + 1) * wide + 1 + j] = x_ref[i * lon + j]
    pad_ref[(lat + 2) * wide] = jnp.zeros(pad_ref.shape[1:], BF16)


def transport(r, index_ref, pad_ref, held_ref, z, neighbours):
    lon, slots = index_ref.shape[2:]
    for k in neighbours:
        block = held_ref[r * slots + index_ref[0, r // lon, r % lon, k]]
        x = pad_ref[index_ref[1, r // lon, r % lon, k]]
        z = z + lax.dot_general(block, x, NT, preferred_element_type=F32)
    return z


def mix(z, high, low):
    z_high = z.astype(BF16)
    z_low = (z - z_high.astype(F32)).astype(BF16)
    dot = functools.partial(jnp.dot, preferred_element_type=F32)
    return dot(high, z_high) + (dot(low, z_high) + dot(high, z_low))


def bulk(
    lat, lon, index_ref, pad_ref, held_ref, high_ref, low_ref, source_ref, state_ref, later_ref
):
    edges = beyond(lat, lon)
    slots = index_ref.shape[3]
    n = 0
    for r, neighbours in edges.items():
        for k in neighbours:
            at = (r // lon, r % lon, k)
            block = held_ref[r * slots + index_ref[0, *at]]
            named = index_ref[1, *at] < (lat + 2) * (lon + 2)
            later_ref[n] = jnp.where(named, block, jnp.zeros_like(block))
            n += 1
    for r in range(lat * lon):
        neighbours = [k for k in range(9) if k not in edges.get(r, ())]
        state_ref[r] = transport(r, index_ref, pad_ref, held_ref, source_ref[r], neighbours)
    for r in range(lat * lon):
        if r not in edges:
            state_ref[r] = mix(state_ref[r], high_ref[r], low_ref[r])


def finish(lat, lon, west_ref, east_ref, state_ref, later_ref, high_ref, low_ref, out_ref):
    edges = beyond(lat, lon)
    at = 0
    for n, (r, neighbours) in enumerate(edges.items()):
        z = state_ref[r]
        for k in neighbours:
            x = (west_ref if r % lon + k % 3 == 0 else east_ref)[r // lon + k // 3]
            z = z + lax.dot_general(later_ref[at], x, NT, preferred_element_type=F32)
            at += 1
        out_ref[n] = z
    for n, r in enumerate(edges):
        out_ref[n] = mix(out_ref[n], high_ref[r], low_ref[r])


def first_kernel(
    lat,
    lon,
    index_ref,
    x_ref,
    north_ref,
    south_ref,
    held_ref,
    high_ref,
    low_ref,
    source_ref,
    y_ref,
    state_ref,
    later_ref,
    pad_ref,
):
    fill(pad_ref, x_ref, north_ref, south_ref, lat, lon)
    bulk(
        lat, lon, index_ref, pad_ref, held_ref, high_ref, low_ref, source_ref, state_ref, later_ref
    )
    tracers = y_ref.shape[1]
    for r in range(lat * lon):
        if r in beyond(lat, lon):
            y_ref[r] = jnp.zeros(y_ref.shape[1:], BF16)
        else:
            y_ref[r] = jnp.transpose(state_ref[r])[tracers:].astype(BF16)


def first_end_kernel(
    lat,
    lon,
    west_ref,
    east_ref,
    state_ref,
    later_ref,
    high_ref,
    low_ref,
    part_ref,
    y_ref,
    first_ref,
    last_ref,
    left_ref,
    right_ref,
    edge_ref,
):
    finish(lat, lon, west_ref, east_ref, state_ref, later_ref, high_ref, low_ref, edge_ref)
    edges = list(beyond(lat, lon))
    tracers = y_ref.shape[1]
    for r in range(lat * lon):
        if r in edges:
            y = jnp.transpose(edge_ref[edges.index(r)])[tracers:].astype(BF16)
        else:
            y = part_ref[r]
        share_out(r, y, y_ref, first_ref, last_ref, left_ref, right_ref)


def share_out(r, x, x_ref, first_ref, last_ref, left_ref, right_ref):
    rows, lon = x_ref.shape[0], first_ref.shape[0]
    x_ref[r] = x
    if r < lon:
        first_ref[r] = x
    if r >= rows - lon:
        last_ref[r - (rows - lon)] = x
    if r % lon == 0:
        left_ref[r // lon] = x
    if r % lon == lon - 1:
        right_ref[r // lon] = x


def second_kernel(
    lat,
    lon,
    index_ref,
    x_ref,
    north_ref,
    south_ref,
    held_ref,
    high_ref,
    low_ref,
    source_ref,
    part_ref,
    state_ref,
    later_ref,
    pad_ref,
):
    rows = lat * lon
    fill(pad_ref, x_ref, north_ref, south_ref, lat, lon)
    bulk(
        lat, lon, index_ref, pad_ref, held_ref, high_ref, low_ref, source_ref, state_ref, later_ref
    )
    tracers = x_ref.shape[1]
    for r in range(rows):
        at = pl.ds(r, tracers, stride=rows)
        if r in beyond(lat, lon):
            part_ref[at, :] = jnp.zeros((tracers, part_ref.shape[1]), F32)
        else:
            part_ref[at, :] = jnp.transpose(state_ref[r])


def second_end_kernel(
    lat,
    lon,
    west_ref,
    east_ref,
    state_ref,
    later_ref,
    high_ref,
    low_ref,
    part_ref,
    gram_ref,
    basis_ref,
    product_ref,
    out_hbm,
    sums_ref,
    edge_ref,
    sem,
):
    finish(lat, lon, west_ref, east_ref, state_ref, later_ref, high_ref, low_ref, edge_ref)
    rows = lat * lon
    product_ref[...] = part_ref[...]
    tracers = product_ref.shape[0] // rows
    for n, r in enumerate(beyond(lat, lon)):
        product_ref[pl.ds(r, tracers, stride=rows), :] = jnp.transpose(edge_ref[n])
    copy = pltpu.make_async_copy(product_ref, out_hbm, sem)
    copy.start()
    product = product_ref[...]
    count = basis_ref.shape[0]
    pairs = count * (count + 1) // 2
    all_sums = gram_ref[...]
    spot = iota(all_sums.shape, 0)
    for k in range(count + 1):
        other = basis_ref[k] if k < count else product
        part = jnp.sum(product * other, 0, keepdims=True)
        all_sums = jnp.where(spot == pairs + k, part, all_sums)
    column = jnp.sum(all_sums, 1, keepdims=True)
    row = jnp.sum(jnp.where(spot == iota(spot.shape, 1), column, 0.0), 0, keepdims=True)
    sums_ref[...] = jnp.broadcast_to(row, sums_ref.shape)
    copy.wait()


def last_kernel(parts_ref, product_ref, basis_ref, next_ref, coeffs_ref, flag_ref):
    count = basis_ref.shape[0]
    row = jnp.sum(parts_ref[...], 0, keepdims=True)
    lane = iota(row.shape, 1)

    def pick(at):
        return jnp.sum(jnp.where(lane == at, row, 0.0), 1, keepdims=True)

    pairs = count * (count + 1) // 2
    heights = [pick(pairs + k) for k in range(count)]
    whole = pick(pairs + count)
    cross = jnp.zeros((1, 1), F32)
    at = 0
    for k in range(count):
        for j in range(k, count):
            twice = 1.0 if k == j else 2.0
            cross = cross + twice * (heights[k] * heights[j] * pick(at))
            at += 1
    squares = sum(h * h for h in heights)
    short = whole - 2.0 * squares + cross
    size = whole + 2.0 * squares + cross
    beta = jnp.sqrt(jnp.maximum(short, 0.0) + 1e-06)
    rest = product_ref[...]
    for k in range(count):
        rest = rest - heights[k] * basis_ref[k]
    next_ref[...] = rest / beta
    for k in range(count):
        coeffs_ref[k] = heights[k][0, 0]
    coeffs_ref[count] = beta[0, 0]
    flag_ref[0] = jnp.where(short < 0.01 * size, 1, 0)[0, 0]


def summed(rows):
    row = jnp.sum(lax.all_to_all(rows, "lon", 0, 0), 0, keepdims=True)
    rows = jnp.broadcast_to(row, (lax.axis_size("lat"), row.shape[1]))
    return lax.all_to_all(rows, "lat", 0, 0)


def moved(a, axis, step):
    size = lax.axis_size(axis)
    return lax.ppermute(a, axis, [(i, (i + step) % size) for i in range(size)])


def rows_around(first, last, beside):
    north = moved(last, "lat", 1)
    south = moved(first, "lat", -1)
    return lax.optimization_barrier((north, south, beside))


def columns_around(left, right, north, south):
    right = jnp.concatenate([north[-1:], right, south[-1:]], 0)
    left = jnp.concatenate([north[:1], left, south[:1]], 0)
    return moved(right, "lon", 1), moved(left, "lon", -1)


def body(
    base_state,
    tangent,
    blocks,
    pattern,
    live,
    column_inverse,
    col_depth,
    uptake_rate,
    stoich,
    basis,
):
    tracers, lat, lon, points = base_state.shape
    slots = pattern.shape[2]
    count = basis.shape[0]
    rows = lat * lon
    total_lon = lon * lax.axis_size("lon")
    size = tracers * rows
    places = (lat + 2) * (lon + 2) + 1
    share = stoich.reshape(1, tracers)

    flat_c = base_state.reshape(size, points)
    flat_v = tangent.reshape(size, points)
    def edges(width):
        return (
            like((rows, width, points), BF16),
            like((lon, width, points), BF16),
            like((lon, width, points), BF16),
            like((lat, width, points), BF16),
            like((lat, width, points), BF16),
        )

    begun = call(begin_kernel, like((8, points)), [], VMEM, flops=PACK)()
    x, first, last, left, right = call(
        pack_kernel, edges(2 * tracers), [VMEM] * 3, [VMEM] * 5, flops=PACK, size=400000
    )(begun, flat_c, flat_v)

    flat_basis = basis.reshape(count, size, points)
    held = blocks.reshape(rows * slots, points, points)
    index, high, low, source, rate_column, gram = call(
        functools.partial(prep_kernel, total_lon),
        (
            like((2, lat, lon, slots), jnp.int32),
            like((rows, points, points), BF16),
            like((rows, points, points), BF16),
            like((rows, points, 2 * tracers)),
            like((points, (rows + 7) // 8 * 8)),
            like((16, points)),
        ),
        [VMEM] * 9,
        [VMEM] * 6,
        flops=PREP,
        size=8000000,
    )(
        pattern,
        live,
        column_inverse,
        col_depth,
        uptake_rate,
        share,
        flat_basis,
        flat_c,
        flat_v,
    )

    work = 2 * 2 * tracers * rows * slots * points * points
    ends = len(beyond(lat, lon))
    later = like((sum(map(len, beyond(lat, lon).values())), points, points), BF16)

    prepared = (index, high, low, source, rate_column, gram)
    north, south, prepared = rows_around(first, last, prepared)
    index, high, low, source, rate_column, gram = prepared
    west, east = columns_around(left, right, north, south)
    part, state, blocks_later = call(
        functools.partial(first_kernel, lat, lon),
        (like((rows, tracers, points), BF16), like((rows, points, 2 * tracers)), later),
        [SMEM] + [VMEM] * 7,
        [VMEM] * 3,
        scratch=[pltpu.VMEM((places, 2 * tracers, points), BF16)],
        flops=BULK,
        size=5000000,
    )(index, x, north, south, held, high, low, source)
    x, first, last, left, right, edge = call(
        functools.partial(first_end_kernel, lat, lon),
        edges(tracers) + (like((ends, points, 2 * tracers)),),
        [VMEM] * 7,
        [VMEM] * 6,
        flops=work // 20,
        size=500000,
    )(west, east, state, blocks_later, high, low, part)

    source = call(
        functools.partial(pull_kernel, lat, lon),
        like((rows, points, tracers)),
        [VMEM] * 4,
        VMEM,
        flops=100000,
        size=2000000,
    )(state, edge, rate_column, share)

    north, south, source = rows_around(first, last, source)
    west, east = columns_around(left, right, north, south)
    part, state, blocks_later = call(
        functools.partial(second_kernel, lat, lon),
        (like((size, points)), like((rows, points, tracers)), later),
        [SMEM] + [VMEM] * 7,
        [VMEM] * 3,
        scratch=[pltpu.VMEM((places, tracers, points), BF16)],
        flops=BULK,
        size=5000000,
    )(index, x, north, south, held, high, low, source)
    product, written, sums = call(
        functools.partial(second_end_kernel, lat, lon),
        (like((size, points)), like((size, points)), like((lax.axis_size("lon"), points))),
        [VMEM] * 9,
        [VMEM, HBM, VMEM],
        scratch=[pltpu.VMEM((ends, points, tracers), F32), pltpu.SemaphoreType.DMA],
        flops=work // 20,
        size=1500000,
    )(west, east, state, blocks_later, high, low, part, gram, flat_basis)

    parts = summed(sums)
    following, coeffs, flag = call(
        last_kernel,
        (like((size, points)), like((count + 1,)), like((1,), jnp.int32)),
        [VMEM] * 3,
        [VMEM, SMEM, SMEM],
        size=700000,
    )(parts, product, flat_basis)

    def again(carry):
        pairs = count * (count + 1) // 2
        heights = jnp.sum(parts, 0)[pairs : pairs + count]
        rest = product - jnp.einsum(
            "k,ksp->sp", heights, flat_basis, precision=lax.Precision.HIGHEST
        )
        part = jnp.pad(jnp.sum(rest * rest).reshape(1, 1), ((0, 0), (0, points - 1)))
        squared = jnp.sum(summed(jnp.broadcast_to(part, (lax.axis_size("lon"), points))), 0)[0]
        beta = jnp.sqrt(squared + 1e-06)
        return rest / beta, jnp.concatenate([heights, beta[None]]), carry[2] * 0

    following, coeffs, flag = lax.while_loop(
        lambda carry: carry[2][0] > 0, again, (following, coeffs, flag)
    )
    shape = base_state.shape
    return written.reshape(shape), following.reshape(shape), coeffs


def solution(mesh):
    placed = (
        P(None, "lat", "lon", None),
        P(None, "lat", "lon", None),
        P("lat", "lon", None, None, None),
        P("lat", "lon", None),
        P("lat", "lon", None),
        P("lat", "lon", None, None, None),
        P("lat", "lon", None),
        P("lat", "lon", None),
        P(),
        P(None, None, "lat", "lon", None),
    )
    return jax.shard_map(
        body,
        mesh=mesh,
        in_specs=placed,
        out_specs=(P(None, "lat", "lon", None), P(None, "lat", "lon", None), P()),
        check_vma=False,
    )
```

```python
import functools

import jax
import jax.numpy as jnp
from jax import lax
from jax.experimental import pallas as pl
from jax.experimental.pallas import tpu as pltpu
from jax.sharding import PartitionSpec as P

F32 = jnp.float32
BF16 = jnp.bfloat16
VMEM = pl.BlockSpec(memory_space=pltpu.VMEM)
SMEM = pl.BlockSpec(memory_space=pltpu.SMEM)
HBM = pl.BlockSpec(memory_space=pltpu.HBM)
PACK = 20000000000
PREP = 10000000000
BULK = 2000000000
NT = (((1,), (1,)), ((), ()))


def call(kernel, outs, ins, out_specs, scratch=(), flops=0, size=0, limit=16):
    return pl.pallas_call(
        kernel,
        out_shape=outs,
        in_specs=ins,
        out_specs=out_specs,
        scratch_shapes=list(scratch),
        compiler_params=pltpu.CompilerParams(vmem_limit_bytes=limit * 2**20),
        cost_estimate=pl.CostEstimate(flops=flops, bytes_accessed=size, transcendentals=0),
    )


def like(shape, dtype=F32):
    return jax.ShapeDtypeStruct(shape, dtype)


def iota(shape, dim):
    return lax.broadcasted_iota(jnp.int32, shape, dim)


def begin_kernel(out_ref):
    out_ref[...] = jnp.zeros(out_ref.shape, F32)


def pack_kernel(
    begun_ref, c_ref, v_ref, x_ref, first_ref, last_ref, left_ref, right_ref
):
    rows = x_ref.shape[0]
    tracers = c_ref.shape[0] // rows
    for r in range(rows):
        at = pl.ds(r, tracers, stride=rows)
        x = jnp.concatenate([c_ref[at, :], v_ref[at, :]], 0).astype(BF16)
        share_out(r, x, x_ref, first_ref, last_ref, left_ref, right_ref)


def prep_kernel(
    total_lon,
    pattern_ref,
    live_ref,
    inverse_ref,
    depth_ref,
    rate_ref,
    stoich_ref,
    basis_ref,
    c_ref,
    v_ref,
    index_ref,
    high_ref,
    low_ref,
    source_ref,
    rate_column_ref,
    gram_ref,
):
    lat, lon, slots = pattern_ref.shape
    rows = lat * lon
    columns, levels = inverse_ref.shape[2:4]
    points = columns * levels
    pattern = pattern_ref[...]
    itself = pattern[:, :, :1]
    far_lat = pattern // total_lon - itself // total_lon
    far_lon = pattern % total_lon - itself % total_lon
    shape = pattern.shape
    named = jnp.where(live_ref[...] > 0, (far_lat + 1) * 3 + far_lon + 1, -1)
    slot = iota(shape, 2)
    place = (iota(shape, 0) + slot // 3) * (lon + 2) + iota(shape, 1) + slot % 3
    held_at = jnp.zeros(shape, jnp.int32)
    found_at = jnp.zeros(shape, jnp.int32)
    for k in range(9):
        match = named == k
        held_at = jnp.where(
            slot == k, jnp.sum(jnp.where(match, slot, 0), 2, keepdims=True), held_at
        )
        found_at = jnp.where(
            slot == k, jnp.sum(jnp.where(match, 1, 0), 2, keepdims=True), found_at
        )
    index_ref[0] = held_at
    index_ref[1] = jnp.where(found_at > 0, place, (lat + 2) * (lon + 2))

    lane = iota((rows, points), 1)
    depth = jnp.concatenate([depth_ref[i] for i in range(lat)], 0)
    below = jnp.zeros((rows, points), jnp.int32)
    for k in range(columns):
        below = jnp.where(lane // levels == k, depth[:, k : k + 1], below)
    wet = (lane % levels < below).astype(F32)

    rate = jnp.concatenate([rate_ref[i] for i in range(lat)], 0)
    uptake, pull = sources(c_ref[:rows, :], v_ref[:rows, :], rate)
    spare = 8 - rows % 8 if rows % 8 else 0
    blank = [jnp.zeros((spare, points), F32)] if spare else []
    columns_of = [
        jnp.transpose(jnp.concatenate([part] + blank, 0)) for part in (uptake, pull, rate, wet)
    ]
    rate_column_ref[...] = columns_of[2]
    tracers = source_ref.shape[2] // 2
    share = stoich_ref[...]
    nothing = jnp.zeros((1, tracers), F32)
    share_c = jnp.concatenate([share, nothing], 1)
    share_v = jnp.concatenate([nothing, share], 1)
    for r in range(rows):
        at = slice(r, r + 1)
        source_ref[r] = columns_of[0][:, at] * share_c + columns_of[1][:, at] * share_v

    spread = (iota((levels, points), 1) % levels == iota((levels, points), 0)).astype(BF16)
    full = (points, points)
    same = iota(full, 0) // levels == iota(full, 1) // levels
    for r in range(rows):
        at = slice(r, r + 1)
        inverse = inverse_ref[r // lon, r % lon].reshape(points, levels)
        high = inverse.astype(BF16)
        low = (inverse - high.astype(F32)).astype(BF16)
        keep = jnp.where(same, wet[at, :] * columns_of[3][:, at], 0.0)
        for ref, part in ((high_ref, high), (low_ref, low)):
            tiled = jnp.dot(part, spread, preferred_element_type=F32)
            ref[r] = (tiled * keep).astype(BF16)

    gram_ref[...] = jnp.zeros(gram_ref.shape, F32)
    count = basis_ref.shape[0]
    row = 0
    for k in range(count):
        for j in range(k, count):
            gram_ref[row : row + 1, :] = jnp.sum(basis_ref[k] * basis_ref[j], 0, keepdims=True)
            row += 1


def sources(own_c, own_v, rate):
    denom = own_c * own_c + 1.0
    uptake = rate * own_c * own_c / denom
    slope = rate * 2.0 * own_c / (denom * denom)
    return uptake, slope * own_v


def beyond(lat, lon):
    found = {}
    for r in range(lat * lon):
        ends = [k for k in range(9) if not 0 <= r % lon + k % 3 - 1 < lon]
        if ends:
            found[r] = ends
    return found


def pull_kernel(lat, lon, state_ref, edge_ref, rate_column_ref, stoich_ref, source_ref):
    rows, _, tracers = source_ref.shape
    share = stoich_ref[...]
    edges = list(beyond(lat, lon))
    for r in range(rows):
        ref, at = (edge_ref, edges.index(r)) if r in edges else (state_ref, r)
        own_c = ref[at, :, 0:1]
        own_v = ref[at, :, tracers : tracers + 1]
        source_ref[r] = sources(own_c, own_v, rate_column_ref[:, r : r + 1])[1] * share


def fill(pad_ref, x_ref, north_ref, south_ref, lat, lon):
    wide = lon + 2
    for j in range(lon):
        pad_ref[1 + j] = north_ref[j]
        pad_ref[(lat + 1) * wide + 1 + j] = south_ref[j]
        for i in range(lat):
            pad_ref[(i + 1) * wide + 1 + j] = x_ref[i * lon + j]
    pad_ref[(lat + 2) * wide] = jnp.zeros(pad_ref.shape[1:], BF16)


def transport(r, index_ref, pad_ref, held_ref, z, neighbours):
    lon, slots = index_ref.shape[2:]
    for k in neighbours:
        block = held_ref[r * slots + index_ref[0, r // lon, r % lon, k]]
        x = pad_ref[index_ref[1, r // lon, r % lon, k]]
        z = z + lax.dot_general(block, x, NT, preferred_element_type=F32)
    return z


def mix(z, high, low):
    z_high = z.astype(BF16)
    z_low = (z - z_high.astype(F32)).astype(BF16)
    dot = functools.partial(jnp.dot, preferred_element_type=F32)
    return dot(high, z_high) + (dot(low, z_high) + dot(high, z_low))


def bulk(
    lat, lon, index_ref, pad_ref, held_ref, high_ref, low_ref, source_ref, state_ref, later_ref
):
    edges = beyond(lat, lon)
    slots = index_ref.shape[3]
    n = 0
    for r, neighbours in edges.items():
        for k in neighbours:
            at = (r // lon, r % lon, k)
            block = held_ref[r * slots + index_ref[0, *at]]
            named = index_ref[1, *at] < (lat + 2) * (lon + 2)
            later_ref[n] = jnp.where(named, block, jnp.zeros_like(block))
            n += 1
    for r in range(lat * lon):
        neighbours = [k for k in range(9) if k not in edges.get(r, ())]
        state_ref[r] = transport(r, index_ref, pad_ref, held_ref, source_ref[r], neighbours)
    for r in range(lat * lon):
        if r not in edges:
            state_ref[r] = mix(state_ref[r], high_ref[r], low_ref[r])


def finish(lat, lon, west_ref, east_ref, state_ref, later_ref, high_ref, low_ref, out_ref):
    edges = beyond(lat, lon)
    at = 0
    for n, (r, neighbours) in enumerate(edges.items()):
        z = state_ref[r]
        for k in neighbours:
            x = (west_ref if r % lon + k % 3 == 0 else east_ref)[r // lon + k // 3]
            z = z + lax.dot_general(later_ref[at], x, NT, preferred_element_type=F32)
            at += 1
        out_ref[n] = z
    for n, r in enumerate(edges):
        out_ref[n] = mix(out_ref[n], high_ref[r], low_ref[r])


def first_kernel(
    lat,
    lon,
    index_ref,
    x_ref,
    north_ref,
    south_ref,
    held_ref,
    high_ref,
    low_ref,
    source_ref,
    y_ref,
    state_ref,
    later_ref,
    pad_ref,
):
    fill(pad_ref, x_ref, north_ref, south_ref, lat, lon)
    bulk(
        lat, lon, index_ref, pad_ref, held_ref, high_ref, low_ref, source_ref, state_ref, later_ref
    )
    tracers = y_ref.shape[1]
    for r in range(lat * lon):
        if r in beyond(lat, lon):
            y_ref[r] = jnp.zeros(y_ref.shape[1:], BF16)
        else:
            y_ref[r] = jnp.transpose(state_ref[r])[tracers:].astype(BF16)


def first_end_kernel(
    lat,
    lon,
    west_ref,
    east_ref,
    state_ref,
    later_ref,
    high_ref,
    low_ref,
    part_ref,
    y_ref,
    first_ref,
    last_ref,
    left_ref,
    right_ref,
    edge_ref,
):
    finish(lat, lon, west_ref, east_ref, state_ref, later_ref, high_ref, low_ref, edge_ref)
    edges = list(beyond(lat, lon))
    tracers = y_ref.shape[1]
    for r in range(lat * lon):
        if r in edges:
            y = jnp.transpose(edge_ref[edges.index(r)])[tracers:].astype(BF16)
        else:
            y = part_ref[r]
        share_out(r, y, y_ref, first_ref, last_ref, left_ref, right_ref)


def share_out(r, x, x_ref, first_ref, last_ref, left_ref, right_ref):
    rows, lon = x_ref.shape[0], first_ref.shape[0]
    x_ref[r] = x
    if r < lon:
        first_ref[r] = x
    if r >= rows - lon:
        last_ref[r - (rows - lon)] = x
    if r % lon == 0:
        left_ref[r // lon] = x
    if r % lon == lon - 1:
        right_ref[r // lon] = x


def second_kernel(
    lat,
    lon,
    index_ref,
    x_ref,
    north_ref,
    south_ref,
    held_ref,
    high_ref,
    low_ref,
    source_ref,
    part_ref,
    state_ref,
    later_ref,
    pad_ref,
):
    rows = lat * lon
    fill(pad_ref, x_ref, north_ref, south_ref, lat, lon)
    bulk(
        lat, lon, index_ref, pad_ref, held_ref, high_ref, low_ref, source_ref, state_ref, later_ref
    )
    tracers = x_ref.shape[1]
    for r in range(rows):
        at = pl.ds(r, tracers, stride=rows)
        if r in beyond(lat, lon):
            part_ref[at, :] = jnp.zeros((tracers, part_ref.shape[1]), F32)
        else:
            part_ref[at, :] = jnp.transpose(state_ref[r])


def second_end_kernel(
    lat,
    lon,
    west_ref,
    east_ref,
    state_ref,
    later_ref,
    high_ref,
    low_ref,
    part_ref,
    gram_ref,
    basis_ref,
    product_ref,
    out_hbm,
    sums_ref,
    edge_ref,
    sem,
):
    finish(lat, lon, west_ref, east_ref, state_ref, later_ref, high_ref, low_ref, edge_ref)
    rows = lat * lon
    product_ref[...] = part_ref[...]
    tracers = product_ref.shape[0] // rows
    for n, r in enumerate(beyond(lat, lon)):
        product_ref[pl.ds(r, tracers, stride=rows), :] = jnp.transpose(edge_ref[n])
    copy = pltpu.make_async_copy(product_ref, out_hbm, sem)
    copy.start()
    product = product_ref[...]
    count = basis_ref.shape[0]
    pairs = count * (count + 1) // 2
    all_sums = gram_ref[...]
    spot = iota(all_sums.shape, 0)
    for k in range(count + 1):
        other = basis_ref[k] if k < count else product
        part = jnp.sum(product * other, 0, keepdims=True)
        all_sums = jnp.where(spot == pairs + k, part, all_sums)
    column = jnp.sum(all_sums, 1, keepdims=True)
    row = jnp.sum(jnp.where(spot == iota(spot.shape, 1), column, 0.0), 0, keepdims=True)
    sums_ref[...] = jnp.broadcast_to(row, sums_ref.shape)
    copy.wait()


def last_kernel(parts_ref, product_ref, basis_ref, next_ref, coeffs_ref, flag_ref):
    count = basis_ref.shape[0]
    row = jnp.sum(parts_ref[...], 0, keepdims=True)
    lane = iota(row.shape, 1)

    def pick(at):
        return jnp.sum(jnp.where(lane == at, row, 0.0), 1, keepdims=True)

    pairs = count * (count + 1) // 2
    heights = [pick(pairs + k) for k in range(count)]
    whole = pick(pairs + count)
    cross = jnp.zeros((1, 1), F32)
    at = 0
    for k in range(count):
        for j in range(k, count):
            twice = 1.0 if k == j else 2.0
            cross = cross + twice * (heights[k] * heights[j] * pick(at))
            at += 1
    squares = sum(h * h for h in heights)
    short = whole - 2.0 * squares + cross
    size = whole + 2.0 * squares + cross
    beta = jnp.sqrt(jnp.maximum(short, 0.0) + 1e-06)
    rest = product_ref[...]
    for k in range(count):
        rest = rest - heights[k] * basis_ref[k]
    next_ref[...] = rest / beta
    for k in range(count):
        coeffs_ref[k] = heights[k][0, 0]
    coeffs_ref[count] = beta[0, 0]
    flag_ref[0] = jnp.where(short < 0.01 * size, 1, 0)[0, 0]


def summed(rows):
    row = jnp.sum(lax.all_to_all(rows, "lon", 0, 0), 0, keepdims=True)
    rows = jnp.broadcast_to(row, (lax.axis_size("lat"), row.shape[1]))
    return lax.all_to_all(rows, "lat", 0, 0)


def moved(a, axis, step, around):
    size = lax.axis_size(axis)
    pairs = [(i, (i + step) % size) for i in range(size) if around or 0 <= i + step < size]
    return lax.ppermute(a, axis, pairs)


def rows_around(first, last, beside):
    north = moved(last, "lat", 1, True)
    south = moved(first, "lat", -1, True)
    return lax.optimization_barrier((north, south, beside))


def columns_around(left, right, north, south):
    right = jnp.concatenate([north[-1:], right, south[-1:]], 0)
    left = jnp.concatenate([north[:1], left, south[:1]], 0)
    return moved(right, "lon", 1, False), moved(left, "lon", -1, False)


def body(
    base_state,
    tangent,
    blocks,
    pattern,
    live,
    column_inverse,
    col_depth,
    uptake_rate,
    stoich,
    basis,
):
    tracers, lat, lon, points = base_state.shape
    slots = pattern.shape[2]
    count = basis.shape[0]
    rows = lat * lon
    total_lon = lon * lax.axis_size("lon")
    size = tracers * rows
    places = (lat + 2) * (lon + 2) + 1
    share = stoich.reshape(1, tracers)

    flat_c = base_state.reshape(size, points)
    flat_v = tangent.reshape(size, points)
    def edges(width):
        return (
            like((rows, width, points), BF16),
            like((lon, width, points), BF16),
            like((lon, width, points), BF16),
            like((lat, width, points), BF16),
            like((lat, width, points), BF16),
        )

    begun = call(begin_kernel, like((8, points)), [], VMEM, flops=PACK)()
    x, first, last, left, right = call(
        pack_kernel, edges(2 * tracers), [VMEM] * 3, [VMEM] * 5, flops=PACK, size=400000
    )(begun, flat_c, flat_v)

    flat_basis = basis.reshape(count, size, points)
    held = blocks.reshape(rows * slots, points, points)
    index, high, low, source, rate_column, gram = call(
        functools.partial(prep_kernel, total_lon),
        (
            like((2, lat, lon, slots), jnp.int32),
            like((rows, points, points), BF16),
            like((rows, points, points), BF16),
            like((rows, points, 2 * tracers)),
            like((points, (rows + 7) // 8 * 8)),
            like((16, points)),
        ),
        [VMEM] * 9,
        [VMEM] * 6,
        flops=PREP,
        size=8000000,
    )(
        pattern,
        live,
        column_inverse,
        col_depth,
        uptake_rate,
        share,
        flat_basis,
        flat_c,
        flat_v,
    )

    work = 2 * 2 * tracers * rows * slots * points * points
    ends = len(beyond(lat, lon))
    later = like((sum(map(len, beyond(lat, lon).values())), points, points), BF16)

    prepared = (index, high, low, source, rate_column, gram)
    north, south, prepared = rows_around(first, last, prepared)
    index, high, low, source, rate_column, gram = prepared
    west, east = columns_around(left, right, north, south)
    part, state, blocks_later = call(
        functools.partial(first_kernel, lat, lon),
        (like((rows, tracers, points), BF16), like((rows, points, 2 * tracers)), later),
        [SMEM] + [VMEM] * 7,
        [VMEM] * 3,
        scratch=[pltpu.VMEM((places, 2 * tracers, points), BF16)],
        flops=BULK,
        size=5000000,
    )(index, x, north, south, held, high, low, source)
    x, first, last, left, right, edge = call(
        functools.partial(first_end_kernel, lat, lon),
        edges(tracers) + (like((ends, points, 2 * tracers)),),
        [VMEM] * 7,
        [VMEM] * 6,
        flops=work // 20,
        size=500000,
    )(west, east, state, blocks_later, high, low, part)

    source = call(
        functools.partial(pull_kernel, lat, lon),
        like((rows, points, tracers)),
        [VMEM] * 4,
        VMEM,
        flops=100000,
        size=2000000,
    )(state, edge, rate_column, share)

    north, south, source = rows_around(first, last, source)
    west, east = columns_around(left, right, north, south)
    part, state, blocks_later = call(
        functools.partial(second_kernel, lat, lon),
        (like((size, points)), like((rows, points, tracers)), later),
        [SMEM] + [VMEM] * 7,
        [VMEM] * 3,
        scratch=[pltpu.VMEM((places, tracers, points), BF16)],
        flops=BULK,
        size=5000000,
    )(index, x, north, south, held, high, low, source)
    product, written, sums = call(
        functools.partial(second_end_kernel, lat, lon),
        (like((size, points)), like((size, points)), like((lax.axis_size("lon"), points))),
        [VMEM] * 9,
        [VMEM, HBM, VMEM],
        scratch=[pltpu.VMEM((ends, points, tracers), F32), pltpu.SemaphoreType.DMA],
        flops=work // 20,
        size=1500000,
    )(west, east, state, blocks_later, high, low, part, gram, flat_basis)

    parts = summed(sums)
    following, coeffs, flag = call(
        last_kernel,
        (like((size, points)), like((count + 1,)), like((1,), jnp.int32)),
        [VMEM] * 3,
        [VMEM, SMEM, SMEM],
        size=700000,
    )(parts, product, flat_basis)

    def again(carry):
        pairs = count * (count + 1) // 2
        heights = jnp.sum(parts, 0)[pairs : pairs + count]
        rest = product - jnp.einsum(
            "k,ksp->sp", heights, flat_basis, precision=lax.Precision.HIGHEST
        )
        part = jnp.pad(jnp.sum(rest * rest).reshape(1, 1), ((0, 0), (0, points - 1)))
        squared = jnp.sum(summed(jnp.broadcast_to(part, (lax.axis_size("lon"), points))), 0)[0]
        beta = jnp.sqrt(squared + 1e-06)
        return rest / beta, jnp.concatenate([heights, beta[None]]), carry[2] * 0

    following, coeffs, flag = lax.while_loop(
        lambda carry: carry[2][0] > 0, again, (following, coeffs, flag)
    )
    shape = base_state.shape
    return written.reshape(shape), following.reshape(shape), coeffs


def solution(mesh):
    placed = (
        P(None, "lat", "lon", None),
        P(None, "lat", "lon", None),
        P("lat", "lon", None, None, None),
        P("lat", "lon", None),
        P("lat", "lon", None),
        P("lat", "lon", None, None, None),
        P("lat", "lon", None),
        P("lat", "lon", None),
        P(),
        P(None, None, "lat", "lon", None),
    )
    return jax.shard_map(
        body,
        mesh=mesh,
        in_specs=placed,
        out_specs=(P(None, "lat", "lon", None), P(None, "lat", "lon", None), P()),
        check_vma=False,
    )
```

```python
import functools

import jax
import jax.numpy as jnp
from jax import lax
from jax.experimental import pallas as pl
from jax.experimental.pallas import tpu as pltpu
from jax.sharding import PartitionSpec as P

F32 = jnp.float32
BF16 = jnp.bfloat16
VMEM = pl.BlockSpec(memory_space=pltpu.VMEM)
SMEM = pl.BlockSpec(memory_space=pltpu.SMEM)
HBM = pl.BlockSpec(memory_space=pltpu.HBM)
PACK = 20000000000
PREP = 10000000000
BULK = 2000000000
NT = (((1,), (1,)), ((), ()))


def call(kernel, outs, ins, out_specs, scratch=(), flops=0, size=0, limit=16):
    return pl.pallas_call(
        kernel,
        out_shape=outs,
        in_specs=ins,
        out_specs=out_specs,
        scratch_shapes=list(scratch),
        compiler_params=pltpu.CompilerParams(vmem_limit_bytes=limit * 2**20),
        cost_estimate=pl.CostEstimate(flops=flops, bytes_accessed=size, transcendentals=0),
    )


def like(shape, dtype=F32):
    return jax.ShapeDtypeStruct(shape, dtype)


def iota(shape, dim):
    return lax.broadcasted_iota(jnp.int32, shape, dim)


def begin_kernel(out_ref):
    out_ref[...] = jnp.zeros(out_ref.shape, F32)


def pack_kernel(
    begun_ref, c_ref, v_ref, x_ref, first_ref, last_ref, left_ref, right_ref
):
    rows = x_ref.shape[0]
    tracers = c_ref.shape[0] // rows
    for r in range(rows):
        at = pl.ds(r, tracers, stride=rows)
        x = jnp.concatenate([c_ref[at, :], v_ref[at, :]], 0).astype(BF16)
        share_out(r, x, x_ref, first_ref, last_ref, left_ref, right_ref)


def prep_kernel(
    total_lon,
    pattern_ref,
    live_ref,
    inverse_ref,
    depth_ref,
    rate_ref,
    stoich_ref,
    basis_ref,
    c_ref,
    v_ref,
    index_ref,
    high_ref,
    low_ref,
    source_ref,
    rate_column_ref,
    gram_ref,
):
    lat, lon, slots = pattern_ref.shape
    rows = lat * lon
    columns, levels = inverse_ref.shape[2:4]
    points = columns * levels
    pattern = pattern_ref[...]
    itself = pattern[:, :, :1]
    far_lat = pattern // total_lon - itself // total_lon
    far_lon = pattern % total_lon - itself % total_lon
    shape = pattern.shape
    named = jnp.where(live_ref[...] > 0, (far_lat + 1) * 3 + far_lon + 1, -1)
    slot = iota(shape, 2)
    place = (iota(shape, 0) + slot // 3) * (lon + 2) + iota(shape, 1) + slot % 3
    held_at = jnp.zeros(shape, jnp.int32)
    found_at = jnp.zeros(shape, jnp.int32)
    for k in range(9):
        match = named == k
        held_at = jnp.where(
            slot == k, jnp.sum(jnp.where(match, slot, 0), 2, keepdims=True), held_at
        )
        found_at = jnp.where(
            slot == k, jnp.sum(jnp.where(match, 1, 0), 2, keepdims=True), found_at
        )
    index_ref[0] = held_at
    index_ref[1] = jnp.where(found_at > 0, place, (lat + 2) * (lon + 2))

    lane = iota((rows, points), 1)
    depth = jnp.concatenate([depth_ref[i] for i in range(lat)], 0)
    below = jnp.zeros((rows, points), jnp.int32)
    for k in range(columns):
        below = jnp.where(lane // levels == k, depth[:, k : k + 1], below)
    wet = (lane % levels < below).astype(F32)

    rate = jnp.concatenate([rate_ref[i] for i in range(lat)], 0)
    uptake, pull = sources(c_ref[:rows, :], v_ref[:rows, :], rate)
    spare = 8 - rows % 8 if rows % 8 else 0
    blank = [jnp.zeros((spare, points), F32)] if spare else []
    columns_of = [
        jnp.transpose(jnp.concatenate([part] + blank, 0)) for part in (uptake, pull, rate, wet)
    ]
    rate_column_ref[...] = columns_of[2]
    tracers = source_ref.shape[2] // 2
    share = stoich_ref[...]
    nothing = jnp.zeros((1, tracers), F32)
    share_c = jnp.concatenate([share, nothing], 1)
    share_v = jnp.concatenate([nothing, share], 1)
    for r in range(rows):
        at = slice(r, r + 1)
        source_ref[r] = columns_of[0][:, at] * share_c + columns_of[1][:, at] * share_v

    spread = (iota((levels, points), 1) % levels == iota((levels, points), 0)).astype(BF16)
    full = (points, points)
    same = iota(full, 0) // levels == iota(full, 1) // levels
    for r in range(rows):
        at = slice(r, r + 1)
        inverse = inverse_ref[r // lon, r % lon].reshape(points, levels)
        high = inverse.astype(BF16)
        low = (inverse - high.astype(F32)).astype(BF16)
        keep = jnp.where(same, wet[at, :] * columns_of[3][:, at], 0.0)
        for ref, part in ((high_ref, high), (low_ref, low)):
            tiled = jnp.dot(part, spread, preferred_element_type=F32)
            ref[r] = (tiled * keep).astype(BF16)

    gram_ref[...] = jnp.zeros(gram_ref.shape, F32)
    count = basis_ref.shape[0]
    row = 0
    for k in range(count):
        for j in range(k, count):
            gram_ref[row : row + 1, :] = jnp.sum(basis_ref[k] * basis_ref[j], 0, keepdims=True)
            row += 1


def sources(own_c, own_v, rate):
    denom = own_c * own_c + 1.0
    uptake = rate * own_c * own_c / denom
    slope = rate * 2.0 * own_c / (denom * denom)
    return uptake, slope * own_v


def beyond(lat, lon):
    found = {}
    for r in range(lat * lon):
        ends = [k for k in range(9) if not 0 <= r % lon + k % 3 - 1 < lon]
        if ends:
            found[r] = ends
    return found


def pull_kernel(lat, lon, state_ref, edge_ref, rate_column_ref, stoich_ref, source_ref):
    rows, _, tracers = source_ref.shape
    share = stoich_ref[...]
    edges = list(beyond(lat, lon))
    for r in range(rows):
        ref, at = (edge_ref, edges.index(r)) if r in edges else (state_ref, r)
        own_c = ref[at, :, 0:1]
        own_v = ref[at, :, tracers : tracers + 1]
        source_ref[r] = sources(own_c, own_v, rate_column_ref[:, r : r + 1])[1] * share


def fill(pad_ref, x_ref, north_ref, south_ref, lat, lon):
    wide = lon + 2
    for j in range(lon):
        pad_ref[1 + j] = north_ref[j]
        pad_ref[(lat + 1) * wide + 1 + j] = south_ref[j]
        for i in range(lat):
            pad_ref[(i + 1) * wide + 1 + j] = x_ref[i * lon + j]
    pad_ref[(lat + 2) * wide] = jnp.zeros(pad_ref.shape[1:], BF16)


def transport(r, index_ref, pad_ref, held_ref, z, neighbours):
    lon, slots = index_ref.shape[2:]
    for k in neighbours:
        block = held_ref[r * slots + index_ref[0, r // lon, r % lon, k]]
        x = pad_ref[index_ref[1, r // lon, r % lon, k]]
        z = z + lax.dot_general(block, x, NT, preferred_element_type=F32)
    return z


def mix(z, high, low):
    z_high = z.astype(BF16)
    z_low = (z - z_high.astype(F32)).astype(BF16)
    dot = functools.partial(jnp.dot, preferred_element_type=F32)
    return dot(high, z_high) + (dot(low, z_high) + dot(high, z_low))


def bulk(
    lat, lon, index_ref, pad_ref, held_ref, high_ref, low_ref, source_ref, state_ref, later_ref
):
    edges = beyond(lat, lon)
    slots = index_ref.shape[3]
    n = 0
    for r, neighbours in edges.items():
        for k in neighbours:
            at = (r // lon, r % lon, k)
            block = held_ref[r * slots + index_ref[0, *at]]
            named = index_ref[1, *at] < (lat + 2) * (lon + 2)
            later_ref[n] = jnp.where(named, block, jnp.zeros_like(block))
            n += 1
    for r in range(lat * lon):
        neighbours = [k for k in range(9) if k not in edges.get(r, ())]
        state_ref[r] = transport(r, index_ref, pad_ref, held_ref, source_ref[r], neighbours)
    for r in range(lat * lon):
        if r not in edges:
            state_ref[r] = mix(state_ref[r], high_ref[r], low_ref[r])


def finish(lat, lon, west_ref, east_ref, state_ref, later_ref, high_ref, low_ref, out_ref):
    edges = beyond(lat, lon)
    at = 0
    for n, (r, neighbours) in enumerate(edges.items()):
        z = state_ref[r]
        for k in neighbours:
            x = (west_ref if r % lon + k % 3 == 0 else east_ref)[r // lon + k // 3]
            z = z + lax.dot_general(later_ref[at], x, NT, preferred_element_type=F32)
            at += 1
        out_ref[n] = z
    for n, r in enumerate(edges):
        out_ref[n] = mix(out_ref[n], high_ref[r], low_ref[r])


def first_kernel(
    lat,
    lon,
    index_ref,
    x_ref,
    north_ref,
    south_ref,
    held_ref,
    high_ref,
    low_ref,
    source_ref,
    y_ref,
    state_ref,
    later_ref,
    pad_ref,
):
    fill(pad_ref, x_ref, north_ref, south_ref, lat, lon)
    bulk(
        lat, lon, index_ref, pad_ref, held_ref, high_ref, low_ref, source_ref, state_ref, later_ref
    )
    tracers = y_ref.shape[1]
    for r in range(lat * lon):
        if r in beyond(lat, lon):
            y_ref[r] = jnp.zeros(y_ref.shape[1:], BF16)
        else:
            y_ref[r] = jnp.transpose(state_ref[r])[tracers:].astype(BF16)


def first_end_kernel(
    lat,
    lon,
    west_ref,
    east_ref,
    state_ref,
    later_ref,
    high_ref,
    low_ref,
    part_ref,
    y_ref,
    first_ref,
    last_ref,
    left_ref,
    right_ref,
    edge_ref,
):
    finish(lat, lon, west_ref, east_ref, state_ref, later_ref, high_ref, low_ref, edge_ref)
    edges = list(beyond(lat, lon))
    tracers = y_ref.shape[1]
    for r in range(lat * lon):
        if r in edges:
            y = jnp.transpose(edge_ref[edges.index(r)])[tracers:].astype(BF16)
        else:
            y = part_ref[r]
        share_out(r, y, y_ref, first_ref, last_ref, left_ref, right_ref)


def share_out(r, x, x_ref, first_ref, last_ref, left_ref, right_ref):
    rows, lon = x_ref.shape[0], first_ref.shape[0]
    x_ref[r] = x
    if r < lon:
        first_ref[r] = x
    if r >= rows - lon:
        last_ref[r - (rows - lon)] = x
    if r % lon == 0:
        left_ref[r // lon] = x
    if r % lon == lon - 1:
        right_ref[r // lon] = x


def second_kernel(
    lat,
    lon,
    index_ref,
    x_ref,
    north_ref,
    south_ref,
    held_ref,
    high_ref,
    low_ref,
    source_ref,
    part_ref,
    state_ref,
    later_ref,
    pad_ref,
):
    rows = lat * lon
    fill(pad_ref, x_ref, north_ref, south_ref, lat, lon)
    bulk(
        lat, lon, index_ref, pad_ref, held_ref, high_ref, low_ref, source_ref, state_ref, later_ref
    )
    tracers = x_ref.shape[1]
    for r in range(rows):
        at = pl.ds(r, tracers, stride=rows)
        if r in beyond(lat, lon):
            part_ref[at, :] = jnp.zeros((tracers, part_ref.shape[1]), F32)
        else:
            part_ref[at, :] = jnp.transpose(state_ref[r])


def second_end_kernel(
    lat,
    lon,
    west_ref,
    east_ref,
    state_ref,
    later_ref,
    high_ref,
    low_ref,
    part_ref,
    gram_ref,
    basis_ref,
    product_ref,
    out_hbm,
    sums_ref,
    edge_ref,
    sem,
):
    finish(lat, lon, west_ref, east_ref, state_ref, later_ref, high_ref, low_ref, edge_ref)
    rows = lat * lon
    product_ref[...] = part_ref[...]
    tracers = product_ref.shape[0] // rows
    for n, r in enumerate(beyond(lat, lon)):
        product_ref[pl.ds(r, tracers, stride=rows), :] = jnp.transpose(edge_ref[n])
    copy = pltpu.make_async_copy(product_ref, out_hbm, sem)
    copy.start()
    product = product_ref[...]
    count = basis_ref.shape[0]
    pairs = count * (count + 1) // 2
    all_sums = gram_ref[...]
    spot = iota(all_sums.shape, 0)
    for k in range(count + 1):
        other = basis_ref[k] if k < count else product
        part = jnp.sum(product * other, 0, keepdims=True)
        all_sums = jnp.where(spot == pairs + k, part, all_sums)
    column = jnp.sum(all_sums, 1, keepdims=True)
    row = jnp.sum(jnp.where(spot == iota(spot.shape, 1), column, 0.0), 0, keepdims=True)
    sums_ref[...] = jnp.broadcast_to(row, sums_ref.shape)
    copy.wait()


def last_kernel(parts_ref, product_ref, basis_ref, next_ref, coeffs_ref, flag_ref):
    count = basis_ref.shape[0]
    row = jnp.sum(parts_ref[...], 0, keepdims=True)
    lane = iota(row.shape, 1)

    def pick(at):
        return jnp.sum(jnp.where(lane == at, row, 0.0), 1, keepdims=True)

    pairs = count * (count + 1) // 2
    heights = [pick(pairs + k) for k in range(count)]
    whole = pick(pairs + count)
    cross = jnp.zeros((1, 1), F32)
    at = 0
    for k in range(count):
        for j in range(k, count):
            twice = 1.0 if k == j else 2.0
            cross = cross + twice * (heights[k] * heights[j] * pick(at))
            at += 1
    squares = sum(h * h for h in heights)
    short = whole - 2.0 * squares + cross
    size = whole + 2.0 * squares + cross
    beta = jnp.sqrt(jnp.maximum(short, 0.0) + 1e-06)
    rest = product_ref[...]
    for k in range(count):
        rest = rest - heights[k] * basis_ref[k]
    next_ref[...] = rest / beta
    for k in range(count):
        coeffs_ref[k] = heights[k][0, 0]
    coeffs_ref[count] = beta[0, 0]
    flag_ref[0] = jnp.where(short < 0.01 * size, 1, 0)[0, 0]


def summed(rows):
    row = jnp.sum(lax.all_to_all(rows, "lon", 0, 0), 0, keepdims=True)
    rows = jnp.broadcast_to(row, (lax.axis_size("lat"), row.shape[1]))
    return lax.all_to_all(rows, "lat", 0, 0)


def rows_around(first, last, beside):
    size = lax.axis_size("lat")
    north = lax.ppermute(last, "lat", [(i, (i + 1) % size) for i in range(size)])
    south = lax.ppermute(first, "lat", [((i + 1) % size, i) for i in range(size)])
    return lax.optimization_barrier((north, south, beside))


def columns_around(left, right, north, south):
    size = lax.axis_size("lon")
    odd = lax.axis_index("lon") % 2 == 1
    right = jnp.concatenate([north[-1:], right, south[-1:]], 0)
    left = jnp.concatenate([north[:1], left, south[:1]], 0)

    def swapped(a, start):
        pairs = [(i, i + 1) for i in range(start, size - 1, 2)]
        return lax.ppermute(a, "lon", pairs + [(j, i) for i, j in pairs])

    near = swapped(jnp.where(odd, left, right), 0)
    far = swapped(jnp.where(odd, right, left), 1)
    far, near = lax.optimization_barrier((far, near))
    return jnp.where(odd, near, far), jnp.where(odd, far, near)


def body(
    base_state,
    tangent,
    blocks,
    pattern,
    live,
    column_inverse,
    col_depth,
    uptake_rate,
    stoich,
    basis,
):
    tracers, lat, lon, points = base_state.shape
    slots = pattern.shape[2]
    count = basis.shape[0]
    rows = lat * lon
    total_lon = lon * lax.axis_size("lon")
    size = tracers * rows
    places = (lat + 2) * (lon + 2) + 1
    share = stoich.reshape(1, tracers)

    flat_c = base_state.reshape(size, points)
    flat_v = tangent.reshape(size, points)
    def edges(width):
        return (
            like((rows, width, points), BF16),
            like((lon, width, points), BF16),
            like((lon, width, points), BF16),
            like((lat, width, points), BF16),
            like((lat, width, points), BF16),
        )

    begun = call(begin_kernel, like((8, points)), [], VMEM, flops=PACK)()
    x, first, last, left, right = call(
        pack_kernel, edges(2 * tracers), [VMEM] * 3, [VMEM] * 5, flops=PACK, size=400000
    )(begun, flat_c, flat_v)

    flat_basis = basis.reshape(count, size, points)
    held = blocks.reshape(rows * slots, points, points)
    index, high, low, source, rate_column, gram = call(
        functools.partial(prep_kernel, total_lon),
        (
            like((2, lat, lon, slots), jnp.int32),
            like((rows, points, points), BF16),
            like((rows, points, points), BF16),
            like((rows, points, 2 * tracers)),
            like((points, (rows + 7) // 8 * 8)),
            like((16, points)),
        ),
        [VMEM] * 9,
        [VMEM] * 6,
        flops=PREP,
        size=8000000,
    )(
        pattern,
        live,
        column_inverse,
        col_depth,
        uptake_rate,
        share,
        flat_basis,
        flat_c,
        flat_v,
    )

    work = 2 * 2 * tracers * rows * slots * points * points
    ends = len(beyond(lat, lon))
    later = like((sum(map(len, beyond(lat, lon).values())), points, points), BF16)

    prepared = (index, high, low, source, rate_column, gram)
    north, south, prepared = rows_around(first, last, prepared)
    index, high, low, source, rate_column, gram = prepared
    west, east = columns_around(left, right, north, south)
    part, state, blocks_later = call(
        functools.partial(first_kernel, lat, lon),
        (like((rows, tracers, points), BF16), like((rows, points, 2 * tracers)), later),
        [SMEM] + [VMEM] * 7,
        [VMEM] * 3,
        scratch=[pltpu.VMEM((places, 2 * tracers, points), BF16)],
        flops=BULK,
        size=5000000,
    )(index, x, north, south, held, high, low, source)
    x, first, last, left, right, edge = call(
        functools.partial(first_end_kernel, lat, lon),
        edges(tracers) + (like((ends, points, 2 * tracers)),),
        [VMEM] * 7,
        [VMEM] * 6,
        flops=work // 20,
        size=500000,
    )(west, east, state, blocks_later, high, low, part)

    source = call(
        functools.partial(pull_kernel, lat, lon),
        like((rows, points, tracers)),
        [VMEM] * 4,
        VMEM,
        flops=100000,
        size=2000000,
    )(state, edge, rate_column, share)

    north, south, source = rows_around(first, last, source)
    west, east = columns_around(left, right, north, south)
    part, state, blocks_later = call(
        functools.partial(second_kernel, lat, lon),
        (like((size, points)), like((rows, points, tracers)), later),
        [SMEM] + [VMEM] * 7,
        [VMEM] * 3,
        scratch=[pltpu.VMEM((places, tracers, points), BF16)],
        flops=BULK,
        size=5000000,
    )(index, x, north, south, held, high, low, source)
    product, written, sums = call(
        functools.partial(second_end_kernel, lat, lon),
        (like((size, points)), like((size, points)), like((lax.axis_size("lon"), points))),
        [VMEM] * 9,
        [VMEM, HBM, VMEM],
        scratch=[pltpu.VMEM((ends, points, tracers), F32), pltpu.SemaphoreType.DMA],
        flops=work // 20,
        size=1500000,
    )(west, east, state, blocks_later, high, low, part, gram, flat_basis)

    parts = summed(sums)
    following, coeffs, flag = call(
        last_kernel,
        (like((size, points)), like((count + 1,)), like((1,), jnp.int32)),
        [VMEM] * 3,
        [VMEM, SMEM, SMEM],
        size=700000,
    )(parts, product, flat_basis)

    def again(carry):
        pairs = count * (count + 1) // 2
        heights = jnp.sum(parts, 0)[pairs : pairs + count]
        rest = product - jnp.einsum(
            "k,ksp->sp", heights, flat_basis, precision=lax.Precision.HIGHEST
        )
        part = jnp.pad(jnp.sum(rest * rest).reshape(1, 1), ((0, 0), (0, points - 1)))
        squared = jnp.sum(summed(jnp.broadcast_to(part, (lax.axis_size("lon"), points))), 0)[0]
        beta = jnp.sqrt(squared + 1e-06)
        return rest / beta, jnp.concatenate([heights, beta[None]]), carry[2] * 0

    following, coeffs, flag = lax.while_loop(
        lambda carry: carry[2][0] > 0, again, (following, coeffs, flag)
    )
    shape = base_state.shape
    return written.reshape(shape), following.reshape(shape), coeffs


def solution(mesh):
    placed = (
        P(None, "lat", "lon", None),
        P(None, "lat", "lon", None),
        P("lat", "lon", None, None, None),
        P("lat", "lon", None),
        P("lat", "lon", None),
        P("lat", "lon", None, None, None),
        P("lat", "lon", None),
        P("lat", "lon", None),
        P(),
        P(None, None, "lat", "lon", None),
    )
    return jax.shard_map(
        body,
        mesh=mesh,
        in_specs=placed,
        out_specs=(P(None, "lat", "lon", None), P(None, "lat", "lon", None), P()),
        check_vma=False,
    )
```

```python
import functools

import jax
import jax.numpy as jnp
from jax import lax
from jax.experimental import pallas as pl
from jax.experimental.pallas import tpu as pltpu
from jax.sharding import PartitionSpec as P

F32 = jnp.float32
BF16 = jnp.bfloat16
VMEM = pl.BlockSpec(memory_space=pltpu.VMEM)
SMEM = pl.BlockSpec(memory_space=pltpu.SMEM)
HBM = pl.BlockSpec(memory_space=pltpu.HBM)
PACK = 20000000000
PREP = 10000000000
BULK = 2000000000
NT = (((1,), (1,)), ((), ()))


def call(kernel, outs, ins, out_specs, scratch=(), flops=0, size=0, limit=16):
    return pl.pallas_call(
        kernel,
        out_shape=outs,
        in_specs=ins,
        out_specs=out_specs,
        scratch_shapes=list(scratch),
        compiler_params=pltpu.CompilerParams(vmem_limit_bytes=limit * 2**20),
        cost_estimate=pl.CostEstimate(flops=flops, bytes_accessed=size, transcendentals=0),
    )


def like(shape, dtype=F32):
    return jax.ShapeDtypeStruct(shape, dtype)


def iota(shape, dim):
    return lax.broadcasted_iota(jnp.int32, shape, dim)


def begin_kernel(odd_ref):
    odd = lax.axis_index("lon") % 2
    odd_ref[...] = jnp.full(odd_ref.shape, odd, jnp.int32).astype(F32)


def pack_kernel(
    odd_ref, c_ref, v_ref, x_ref, first_ref, last_ref, left_ref, right_ref
):
    rows = x_ref.shape[0]
    tracers = c_ref.shape[0] // rows
    for r in range(rows):
        at = pl.ds(r, tracers, stride=rows)
        x = jnp.concatenate([c_ref[at, :], v_ref[at, :]], 0).astype(BF16)
        share_out(r, x, x_ref, first_ref, last_ref, left_ref, right_ref)


def prep_kernel(
    total_lon,
    pattern_ref,
    live_ref,
    inverse_ref,
    depth_ref,
    rate_ref,
    stoich_ref,
    basis_ref,
    c_ref,
    v_ref,
    index_ref,
    high_ref,
    low_ref,
    source_ref,
    rate_column_ref,
    gram_ref,
):
    lat, lon, slots = pattern_ref.shape
    rows = lat * lon
    columns, levels = inverse_ref.shape[2:4]
    points = columns * levels
    pattern = pattern_ref[...]
    itself = pattern[:, :, :1]
    far_lat = pattern // total_lon - itself // total_lon
    far_lon = pattern % total_lon - itself % total_lon
    shape = pattern.shape
    named = jnp.where(live_ref[...] > 0, (far_lat + 1) * 3 + far_lon + 1, -1)
    slot = iota(shape, 2)
    place = (iota(shape, 0) + slot // 3) * (lon + 2) + iota(shape, 1) + slot % 3
    held_at = jnp.zeros(shape, jnp.int32)
    found_at = jnp.zeros(shape, jnp.int32)
    for k in range(9):
        match = named == k
        held_at = jnp.where(
            slot == k, jnp.sum(jnp.where(match, slot, 0), 2, keepdims=True), held_at
        )
        found_at = jnp.where(
            slot == k, jnp.sum(jnp.where(match, 1, 0), 2, keepdims=True), found_at
        )
    index_ref[0] = held_at
    index_ref[1] = jnp.where(found_at > 0, place, (lat + 2) * (lon + 2))

    lane = iota((rows, points), 1)
    depth = jnp.concatenate([depth_ref[i] for i in range(lat)], 0)
    below = jnp.zeros((rows, points), jnp.int32)
    for k in range(columns):
        below = jnp.where(lane // levels == k, depth[:, k : k + 1], below)
    wet = (lane % levels < below).astype(F32)

    rate = jnp.concatenate([rate_ref[i] for i in range(lat)], 0)
    uptake, pull = sources(c_ref[:rows, :], v_ref[:rows, :], rate)
    spare = 8 - rows % 8 if rows % 8 else 0
    blank = [jnp.zeros((spare, points), F32)] if spare else []
    columns_of = [
        jnp.transpose(jnp.concatenate([part] + blank, 0)) for part in (uptake, pull, rate, wet)
    ]
    rate_column_ref[...] = columns_of[2]
    tracers = source_ref.shape[2] // 2
    share = stoich_ref[...]
    nothing = jnp.zeros((1, tracers), F32)
    share_c = jnp.concatenate([share, nothing], 1)
    share_v = jnp.concatenate([nothing, share], 1)
    for r in range(rows):
        at = slice(r, r + 1)
        source_ref[r] = columns_of[0][:, at] * share_c + columns_of[1][:, at] * share_v

    spread = (iota((levels, points), 1) % levels == iota((levels, points), 0)).astype(BF16)
    full = (points, points)
    same = iota(full, 0) // levels == iota(full, 1) // levels
    for r in range(rows):
        at = slice(r, r + 1)
        inverse = inverse_ref[r // lon, r % lon].reshape(points, levels)
        high = inverse.astype(BF16)
        low = (inverse - high.astype(F32)).astype(BF16)
        keep = jnp.where(same, wet[at, :] * columns_of[3][:, at], 0.0)
        for ref, part in ((high_ref, high), (low_ref, low)):
            tiled = jnp.dot(part, spread, preferred_element_type=F32)
            ref[r] = (tiled * keep).astype(BF16)

    gram_ref[...] = jnp.zeros(gram_ref.shape, F32)
    count = basis_ref.shape[0]
    row = 0
    for k in range(count):
        for j in range(k, count):
            gram_ref[row : row + 1, :] = jnp.sum(basis_ref[k] * basis_ref[j], 0, keepdims=True)
            row += 1


def sources(own_c, own_v, rate):
    denom = own_c * own_c + 1.0
    uptake = rate * own_c * own_c / denom
    slope = rate * 2.0 * own_c / (denom * denom)
    return uptake, slope * own_v


def beyond(lat, lon):
    found = {}
    for r in range(lat * lon):
        ends = [k for k in range(9) if not 0 <= r % lon + k % 3 - 1 < lon]
        if ends:
            found[r] = ends
    return found


def pull_kernel(lat, lon, state_ref, edge_ref, rate_column_ref, stoich_ref, source_ref):
    rows, _, tracers = source_ref.shape
    share = stoich_ref[...]
    edges = list(beyond(lat, lon))
    for r in range(rows):
        ref, at = (edge_ref, edges.index(r)) if r in edges else (state_ref, r)
        own_c = ref[at, :, 0:1]
        own_v = ref[at, :, tracers : tracers + 1]
        source_ref[r] = sources(own_c, own_v, rate_column_ref[:, r : r + 1])[1] * share


def fill(pad_ref, x_ref, north_ref, south_ref, lat, lon):
    wide = lon + 2
    for j in range(lon):
        pad_ref[1 + j] = north_ref[j]
        pad_ref[(lat + 1) * wide + 1 + j] = south_ref[j]
        for i in range(lat):
            pad_ref[(i + 1) * wide + 1 + j] = x_ref[i * lon + j]
    pad_ref[(lat + 2) * wide] = jnp.zeros(pad_ref.shape[1:], BF16)


def transport(r, index_ref, pad_ref, held_ref, z, neighbours):
    lon, slots = index_ref.shape[2:]
    for k in neighbours:
        block = held_ref[r * slots + index_ref[0, r // lon, r % lon, k]]
        x = pad_ref[index_ref[1, r // lon, r % lon, k]]
        z = z + lax.dot_general(block, x, NT, preferred_element_type=F32)
    return z


def mix(z, high, low):
    z_high = z.astype(BF16)
    z_low = (z - z_high.astype(F32)).astype(BF16)
    dot = functools.partial(jnp.dot, preferred_element_type=F32)
    return dot(high, z_high) + (dot(low, z_high) + dot(high, z_low))


def bulk(
    lat, lon, index_ref, pad_ref, held_ref, high_ref, low_ref, source_ref, state_ref, later_ref
):
    edges = beyond(lat, lon)
    slots = index_ref.shape[3]
    n = 0
    for r, neighbours in edges.items():
        for k in neighbours:
            at = (r // lon, r % lon, k)
            block = held_ref[r * slots + index_ref[0, *at]]
            named = index_ref[1, *at] < (lat + 2) * (lon + 2)
            later_ref[n] = jnp.where(named, block, jnp.zeros_like(block))
            n += 1
    for r in range(lat * lon):
        neighbours = [k for k in range(9) if k not in edges.get(r, ())]
        state_ref[r] = transport(r, index_ref, pad_ref, held_ref, source_ref[r], neighbours)
    for r in range(lat * lon):
        if r not in edges:
            state_ref[r] = mix(state_ref[r], high_ref[r], low_ref[r])


def finish(lat, lon, west_ref, east_ref, state_ref, later_ref, high_ref, low_ref, out_ref):
    edges = beyond(lat, lon)
    at = 0
    for n, (r, neighbours) in enumerate(edges.items()):
        z = state_ref[r]
        for k in neighbours:
            x = (west_ref if r % lon + k % 3 == 0 else east_ref)[r // lon + k // 3]
            z = z + lax.dot_general(later_ref[at], x, NT, preferred_element_type=F32)
            at += 1
        out_ref[n] = z
    for n, r in enumerate(edges):
        out_ref[n] = mix(out_ref[n], high_ref[r], low_ref[r])


def first_kernel(
    lat,
    lon,
    index_ref,
    x_ref,
    north_ref,
    south_ref,
    held_ref,
    high_ref,
    low_ref,
    source_ref,
    y_ref,
    state_ref,
    later_ref,
    pad_ref,
):
    fill(pad_ref, x_ref, north_ref, south_ref, lat, lon)
    bulk(
        lat, lon, index_ref, pad_ref, held_ref, high_ref, low_ref, source_ref, state_ref, later_ref
    )
    tracers = y_ref.shape[1]
    for r in range(lat * lon):
        if r in beyond(lat, lon):
            y_ref[r] = jnp.zeros(y_ref.shape[1:], BF16)
        else:
            y_ref[r] = jnp.transpose(state_ref[r])[tracers:].astype(BF16)


def first_end_kernel(
    lat,
    lon,
    west_ref,
    east_ref,
    state_ref,
    later_ref,
    high_ref,
    low_ref,
    part_ref,
    y_ref,
    first_ref,
    last_ref,
    left_ref,
    right_ref,
    edge_ref,
):
    finish(lat, lon, west_ref, east_ref, state_ref, later_ref, high_ref, low_ref, edge_ref)
    edges = list(beyond(lat, lon))
    tracers = y_ref.shape[1]
    for r in range(lat * lon):
        if r in edges:
            y = jnp.transpose(edge_ref[edges.index(r)])[tracers:].astype(BF16)
        else:
            y = part_ref[r]
        share_out(r, y, y_ref, first_ref, last_ref, left_ref, right_ref)


def share_out(r, x, x_ref, first_ref, last_ref, left_ref, right_ref):
    rows, lon = x_ref.shape[0], first_ref.shape[0]
    x_ref[r] = x
    if r < lon:
        first_ref[r] = x
    if r >= rows - lon:
        last_ref[r - (rows - lon)] = x
    if r % lon == 0:
        left_ref[r // lon] = x
    if r % lon == lon - 1:
        right_ref[r // lon] = x


def second_kernel(
    lat,
    lon,
    index_ref,
    x_ref,
    north_ref,
    south_ref,
    held_ref,
    high_ref,
    low_ref,
    source_ref,
    part_ref,
    state_ref,
    later_ref,
    pad_ref,
):
    rows = lat * lon
    fill(pad_ref, x_ref, north_ref, south_ref, lat, lon)
    bulk(
        lat, lon, index_ref, pad_ref, held_ref, high_ref, low_ref, source_ref, state_ref, later_ref
    )
    tracers = x_ref.shape[1]
    for r in range(rows):
        at = pl.ds(r, tracers, stride=rows)
        if r in beyond(lat, lon):
            part_ref[at, :] = jnp.zeros((tracers, part_ref.shape[1]), F32)
        else:
            part_ref[at, :] = jnp.transpose(state_ref[r])


def second_end_kernel(
    lat,
    lon,
    west_ref,
    east_ref,
    state_ref,
    later_ref,
    high_ref,
    low_ref,
    part_ref,
    gram_ref,
    basis_ref,
    product_ref,
    out_hbm,
    sums_ref,
    edge_ref,
    sem,
):
    finish(lat, lon, west_ref, east_ref, state_ref, later_ref, high_ref, low_ref, edge_ref)
    rows = lat * lon
    product_ref[...] = part_ref[...]
    tracers = product_ref.shape[0] // rows
    for n, r in enumerate(beyond(lat, lon)):
        product_ref[pl.ds(r, tracers, stride=rows), :] = jnp.transpose(edge_ref[n])
    copy = pltpu.make_async_copy(product_ref, out_hbm, sem)
    copy.start()
    product = product_ref[...]
    count = basis_ref.shape[0]
    pairs = count * (count + 1) // 2
    all_sums = gram_ref[...]
    spot = iota(all_sums.shape, 0)
    for k in range(count + 1):
        other = basis_ref[k] if k < count else product
        part = jnp.sum(product * other, 0, keepdims=True)
        all_sums = jnp.where(spot == pairs + k, part, all_sums)
    column = jnp.sum(all_sums, 1, keepdims=True)
    row = jnp.sum(jnp.where(spot == iota(spot.shape, 1), column, 0.0), 0, keepdims=True)
    sums_ref[...] = jnp.broadcast_to(row, sums_ref.shape)
    copy.wait()


def last_kernel(parts_ref, product_ref, basis_ref, next_ref, coeffs_ref, flag_ref):
    count = basis_ref.shape[0]
    row = jnp.sum(parts_ref[...], 0, keepdims=True)
    lane = iota(row.shape, 1)

    def pick(at):
        return jnp.sum(jnp.where(lane == at, row, 0.0), 1, keepdims=True)

    pairs = count * (count + 1) // 2
    heights = [pick(pairs + k) for k in range(count)]
    whole = pick(pairs + count)
    cross = jnp.zeros((1, 1), F32)
    at = 0
    for k in range(count):
        for j in range(k, count):
            twice = 1.0 if k == j else 2.0
            cross = cross + twice * (heights[k] * heights[j] * pick(at))
            at += 1
    squares = sum(h * h for h in heights)
    short = whole - 2.0 * squares + cross
    size = whole + 2.0 * squares + cross
    beta = jnp.sqrt(jnp.maximum(short, 0.0) + 1e-06)
    rest = product_ref[...]
    for k in range(count):
        rest = rest - heights[k] * basis_ref[k]
    next_ref[...] = rest / beta
    for k in range(count):
        coeffs_ref[k] = heights[k][0, 0]
    coeffs_ref[count] = beta[0, 0]
    flag_ref[0] = jnp.where(short < 0.01 * size, 1, 0)[0, 0]


def summed(rows):
    row = jnp.sum(lax.all_to_all(rows, "lon", 0, 0), 0, keepdims=True)
    rows = jnp.broadcast_to(row, (lax.axis_size("lat"), row.shape[1]))
    return lax.all_to_all(rows, "lat", 0, 0)


def rows_around(first, last, beside):
    size = lax.axis_size("lat")
    north = lax.ppermute(last, "lat", [(i, (i + 1) % size) for i in range(size)])
    south = lax.ppermute(first, "lat", [((i + 1) % size, i) for i in range(size)])
    return lax.optimization_barrier((north, south, beside))


def columns_around(left, right, north, south, odd):
    size = lax.axis_size("lon")
    odd = odd[None, : left.shape[1]] > 0.5
    right = jnp.concatenate([north[-1:], right, south[-1:]], 0)
    left = jnp.concatenate([north[:1], left, south[:1]], 0)

    def swapped(a, start):
        pairs = [(i, i + 1) for i in range(start, size - 1, 2)]
        return lax.ppermute(a, "lon", pairs + [(j, i) for i, j in pairs])

    near = swapped(jnp.where(odd, left, right), 0)
    far = swapped(jnp.where(odd, right, left), 1)
    far, near = lax.optimization_barrier((far, near))
    return jnp.where(odd, near, far), jnp.where(odd, far, near)


def body(
    base_state,
    tangent,
    blocks,
    pattern,
    live,
    column_inverse,
    col_depth,
    uptake_rate,
    stoich,
    basis,
):
    tracers, lat, lon, points = base_state.shape
    slots = pattern.shape[2]
    count = basis.shape[0]
    rows = lat * lon
    total_lon = lon * lax.axis_size("lon")
    size = tracers * rows
    places = (lat + 2) * (lon + 2) + 1
    share = stoich.reshape(1, tracers)

    flat_c = base_state.reshape(size, points)
    flat_v = tangent.reshape(size, points)
    def edges(width):
        return (
            like((rows, width, points), BF16),
            like((lon, width, points), BF16),
            like((lon, width, points), BF16),
            like((lat, width, points), BF16),
            like((lat, width, points), BF16),
        )

    odd = call(begin_kernel, like((2 * tracers, points)), [], VMEM, flops=PACK)()
    x, first, last, left, right = call(
        pack_kernel, edges(2 * tracers), [VMEM] * 3, [VMEM] * 5, flops=PACK, size=400000
    )(odd, flat_c, flat_v)

    flat_basis = basis.reshape(count, size, points)
    held = blocks.reshape(rows * slots, points, points)
    index, high, low, source, rate_column, gram = call(
        functools.partial(prep_kernel, total_lon),
        (
            like((2, lat, lon, slots), jnp.int32),
            like((rows, points, points), BF16),
            like((rows, points, points), BF16),
            like((rows, points, 2 * tracers)),
            like((points, (rows + 7) // 8 * 8)),
            like((16, points)),
        ),
        [VMEM] * 9,
        [VMEM] * 6,
        flops=PREP,
        size=8000000,
    )(
        pattern,
        live,
        column_inverse,
        col_depth,
        uptake_rate,
        share,
        flat_basis,
        flat_c,
        flat_v,
    )

    work = 2 * 2 * tracers * rows * slots * points * points
    ends = len(beyond(lat, lon))
    later = like((sum(map(len, beyond(lat, lon).values())), points, points), BF16)

    prepared = (index, high, low, source, rate_column, gram)
    north, south, prepared = rows_around(first, last, prepared)
    index, high, low, source, rate_column, gram = prepared
    west, east = columns_around(left, right, north, south, odd)
    part, state, blocks_later = call(
        functools.partial(first_kernel, lat, lon),
        (like((rows, tracers, points), BF16), like((rows, points, 2 * tracers)), later),
        [SMEM] + [VMEM] * 7,
        [VMEM] * 3,
        scratch=[pltpu.VMEM((places, 2 * tracers, points), BF16)],
        flops=BULK,
        size=5000000,
    )(index, x, north, south, held, high, low, source)
    x, first, last, left, right, edge = call(
        functools.partial(first_end_kernel, lat, lon),
        edges(tracers) + (like((ends, points, 2 * tracers)),),
        [VMEM] * 7,
        [VMEM] * 6,
        flops=work // 20,
        size=500000,
    )(west, east, state, blocks_later, high, low, part)

    source = call(
        functools.partial(pull_kernel, lat, lon),
        like((rows, points, tracers)),
        [VMEM] * 4,
        VMEM,
        flops=100000,
        size=2000000,
    )(state, edge, rate_column, share)

    north, south, source = rows_around(first, last, source)
    west, east = columns_around(left, right, north, south, odd)
    part, state, blocks_later = call(
        functools.partial(second_kernel, lat, lon),
        (like((size, points)), like((rows, points, tracers)), later),
        [SMEM] + [VMEM] * 7,
        [VMEM] * 3,
        scratch=[pltpu.VMEM((places, tracers, points), BF16)],
        flops=BULK,
        size=5000000,
    )(index, x, north, south, held, high, low, source)
    product, written, sums = call(
        functools.partial(second_end_kernel, lat, lon),
        (like((size, points)), like((size, points)), like((lax.axis_size("lon"), points))),
        [VMEM] * 9,
        [VMEM, HBM, VMEM],
        scratch=[pltpu.VMEM((ends, points, tracers), F32), pltpu.SemaphoreType.DMA],
        flops=work // 20,
        size=1500000,
    )(west, east, state, blocks_later, high, low, part, gram, flat_basis)

    parts = summed(sums)
    following, coeffs, flag = call(
        last_kernel,
        (like((size, points)), like((count + 1,)), like((1,), jnp.int32)),
        [VMEM] * 3,
        [VMEM, SMEM, SMEM],
        size=700000,
    )(parts, product, flat_basis)

    def again(carry):
        pairs = count * (count + 1) // 2
        heights = jnp.sum(parts, 0)[pairs : pairs + count]
        rest = product - jnp.einsum(
            "k,ksp->sp", heights, flat_basis, precision=lax.Precision.HIGHEST
        )
        part = jnp.pad(jnp.sum(rest * rest).reshape(1, 1), ((0, 0), (0, points - 1)))
        squared = jnp.sum(summed(jnp.broadcast_to(part, (lax.axis_size("lon"), points))), 0)[0]
        beta = jnp.sqrt(squared + 1e-06)
        return rest / beta, jnp.concatenate([heights, beta[None]]), carry[2] * 0

    following, coeffs, flag = lax.while_loop(
        lambda carry: carry[2][0] > 0, again, (following, coeffs, flag)
    )
    shape = base_state.shape
    return written.reshape(shape), following.reshape(shape), coeffs


def solution(mesh):
    placed = (
        P(None, "lat", "lon", None),
        P(None, "lat", "lon", None),
        P("lat", "lon", None, None, None),
        P("lat", "lon", None),
        P("lat", "lon", None),
        P("lat", "lon", None, None, None),
        P("lat", "lon", None),
        P("lat", "lon", None),
        P(),
        P(None, None, "lat", "lon", None),
    )
    return jax.shard_map(
        body,
        mesh=mesh,
        in_specs=placed,
        out_specs=(P(None, "lat", "lon", None), P(None, "lat", "lon", None), P()),
        check_vma=False,
    )
```

```python
import functools

import jax
import jax.numpy as jnp
from jax import lax
from jax.experimental import pallas as pl
from jax.experimental.pallas import tpu as pltpu
from jax.sharding import PartitionSpec as P

F32 = jnp.float32
BF16 = jnp.bfloat16
VMEM = pl.BlockSpec(memory_space=pltpu.VMEM)
SMEM = pl.BlockSpec(memory_space=pltpu.SMEM)
HBM = pl.BlockSpec(memory_space=pltpu.HBM)
PACK = 20000000000
PREP = 10000000000
BULK = 2000000000
NT = (((1,), (1,)), ((), ()))


def call(kernel, outs, ins, out_specs, scratch=(), flops=0, size=0, limit=16):
    return pl.pallas_call(
        kernel,
        out_shape=outs,
        in_specs=ins,
        out_specs=out_specs,
        scratch_shapes=list(scratch),
        compiler_params=pltpu.CompilerParams(vmem_limit_bytes=limit * 2**20),
        cost_estimate=pl.CostEstimate(flops=flops, bytes_accessed=size, transcendentals=0),
    )


def like(shape, dtype=F32):
    return jax.ShapeDtypeStruct(shape, dtype)


def iota(shape, dim):
    return lax.broadcasted_iota(jnp.int32, shape, dim)


def begin_kernel(odd_ref):
    odd = lax.axis_index("lon") % 2
    odd_ref[...] = jnp.full(odd_ref.shape, odd, jnp.int32).astype(F32)


def pack_kernel(
    odd_ref, c_ref, v_ref, x_ref, first_ref, last_ref, left_ref, right_ref
):
    rows = x_ref.shape[0]
    tracers = c_ref.shape[0] // rows
    for r in range(rows):
        at = pl.ds(r, tracers, stride=rows)
        x = jnp.concatenate([c_ref[at, :], v_ref[at, :]], 0).astype(BF16)
        share_out(r, x, x_ref, first_ref, last_ref, left_ref, right_ref)


def prep_kernel(
    total_lon,
    pattern_ref,
    live_ref,
    inverse_ref,
    depth_ref,
    rate_ref,
    stoich_ref,
    basis_ref,
    c_ref,
    v_ref,
    index_ref,
    high_ref,
    low_ref,
    source_ref,
    rate_column_ref,
    gram_ref,
):
    lat, lon, slots = pattern_ref.shape
    rows = lat * lon
    columns, levels = inverse_ref.shape[2:4]
    points = columns * levels
    pattern = pattern_ref[...]
    itself = pattern[:, :, :1]
    far_lat = pattern // total_lon - itself // total_lon
    far_lon = pattern % total_lon - itself % total_lon
    shape = pattern.shape
    named = jnp.where(live_ref[...] > 0, (far_lat + 1) * 3 + far_lon + 1, -1)
    slot = iota(shape, 2)
    place = (iota(shape, 0) + slot // 3) * (lon + 2) + iota(shape, 1) + slot % 3
    held_at = jnp.zeros(shape, jnp.int32)
    found_at = jnp.zeros(shape, jnp.int32)
    for k in range(9):
        match = named == k
        held_at = jnp.where(
            slot == k, jnp.sum(jnp.where(match, slot, 0), 2, keepdims=True), held_at
        )
        found_at = jnp.where(
            slot == k, jnp.sum(jnp.where(match, 1, 0), 2, keepdims=True), found_at
        )
    index_ref[0] = held_at
    index_ref[1] = jnp.where(found_at > 0, place, (lat + 2) * (lon + 2))

    lane = iota((rows, points), 1)
    depth = jnp.concatenate([depth_ref[i] for i in range(lat)], 0)
    below = jnp.zeros((rows, points), jnp.int32)
    for k in range(columns):
        below = jnp.where(lane // levels == k, depth[:, k : k + 1], below)
    wet = (lane % levels < below).astype(F32)

    rate = jnp.concatenate([rate_ref[i] for i in range(lat)], 0)
    uptake, pull = sources(c_ref[:rows, :], v_ref[:rows, :], rate)
    spare = 8 - rows % 8 if rows % 8 else 0
    blank = [jnp.zeros((spare, points), F32)] if spare else []
    columns_of = [
        jnp.transpose(jnp.concatenate([part] + blank, 0)) for part in (uptake, pull, rate, wet)
    ]
    rate_column_ref[...] = columns_of[2]
    tracers = source_ref.shape[2] // 2
    share = stoich_ref[...]
    nothing = jnp.zeros((1, tracers), F32)
    share_c = jnp.concatenate([share, nothing], 1)
    share_v = jnp.concatenate([nothing, share], 1)
    for r in range(rows):
        at = slice(r, r + 1)
        source_ref[r] = columns_of[0][:, at] * share_c + columns_of[1][:, at] * share_v

    spread = (iota((levels, points), 1) % levels == iota((levels, points), 0)).astype(BF16)
    full = (points, points)
    same = iota(full, 0) // levels == iota(full, 1) // levels
    for r in range(rows):
        at = slice(r, r + 1)
        inverse = inverse_ref[r // lon, r % lon].reshape(points, levels)
        high = inverse.astype(BF16)
        low = (inverse - high.astype(F32)).astype(BF16)
        keep = jnp.where(same, wet[at, :] * columns_of[3][:, at], 0.0)
        for ref, part in ((high_ref, high), (low_ref, low)):
            tiled = jnp.dot(part, spread, preferred_element_type=F32)
            ref[r] = (tiled * keep).astype(BF16)

    gram_ref[...] = jnp.zeros(gram_ref.shape, F32)
    count = basis_ref.shape[0]
    row = 0
    for k in range(count):
        for j in range(k, count):
            gram_ref[row : row + 1, :] = jnp.sum(basis_ref[k] * basis_ref[j], 0, keepdims=True)
            row += 1


def sources(own_c, own_v, rate):
    denom = own_c * own_c + 1.0
    uptake = rate * own_c * own_c / denom
    slope = rate * 2.0 * own_c / (denom * denom)
    return uptake, slope * own_v


def beyond(lat, lon):
    found = {}
    for r in range(lat * lon):
        ends = [k for k in range(9) if not 0 <= r % lon + k % 3 - 1 < lon]
        if ends:
            found[r] = ends
    return found


def pull_kernel(lat, lon, state_ref, edge_ref, rate_column_ref, stoich_ref, source_ref):
    rows, _, tracers = source_ref.shape
    share = stoich_ref[...]
    edges = list(beyond(lat, lon))
    for r in range(rows):
        ref, at = (edge_ref, edges.index(r)) if r in edges else (state_ref, r)
        own_c = ref[at, :, 0:1]
        own_v = ref[at, :, tracers : tracers + 1]
        source_ref[r] = sources(own_c, own_v, rate_column_ref[:, r : r + 1])[1] * share


def fill(pad_ref, x_ref, north_ref, south_ref, lat, lon):
    wide = lon + 2
    for j in range(lon):
        pad_ref[1 + j] = north_ref[j]
        pad_ref[(lat + 1) * wide + 1 + j] = south_ref[j]
        for i in range(lat):
            pad_ref[(i + 1) * wide + 1 + j] = x_ref[i * lon + j]
    pad_ref[(lat + 2) * wide] = jnp.zeros(pad_ref.shape[1:], BF16)


def transport(r, index_ref, pad_ref, held_ref, z, neighbours):
    lon, slots = index_ref.shape[2:]
    for k in neighbours:
        block = held_ref[r * slots + index_ref[0, r // lon, r % lon, k]]
        x = pad_ref[index_ref[1, r // lon, r % lon, k]]
        z = z + lax.dot_general(block, x, NT, preferred_element_type=F32)
    return z


def mix(z, high, low):
    z_high = z.astype(BF16)
    z_low = (z - z_high.astype(F32)).astype(BF16)
    dot = functools.partial(jnp.dot, preferred_element_type=F32)
    return dot(high, z_high) + (dot(low, z_high) + dot(high, z_low))


def bulk(
    lat, lon, index_ref, pad_ref, held_ref, high_ref, low_ref, source_ref, state_ref, later_ref
):
    edges = beyond(lat, lon)
    slots = index_ref.shape[3]
    n = 0
    for r, neighbours in edges.items():
        for k in neighbours:
            at = (r // lon, r % lon, k)
            block = held_ref[r * slots + index_ref[0, *at]]
            named = index_ref[1, *at] < (lat + 2) * (lon + 2)
            later_ref[n] = jnp.where(named, block, jnp.zeros_like(block))
            n += 1
    for r in range(lat * lon):
        neighbours = [k for k in range(9) if k not in edges.get(r, ())]
        state_ref[r] = transport(r, index_ref, pad_ref, held_ref, source_ref[r], neighbours)
    for r in range(lat * lon):
        if r not in edges:
            state_ref[r] = mix(state_ref[r], high_ref[r], low_ref[r])


def finish(lat, lon, west_ref, east_ref, state_ref, later_ref, high_ref, low_ref, out_ref):
    edges = beyond(lat, lon)
    at = 0
    for n, (r, neighbours) in enumerate(edges.items()):
        z = state_ref[r]
        for k in neighbours:
            x = (west_ref if r % lon + k % 3 == 0 else east_ref)[r // lon + k // 3]
            z = z + lax.dot_general(later_ref[at], x, NT, preferred_element_type=F32)
            at += 1
        out_ref[n] = z
    for n, r in enumerate(edges):
        out_ref[n] = mix(out_ref[n], high_ref[r], low_ref[r])


def first_kernel(
    lat,
    lon,
    index_ref,
    x_ref,
    north_ref,
    south_ref,
    held_ref,
    high_ref,
    low_ref,
    source_ref,
    y_ref,
    state_ref,
    later_ref,
    pad_ref,
):
    fill(pad_ref, x_ref, north_ref, south_ref, lat, lon)
    bulk(
        lat, lon, index_ref, pad_ref, held_ref, high_ref, low_ref, source_ref, state_ref, later_ref
    )
    tracers = y_ref.shape[1]
    for r in range(lat * lon):
        if r in beyond(lat, lon):
            y_ref[r] = jnp.zeros(y_ref.shape[1:], BF16)
        else:
            y_ref[r] = jnp.transpose(state_ref[r])[tracers:].astype(BF16)


def first_end_kernel(
    lat,
    lon,
    west_ref,
    east_ref,
    state_ref,
    later_ref,
    high_ref,
    low_ref,
    part_ref,
    y_ref,
    first_ref,
    last_ref,
    left_ref,
    right_ref,
    edge_ref,
):
    finish(lat, lon, west_ref, east_ref, state_ref, later_ref, high_ref, low_ref, edge_ref)
    edges = list(beyond(lat, lon))
    tracers = y_ref.shape[1]
    for r in range(lat * lon):
        if r in edges:
            y = jnp.transpose(edge_ref[edges.index(r)])[tracers:].astype(BF16)
        else:
            y = part_ref[r]
        share_out(r, y, y_ref, first_ref, last_ref, left_ref, right_ref)


def share_out(r, x, x_ref, first_ref, last_ref, left_ref, right_ref):
    rows, lon = x_ref.shape[0], first_ref.shape[0]
    x_ref[r] = x
    if r < lon:
        first_ref[r] = x
    if r >= rows - lon:
        last_ref[r - (rows - lon)] = x
    if r % lon == 0:
        left_ref[r // lon] = x
    if r % lon == lon - 1:
        right_ref[r // lon] = x


def second_kernel(
    lat,
    lon,
    index_ref,
    x_ref,
    north_ref,
    south_ref,
    held_ref,
    high_ref,
    low_ref,
    source_ref,
    part_ref,
    state_ref,
    later_ref,
    pad_ref,
):
    rows = lat * lon
    fill(pad_ref, x_ref, north_ref, south_ref, lat, lon)
    bulk(
        lat, lon, index_ref, pad_ref, held_ref, high_ref, low_ref, source_ref, state_ref, later_ref
    )
    tracers = x_ref.shape[1]
    for r in range(rows):
        at = pl.ds(r, tracers, stride=rows)
        if r in beyond(lat, lon):
            part_ref[at, :] = jnp.zeros((tracers, part_ref.shape[1]), F32)
        else:
            part_ref[at, :] = jnp.transpose(state_ref[r])


def second_end_kernel(
    lat,
    lon,
    west_ref,
    east_ref,
    state_ref,
    later_ref,
    high_ref,
    low_ref,
    part_ref,
    gram_ref,
    basis_ref,
    product_ref,
    out_hbm,
    sums_ref,
    edge_ref,
    sem,
):
    finish(lat, lon, west_ref, east_ref, state_ref, later_ref, high_ref, low_ref, edge_ref)
    rows = lat * lon
    product_ref[...] = part_ref[...]
    tracers = product_ref.shape[0] // rows
    for n, r in enumerate(beyond(lat, lon)):
        product_ref[pl.ds(r, tracers, stride=rows), :] = jnp.transpose(edge_ref[n])
    copy = pltpu.make_async_copy(product_ref, out_hbm, sem)
    copy.start()
    product = product_ref[...]
    count = basis_ref.shape[0]
    pairs = count * (count + 1) // 2
    all_sums = gram_ref[...]
    spot = iota(all_sums.shape, 0)
    for k in range(count + 1):
        other = basis_ref[k] if k < count else product
        part = jnp.sum(product * other, 0, keepdims=True)
        all_sums = jnp.where(spot == pairs + k, part, all_sums)
    column = jnp.sum(all_sums, 1, keepdims=True)
    row = jnp.sum(jnp.where(spot == iota(spot.shape, 1), column, 0.0), 0, keepdims=True)
    sums_ref[...] = jnp.broadcast_to(row, sums_ref.shape)
    copy.wait()


def last_kernel(parts_ref, product_ref, basis_ref, next_ref, coeffs_ref, flag_ref):
    count = basis_ref.shape[0]
    row = jnp.sum(parts_ref[...], 0, keepdims=True)
    lane = iota(row.shape, 1)

    def pick(at):
        return jnp.sum(jnp.where(lane == at, row, 0.0), 1, keepdims=True)

    pairs = count * (count + 1) // 2
    heights = [pick(pairs + k) for k in range(count)]
    whole = pick(pairs + count)
    cross = jnp.zeros((1, 1), F32)
    at = 0
    for k in range(count):
        for j in range(k, count):
            twice = 1.0 if k == j else 2.0
            cross = cross + twice * (heights[k] * heights[j] * pick(at))
            at += 1
    squares = sum(h * h for h in heights)
    short = whole - 2.0 * squares + cross
    size = whole + 2.0 * squares + cross
    beta = jnp.sqrt(jnp.maximum(short, 0.0) + 1e-06)
    rest = product_ref[...]
    for k in range(count):
        rest = rest - heights[k] * basis_ref[k]
    next_ref[...] = rest / beta
    for k in range(count):
        coeffs_ref[k] = heights[k][0, 0]
    coeffs_ref[count] = beta[0, 0]
    flag_ref[0] = jnp.where(short < 0.01 * size, 1, 0)[0, 0]


def summed(rows):
    row = jnp.sum(lax.all_to_all(rows, "lat", 0, 0), 0, keepdims=True)
    rows = jnp.broadcast_to(row, (lax.axis_size("lon"), row.shape[1]))
    return lax.all_to_all(rows, "lon", 0, 0)


def rows_around(first, last, beside):
    size = lax.axis_size("lat")
    north = lax.ppermute(last, "lat", [(i, (i + 1) % size) for i in range(size)])
    south = lax.ppermute(first, "lat", [((i + 1) % size, i) for i in range(size)])
    return lax.optimization_barrier((north, south, beside))


def columns_around(left, right, north, south, odd):
    size = lax.axis_size("lon")
    odd = odd[None, : left.shape[1]] > 0.5
    right = jnp.concatenate([north[-1:], right, south[-1:]], 0)
    left = jnp.concatenate([north[:1], left, south[:1]], 0)

    def swapped(a, start):
        pairs = [(i, i + 1) for i in range(start, size - 1, 2)]
        return lax.ppermute(a, "lon", pairs + [(j, i) for i, j in pairs])

    near = swapped(jnp.where(odd, left, right), 0)
    far = swapped(jnp.where(odd, right, left), 1)
    far, near = lax.optimization_barrier((far, near))
    return jnp.where(odd, near, far), jnp.where(odd, far, near)


def body(
    base_state,
    tangent,
    blocks,
    pattern,
    live,
    column_inverse,
    col_depth,
    uptake_rate,
    stoich,
    basis,
):
    tracers, lat, lon, points = base_state.shape
    slots = pattern.shape[2]
    count = basis.shape[0]
    rows = lat * lon
    total_lon = lon * lax.axis_size("lon")
    size = tracers * rows
    places = (lat + 2) * (lon + 2) + 1
    share = stoich.reshape(1, tracers)

    flat_c = base_state.reshape(size, points)
    flat_v = tangent.reshape(size, points)
    def edges(width):
        return (
            like((rows, width, points), BF16),
            like((lon, width, points), BF16),
            like((lon, width, points), BF16),
            like((lat, width, points), BF16),
            like((lat, width, points), BF16),
        )

    odd = call(begin_kernel, like((2 * tracers, points)), [], VMEM, flops=PACK)()
    x, first, last, left, right = call(
        pack_kernel, edges(2 * tracers), [VMEM] * 3, [VMEM] * 5, flops=PACK, size=400000
    )(odd, flat_c, flat_v)

    flat_basis = basis.reshape(count, size, points)
    held = blocks.reshape(rows * slots, points, points)
    index, high, low, source, rate_column, gram = call(
        functools.partial(prep_kernel, total_lon),
        (
            like((2, lat, lon, slots), jnp.int32),
            like((rows, points, points), BF16),
            like((rows, points, points), BF16),
            like((rows, points, 2 * tracers)),
            like((points, (rows + 7) // 8 * 8)),
            like((16, points)),
        ),
        [VMEM] * 9,
        [VMEM] * 6,
        flops=PREP,
        size=8000000,
    )(
        pattern,
        live,
        column_inverse,
        col_depth,
        uptake_rate,
        share,
        flat_basis,
        flat_c,
        flat_v,
    )

    work = 2 * 2 * tracers * rows * slots * points * points
    ends = len(beyond(lat, lon))
    later = like((sum(map(len, beyond(lat, lon).values())), points, points), BF16)

    prepared = (index, high, low, source, rate_column, gram)
    north, south, prepared = rows_around(first, last, prepared)
    index, high, low, source, rate_column, gram = prepared
    west, east = columns_around(left, right, north, south, odd)
    part, state, blocks_later = call(
        functools.partial(first_kernel, lat, lon),
        (like((rows, tracers, points), BF16), like((rows, points, 2 * tracers)), later),
        [SMEM] + [VMEM] * 7,
        [VMEM] * 3,
        scratch=[pltpu.VMEM((places, 2 * tracers, points), BF16)],
        flops=BULK,
        size=5000000,
    )(index, x, north, south, held, high, low, source)
    x, first, last, left, right, edge = call(
        functools.partial(first_end_kernel, lat, lon),
        edges(tracers) + (like((ends, points, 2 * tracers)),),
        [VMEM] * 7,
        [VMEM] * 6,
        flops=work // 20,
        size=500000,
    )(west, east, state, blocks_later, high, low, part)

    source = call(
        functools.partial(pull_kernel, lat, lon),
        like((rows, points, tracers)),
        [VMEM] * 4,
        VMEM,
        flops=100000,
        size=2000000,
    )(state, edge, rate_column, share)

    north, south, source = rows_around(first, last, source)
    west, east = columns_around(left, right, north, south, odd)
    part, state, blocks_later = call(
        functools.partial(second_kernel, lat, lon),
        (like((size, points)), like((rows, points, tracers)), later),
        [SMEM] + [VMEM] * 7,
        [VMEM] * 3,
        scratch=[pltpu.VMEM((places, tracers, points), BF16)],
        flops=BULK,
        size=5000000,
    )(index, x, north, south, held, high, low, source)
    product, written, sums = call(
        functools.partial(second_end_kernel, lat, lon),
        (like((size, points)), like((size, points)), like((lax.axis_size("lat"), points))),
        [VMEM] * 9,
        [VMEM, HBM, VMEM],
        scratch=[pltpu.VMEM((ends, points, tracers), F32), pltpu.SemaphoreType.DMA],
        flops=work // 20,
        size=1500000,
    )(west, east, state, blocks_later, high, low, part, gram, flat_basis)

    parts = summed(sums)
    following, coeffs, flag = call(
        last_kernel,
        (like((size, points)), like((count + 1,)), like((1,), jnp.int32)),
        [VMEM] * 3,
        [VMEM, SMEM, SMEM],
        size=700000,
    )(parts, product, flat_basis)

    def again(carry):
        pairs = count * (count + 1) // 2
        heights = jnp.sum(parts, 0)[pairs : pairs + count]
        rest = product - jnp.einsum(
            "k,ksp->sp", heights, flat_basis, precision=lax.Precision.HIGHEST
        )
        part = jnp.pad(jnp.sum(rest * rest).reshape(1, 1), ((0, 0), (0, points - 1)))
        squared = jnp.sum(summed(jnp.broadcast_to(part, (lax.axis_size("lat"), points))), 0)[0]
        beta = jnp.sqrt(squared + 1e-06)
        return rest / beta, jnp.concatenate([heights, beta[None]]), carry[2] * 0

    following, coeffs, flag = lax.while_loop(
        lambda carry: carry[2][0] > 0, again, (following, coeffs, flag)
    )
    shape = base_state.shape
    return written.reshape(shape), following.reshape(shape), coeffs


def solution(mesh):
    placed = (
        P(None, "lat", "lon", None),
        P(None, "lat", "lon", None),
        P("lat", "lon", None, None, None),
        P("lat", "lon", None),
        P("lat", "lon", None),
        P("lat", "lon", None, None, None),
        P("lat", "lon", None),
        P("lat", "lon", None),
        P(),
        P(None, None, "lat", "lon", None),
    )
    return jax.shard_map(
        body,
        mesh=mesh,
        in_specs=placed,
        out_specs=(P(None, "lat", "lon", None), P(None, "lat", "lon", None), P()),
        check_vma=False,
    )
```
